32 devices in a mesh: parts: 2 (over x), region: 4 (over y, core), sub: 4 (over z).
Axes of the slice: x: 2, y: 2, z: 4, core: 2. Of those that a mesh axis runs over, the one named last changes fastest.
Arguments:
- node_feats: bfloat16 [16384, 128], P(('parts', 'region', 'sub')), parts along dimension 0, may hold values from -6 to 6
- fine_senders: int32 [98304], P(('parts', 'region', 'sub')), parts along dimension 0, may hold values from 0 to 639
- fine_receivers: int32 [98304], P(('parts', 'region', 'sub')), parts along dimension 0, may hold values from 0 to 511
- fine_edges: bfloat16 [98304, 128], P(('parts', 'region', 'sub')), parts along dimension 0, may hold values from -6 to 6
- halo_rows: int32 [64, 64], P(('parts', 'region', 'sub')), parts along dimension 0, may hold values from 0 to 511
- coarse_senders: int32 [49152], P(('parts', 'region', 'sub')), parts along dimension 0, may hold values from 0 to 319
- coarse_receivers: int32 [49152], P(('parts', 'region', 'sub')), parts along dimension 0, may hold values from 0 to 255
- coarse_edges: bfloat16 [49152, 128], P(('parts', 'region', 'sub')), parts along dimension 0, may hold values from -6 to 6
- coarse_halo_rows: int32 [64, 32], P(('parts', 'region', 'sub')), parts along dimension 0, may hold values from 0 to 255
- pool_dest: int32 [16384, 1], P(('parts', 'region', 'sub')), parts along dimension 0, may hold values from 0 to 3; in each aligned block of 512 rows (0 to 511, 512 to 1023, ...) at most 256 rows name the same one
- pool_target: int32 [16384], P(('parts', 'region', 'sub')), parts along dimension 0, may hold values from 0 to 255
- pool3_target: int32 [8192], P(('parts', 'region', 'sub')), parts along dimension 0, may hold values from 0 to 2047
- top_senders: int32 [16384], P('parts'), parts along dimension 0, may hold values from 0 to 2047
- top_receivers: int32 [16384], P('parts'), parts along dimension 0, may hold values from 0 to 2047
- top_edges: bfloat16 [16384, 128], P('parts'), parts along dimension 0, may hold values from -6 to 6
- edge_in: bfloat16 [5, 384, 128], replicated, may hold values from -0.3125 to 0.3125
- edge_out: bfloat16 [5, 128, 128], replicated, may hold values from -0.5 to 0.5
- node_in: bfloat16 [5, 256, 128], replicated, may hold values from -0.375 to 0.375
- node_out: bfloat16 [5, 128, 128], replicated, may hold values from -0.5 to 0.5
Outputs:
- fine_final: bfloat16 [16384, 128], P(('parts', 'region', 'sub')), parts along dimension 0
The draws below stay inside these ranges and needn't reach their ends.
There are 2 independent parts, one for each index of `parts`. The reference program is written for one: setup_inputs(seed, part) draws one part's arguments, and reference() takes and returns one part's arrays. A program takes and returns all parts, laid end to end along the dimension named above; an argument that names none is the same for every part. Nothing has to cross between parts.
Inputs may be any that keep to these rules, and one draw needn't show every extreme that they name: `pool_dest`: among the rows of one device no region index is named by more than 256 rows; in some devices one index is named by exactly 256.
All inputs are finite; a program needn't handle non-finite values.
Results may differ from the reference program's by a relative error of at most 0.013.
Values may be sent and summed in bfloat16 or wider, within the bound.
No kernel may reach another device: no remote copies, remote signals or barrier semaphores. Data moves between devices by JAX's collectives and lax.ppermute only.
A program may use at most 64 MiB of HBM per device.

```python
import math
import jax
import jax.numpy as jnp
import numpy as np
from jax import lax

L = 128
NF_DEV = 512
NC3 = 2048
PASSES = 5
GROUP = 16
NC2_DEV = 256
EDGE_DEV = 3072
EDGE2_DEV = 1536
HALO = 64
HALO2 = 32
CAP = 256
TOP_EDGES = 8192
FINE = 8192
FINE_EDGES = 49152
COARSE = 4096
COARSE_EDGES = 24576
N_REGION = 4
N_SUB = 4


def with_ends(entries, own_key, smallest, top_value):
    dims = entries.shape
    index_at = [jax.random.randint(jax.random.fold_in(own_key, axis), (), 0, dims[axis]) for axis in range(len(dims))]
    entries = entries.at[tuple(index_at)].set(smallest)
    longest = dims.index(max(dims))
    index_at[longest] = (index_at[longest] + 1) % dims[longest]
    return entries.at[tuple(index_at)].set(top_value)


def block_scale(stream_key, extent, split, smallest, high):
    def one(axis_at, shards_of):
        heights = jax.random.uniform(jax.random.fold_in(jax.random.fold_in(stream_key, 6), axis_at), (shards_of,), jnp.float32, smallest / len(split), high / len(split))
        return jnp.repeat(jnp.exp(heights), extent[axis_at] // shards_of).reshape((-1,) + (1,) * (len(extent) - axis_at - 1))

    gain = one(*split[0])
    for cut in split[1:]:
        gain = gain * one(*cut)
    return gain


def cumulative_ranks(count, slope):
    loads = [(1 << 20) // math.isqrt(rank ** slope) + 1 for rank in range(1, count + 1)]
    spread = 1 + sum(loads) // (1 << 30)
    return np.cumsum(np.array([max(1, weight // spread) for weight in loads]))


def ranked_ids(rng, shape, count, skew):
    listing = cumulative_ranks(count, skew)
    ticket = jax.random.randint(jax.random.fold_in(rng, 1), shape, 0, int(listing[count - 1]))
    grade = jnp.searchsorted(jnp.asarray(listing, jnp.int32), ticket, side="right")
    return jax.random.permutation(jax.random.fold_in(rng, 2), count)[grade].astype(jnp.int32)


def shared_out(rng, own, number, rows, number_of, top, bound, slope):
    order = jax.random.permutation(rng, number_of)
    crowded, common = portions_of(number_of, rows * top, bound, slope, True), portions_of(number_of, rows * top, bound, slope, False)
    places = jnp.arange(number_of)

    def named(tallies, offset_by):
        used = int((tallies > 0).sum())
        fixed = max(1, used // 4)
        moved = fixed + (places - fixed + offset_by * (used - fixed)) % max(1, number_of - fixed)
        return jnp.zeros((number_of,), jnp.int32).at[order[jnp.where(places < fixed, places, moved)]].set(jnp.asarray(tallies, jnp.int32))

    tallies = jnp.where(number % 4 == 0, named(crowded, number // 4), named(common, number - number // 4 - 1))
    mixed = jax.random.permutation(jax.random.fold_in(own, 3), number_of)
    donor, taker = mixed[0:number_of // 2 * 2:2], mixed[1:number_of // 2 * 2:2]
    slack = jnp.minimum(tallies[donor] - 1, bound - tallies[taker]) // 2
    slack = jnp.where((donor == order[0]) | (taker == order[0]) | (tallies[taker] == 0), 0, jnp.maximum(slack, 0))
    moved = jax.random.randint(jax.random.fold_in(own, 4), (number_of // 2,), 0, 1 << 20) % (slack + 1)
    tallies = tallies.at[donor].add(-moved).at[taker].add(moved)
    items = jnp.searchsorted(jnp.cumsum(tallies), jnp.arange(rows * top), side="right").astype(jnp.int32)
    table = items.reshape(top, rows).T
    table = table[jax.random.permutation(jax.random.fold_in(own, 1), rows)]
    offset_by = jax.random.randint(jax.random.fold_in(own, 2), (rows, 1), 0, top)
    return jnp.take_along_axis(table, (jnp.arange(top)[None, :] + offset_by) % top, axis=1)


def portions_of(count, total, limit, lean, full):
    loads = [(1 << 20) // math.isqrt(rank ** lean) + 1 for rank in range(1, count + 1)]
    largest = limit if full else min(limit, max(-(-total // count), total * loads[0] // sum(loads)))
    least = 1 if total - largest >= count - 1 else 0
    holding, rest = [largest] + [least] * (count - 1), total - largest - least * (count - 1)
    while rest > 0:
        free = [i for i in range(1, count) if holding[i] < largest] or [i for i in range(1, count) if holding[i] < limit]
        whole, budget = sum([loads[i] for i in free]), rest
        for i in free:
            addition = min(limit - holding[i], max(1, budget * loads[i] // whole), rest)
            holding[i] = holding[i] + addition
            rest = rest - addition
    return np.array(holding)


def scatter_about(rng, extent, scale, most, split=(), held_as=jnp.bfloat16):
    loudness = block_scale(rng, extent, split, -0.22, 0.18) if split else 1.0
    values = jax.random.normal(rng, extent, jnp.float32) * scale * loudness
    return jnp.minimum(jnp.maximum(values, -most), most).astype(held_as)


def setup_inputs(seed: int = 0, part: int = 0) -> dict:
    key_of = jax.random.split(jax.random.key(seed), 20)
    own_keys = jax.random.split(jax.random.fold_in(key_of[19], part), 20)
    node_feats = scatter_about(own_keys[0], (FINE, L), 1.0, 6.0, ((0, 16),))
    fine_senders = with_ends(jax.random.randint(own_keys[1], (FINE_EDGES,), 0, NF_DEV + 2 * HALO), jax.random.fold_in(own_keys[1], 1), 0, (NF_DEV + 2 * HALO) - 1).astype(jnp.int32)
    fine_receivers = with_ends(jax.random.randint(own_keys[2], (FINE_EDGES,), 0, NF_DEV), jax.random.fold_in(own_keys[2], 1), 0, NF_DEV - 1).astype(jnp.int32)
    fine_edges = scatter_about(own_keys[3], (FINE_EDGES, L), 1.0, 6.0, ((0, 16),))
    halo_rows = with_ends(jax.random.randint(own_keys[4], (2 * GROUP, HALO), 0, NF_DEV), jax.random.fold_in(own_keys[4], 1), 0, NF_DEV - 1).astype(jnp.int32)
    coarse_senders = with_ends(jax.random.randint(own_keys[5], (COARSE_EDGES,), 0, NC2_DEV + 2 * HALO2), jax.random.fold_in(own_keys[5], 1), 0, (NC2_DEV + 2 * HALO2) - 1).astype(jnp.int32)
    coarse_receivers = with_ends(jax.random.randint(own_keys[6], (COARSE_EDGES,), 0, NC2_DEV), jax.random.fold_in(own_keys[6], 1), 0, NC2_DEV - 1).astype(jnp.int32)
    coarse_edges = scatter_about(own_keys[7], (COARSE_EDGES, L), 1.0, 6.0, ((0, 16),))
    coarse_halo_rows = with_ends(jax.random.randint(own_keys[8], (2 * GROUP, HALO2), 0, NC2_DEV), jax.random.fold_in(own_keys[8], 1), 0, NC2_DEV - 1).astype(jnp.int32)
    pool_dest_keys = jax.random.split(jax.random.fold_in(own_keys[9], 1), FINE // NF_DEV)
    pool_dest_turns = jax.random.permutation(jax.random.fold_in(own_keys[9], 3), FINE // NF_DEV)
    pool_dest = jax.vmap(lambda own, number: shared_out(jax.random.fold_in(own_keys[9], 2), own, number, NF_DEV, N_REGION, 1, CAP, 2))(pool_dest_keys, pool_dest_turns).reshape((FINE, 1))
    pool_target = with_ends(jax.random.randint(own_keys[10], (FINE,), 0, NC2_DEV), jax.random.fold_in(own_keys[10], 1), 0, NC2_DEV - 1).astype(jnp.int32)
    pool3_target = with_ends(ranked_ids(own_keys[11], (COARSE,), NC3, 3), jax.random.fold_in(own_keys[11], 3), 0, NC3 - 1).astype(jnp.int32)
    top_senders = with_ends(jax.random.randint(own_keys[12], (TOP_EDGES,), 0, NC3), jax.random.fold_in(own_keys[12], 1), 0, NC3 - 1).astype(jnp.int32)
    top_receivers = with_ends(jax.random.randint(own_keys[13], (TOP_EDGES,), 0, NC3), jax.random.fold_in(own_keys[13], 1), 0, NC3 - 1).astype(jnp.int32)
    top_edges = scatter_about(own_keys[14], (TOP_EDGES, L), 1.0, 6.0)
    edge_in = scatter_about(key_of[15], (PASSES, 3 * L, L), (3 * L) ** -0.5, 0.3125)
    edge_out = scatter_about(key_of[16], (PASSES, L, L), L ** -0.5, 0.5)
    node_in = scatter_about(key_of[17], (PASSES, 2 * L, L), (2 * L) ** -0.5, 0.375)
    node_out = scatter_about(key_of[18], (PASSES, L, L), L ** -0.5, 0.5)
    return {"node_feats": node_feats, "fine_senders": fine_senders, "fine_receivers": fine_receivers, "fine_edges": fine_edges, "halo_rows": halo_rows, "coarse_senders": coarse_senders, "coarse_receivers": coarse_receivers, "coarse_edges": coarse_edges, "coarse_halo_rows": coarse_halo_rows, "pool_dest": pool_dest, "pool_target": pool_target, "pool3_target": pool3_target, "top_senders": top_senders, "top_receivers": top_receivers, "top_edges": top_edges, "edge_in": edge_in, "edge_out": edge_out, "node_in": node_in, "node_out": node_out}


EPSILON = 1e-05

def normalize(values):
    centred = values - lax.optimization_barrier(jnp.mean(values, axis=-1, keepdims=True))
    variance = lax.optimization_barrier(jnp.mean(centred * centred, axis=-1, keepdims=True))
    return centred * lax.rsqrt(variance + EPSILON)

def perceptron(features, first_layer, second_layer):
    hidden = jnp.maximum(jnp.dot(features, first_layer, preferred_element_type=jnp.float32), 0.0).astype(jnp.bfloat16)
    return normalize(jnp.dot(hidden, second_layer, preferred_element_type=jnp.float32))

def message_pass(node_table, own_nodes, senders, receivers, edge_feat, edge_first, edge_second, node_first, node_second):
    joined = jnp.concatenate([node_table[senders], node_table[receivers], edge_feat], axis=1)
    new_edges = (edge_feat.astype(jnp.float32) + perceptron(joined, edge_first, edge_second)).astype(jnp.bfloat16)
    summed = jax.ops.segment_sum(new_edges.astype(jnp.float32), receivers, own_nodes.shape[0]).astype(jnp.bfloat16)
    joined_nodes = jnp.concatenate([own_nodes, summed], axis=1)
    new_nodes = (own_nodes.astype(jnp.float32) + perceptron(joined_nodes, node_first, node_second)).astype(jnp.bfloat16)
    return (new_nodes, new_edges)

def with_halo(nodes, row_lists):
    outgoing = jax.vmap(jax.vmap(lambda own_rows, listed: own_rows[listed]))(nodes, row_lists)
    blank = jnp.zeros_like(outgoing[:1, :, 0])
    from_lower = jnp.concatenate([blank, outgoing[:-1, :, 1]], axis=0)
    from_higher = jnp.concatenate([outgoing[1:, :, 0], blank], axis=0)
    return jnp.concatenate([nodes, from_lower, from_higher], axis=2)

def level_pass(nodes, row_lists, senders, receivers, edge_feat, weights, index):
    node_table = with_halo(nodes, row_lists)
    count = N_REGION * N_SUB

    def flatten(array):
        return array.reshape((count,) + array.shape[2:])

    def one_device(operands):
        return message_pass(*operands, *[matrix[index] for matrix in weights])
    new_nodes, new_edges = lax.map(one_device, (flatten(node_table), flatten(nodes), flatten(senders), flatten(receivers), flatten(edge_feat)))
    return (new_nodes.reshape(nodes.shape), new_edges.reshape(edge_feat.shape))

def reference(node_feats, fine_senders, fine_receivers, fine_edges, halo_rows, coarse_senders, coarse_receivers, coarse_edges, coarse_halo_rows, pool_dest, pool_target, pool3_target, top_senders, top_receivers, top_edges, edge_in, edge_out, node_in, node_out):
    weights = (edge_in, edge_out, node_in, node_out)
    grid = (N_REGION, N_SUB)
    fine_nodes = node_feats.reshape(grid + (NF_DEV, L))
    fine_links = (fine_senders.reshape(grid + (EDGE_DEV,)), fine_receivers.reshape(grid + (EDGE_DEV,)))
    coarse_links = (coarse_senders.reshape(grid + (EDGE2_DEV,)), coarse_receivers.reshape(grid + (EDGE2_DEV,)))
    fine_lists = halo_rows.reshape(grid + (2, HALO))
    coarse_lists = coarse_halo_rows.reshape(grid + (2, HALO2))
    fine_down, fine_edges2 = level_pass(fine_nodes, fine_lists, fine_links[0], fine_links[1], fine_edges.reshape(grid + (EDGE_DEV, L)), weights, 0)
    column = jnp.arange(N_SUB, dtype=jnp.int32)[None, :, None]
    parent = ((pool_dest.reshape(grid + (NF_DEV,)) * N_SUB + column) * NC2_DEV + pool_target.reshape(grid + (NF_DEV,))).reshape(-1).astype(jnp.int32)
    fine_flat = fine_down.reshape(FINE, L)
    totals = jax.ops.segment_sum(fine_flat.astype(jnp.float32), parent, COARSE)
    members = jax.ops.segment_sum(jnp.ones((FINE,), jnp.float32), parent, COARSE)
    coarse = (totals / jnp.maximum(members, 1.0)[:, None]).astype(jnp.bfloat16)
    coarse_down, coarse_edges2 = level_pass(coarse.reshape(grid + (NC2_DEV, L)), coarse_lists, coarse_links[0], coarse_links[1], coarse_edges.reshape(grid + (EDGE2_DEV, L)), weights, 1)
    coarse_flat = coarse_down.reshape(COARSE, L)
    top_totals = jax.ops.segment_sum(coarse_flat.astype(jnp.float32), pool3_target, NC3)
    top_members = jax.ops.segment_sum(jnp.ones((COARSE,), jnp.float32), pool3_target, NC3)
    top = (top_totals / jnp.maximum(top_members, 1.0)[:, None]).astype(jnp.bfloat16)
    top_final, unused_edges = message_pass(top, top, top_senders, top_receivers, top_edges, *[matrix[2] for matrix in weights])
    coarse_up = (coarse_flat.astype(jnp.float32) + top_final[pool3_target].astype(jnp.float32)).astype(jnp.bfloat16)
    coarse_final, unused_coarse = level_pass(coarse_up.reshape(grid + (NC2_DEV, L)), coarse_lists, coarse_links[0], coarse_links[1], coarse_edges2, weights, 3)
    fine_up = (fine_flat.astype(jnp.float32) + coarse_final.reshape(COARSE, L)[parent].astype(jnp.float32)).astype(jnp.bfloat16)
    fine_final, unused_fine = level_pass(fine_up.reshape(grid + (NF_DEV, L)), fine_lists, fine_links[0], fine_links[1], fine_edges2, weights, 4)
    return fine_final.reshape(FINE, L)
```

```python
import functools

import jax
import jax.numpy as jnp
from jax import lax
from jax.experimental import pallas as pl
from jax.experimental.pallas import tpu as pltpu
from jax.sharding import PartitionSpec as P

EPSILON = 1e-05
TOP = 2048
LANES = 128
F32, BF16, I32 = jnp.float32, jnp.bfloat16, jnp.int32
TAIL = 16
LIMIT = 40 * 1024 * 1024


def dot(a, b):
    return jnp.dot(a, b, preferred_element_type=F32)


def lane_iota(rows, first=0):
    return lax.broadcasted_iota(I32, (rows, LANES), 1) + first


def column(row):
    return jnp.transpose(jnp.broadcast_to(row, (LANES, row.shape[1])))


def columns(rows):
    return jnp.concatenate([column(rows[i : i + 1]) for i in range(rows.shape[0])], axis=0)


def hot(mask):
    return jnp.where(mask, 1.0, 0.0).astype(BF16)


def hot_rows(col, count):
    return jnp.concatenate(
        [hot(col == lane_iota(col.shape[0], first)) for first in range(0, count, LANES)], axis=1
    )


def hot_cols(rows, count):
    place = lax.broadcasted_iota(I32, (count, LANES), 0)
    return jnp.concatenate([hot(place == rows[i : i + 1]) for i in range(rows.shape[0])], axis=1)


def hot_codes(col, rows):
    return jnp.concatenate([hot(col == rows[i : i + 1]) for i in range(rows.shape[0])], axis=1)


def normalize(values):
    centred = values - jnp.mean(values, axis=-1, keepdims=True)
    variance = jnp.mean(centred * centred, axis=-1, keepdims=True)
    return centred * lax.rsqrt(variance + EPSILON)


def perceptron(features, first, second):
    hidden = jnp.maximum(dot(features, first), 0.0).astype(BF16)
    return normalize(dot(hidden, second))


def node_update(nodes, summed, first, second):
    joined = jnp.concatenate([nodes, summed.astype(BF16)], axis=1)
    return (nodes.astype(F32) + perceptron(joined, first, second)).astype(BF16)


def message_pass(table, own, senders, receivers, edges, weights, new_edges=None, step=1024):
    edge_in, edge_out, node_in, node_out = weights
    first, second = edge_in[...], edge_out[...]
    nodes = table[:own]
    short = -table.shape[0] % LANES
    if short:
        table = jnp.concatenate([table, jnp.zeros((short, LANES), BF16)], axis=0)
    count = edges.shape[0]
    step = min(step, count)
    summed = jnp.zeros((own, LANES), F32)
    for at in range(0, count, step):
        rows = slice(at // LANES, (at + step) // LANES)
        send, recv = senders[rows, :], receivers[rows, :]
        from_send = dot(hot_rows(columns(send), table.shape[0]), table).astype(BF16)
        from_recv = dot(hot_rows(columns(recv), own), nodes).astype(BF16)
        edge = edges[at : at + step, :]
        joined = jnp.concatenate([from_send, from_recv, edge], axis=1)
        new = (edge.astype(F32) + perceptron(joined, first, second)).astype(BF16)
        if new_edges is not None:
            new_edges[at : at + step, :] = new
        summed = summed + dot(hot_cols(recv, own), new)
    return node_update(nodes, summed, node_in[...], node_out[...])


def block_weights(refs, index):
    return [ref.at[index] for ref in refs]


def tail_of(block, count):
    return block[count : count + TAIL, :].astype(F32).astype(I32)


def row_layout(fine, coarse):
    f, c = fine // LANES, coarse // LANES
    return {"dest": 0, "target": f, "high": 2 * f, "low": 2 * f + c, "coarse": 2 * f + 2 * c, "fine_high": 2 * f + 2 * c + 1, "fine_low": 2 * f + 2 * c + 2}


def near_tails(tails, me, count):
    out = []
    for other in (me - 1, me + 1):
        there = jnp.logical_and(other >= 0, other < count)
        near = jnp.where(there, jnp.bitwise_xor(me, other), 0)
        picked = sum(jnp.where(near == j, tail, 0) for j, tail in enumerate(tails))
        out.append((other, there, picked))
    return out


def pick_kernel(nodes, rows, lower, higher):
    for at, out in ((0, lower), (1, higher)):
        col = column(rows[at : at + 1, :])
        out[...] = dot(hot_rows(col, nodes.shape[0]), nodes[...]).astype(BF16)


def fine_kernel(nodes, from_lower, from_higher, senders, receivers, edges, tail, *rest):
    *weights, payload, new_edges = rest
    weights = block_weights(weights, 0)
    own = nodes.shape[0]
    table = jnp.concatenate([nodes[...], from_lower[...], from_higher[...]], axis=0)
    payload[:own, :] = message_pass(table, own, senders, receivers, edges, weights, new_edges)
    payload[own:, :] = tail[...]


def coarse_kernel(regions, halo, coarse, *refs):
    blocks, (senders, receivers, edges, *rest) = refs[:regions], refs[regions:]
    *weights, payload, new_edges = rest
    weights = block_weights(weights, 1)
    me = lax.axis_index("region")
    fine = blocks[0].shape[0] - TAIL
    at = row_layout(fine, coarse)
    tails = [tail_of(block, fine) for block in blocks]
    near = near_tails(tails, me, regions)
    codes = [me * coarse + lax.broadcasted_iota(I32, (coarse, LANES), 0)]
    for side, (other, there, tail) in enumerate(near):
        listed = tail[at["coarse"] : at["coarse"] + 1, :]
        first = halo * (1 - side)
        col = columns(listed)[first : first + halo]
        codes.append(jnp.where(there, other * coarse + col, -1))
    codes = jnp.concatenate(codes, axis=0)
    total = jnp.zeros((codes.shape[0], LANES), F32)
    members = jnp.zeros((codes.shape[0], LANES), F32)
    for block, tail in zip(blocks, tails):
        f = fine // LANES
        parent = tail[at["dest"] : at["dest"] + f] * coarse + tail[at["target"] : at["target"] + f]
        chosen = hot_codes(codes, parent)
        total = total + dot(chosen, block[:fine, :])
        for i in range(f):
            members = members + chosen[:, i * LANES : (i + 1) * LANES].astype(F32)
    members = jnp.sum(members, axis=1, keepdims=True)
    table = (total / jnp.maximum(members, 1.0)).astype(BF16)
    payload[:coarse, :] = message_pass(table, coarse, senders, receivers, edges, weights, new_edges)
    own_tail = tails[0]
    c = coarse // LANES
    payload[coarse:, :] = jnp.concatenate(
        [own_tail[at["high"] : at["high"] + 2 * c], jnp.zeros((TAIL - 2 * c, LANES), I32)], axis=0
    ).astype(F32).astype(BF16)


def compact(first, ranks, codes, edges, size, at_once=8):
    place = lax.broadcasted_iota(I32, (size, LANES), 0) + first

    def body(g, carry):
        latents, found = carry
        rank = ranks[pl.ds(pl.multiple_of(g * at_once, at_once), at_once), :]
        code = codes[pl.ds(pl.multiple_of(g * at_once, at_once), at_once), :]
        hots = []
        for i in range(at_once):
            mask = place == rank[i : i + 1]
            hots.append(hot(mask))
            found = found + jnp.where(mask, code[i : i + 1], 0)
        wide = at_once * LANES
        rows = edges[pl.ds(pl.multiple_of(g * wide, wide), wide), :]
        return latents + dot(jnp.concatenate(hots, axis=1), rows), found

    zero = jnp.zeros((size, LANES), F32), jnp.zeros((size, LANES), I32)
    latents, found = lax.fori_loop(0, ranks.shape[0] // at_once, body, zero)
    found = jnp.sum(found.astype(F32), axis=1, keepdims=True).astype(I32)
    return latents.astype(BF16), jnp.broadcast_to(found, (size, LANES))


def listed_kernel(regions, halo, coarse, wide, size, *refs):
    blocks, refs = refs[:regions], refs[regions:]
    senders, receivers, edges, parents, halo_codes, ranks, codes, latents, found, number = refs
    me = lax.axis_index("region")
    fine = blocks[0].shape[0] - TAIL
    at = row_layout(fine, coarse)
    tails = [tail_of(block, fine) for block in blocks]
    c = coarse // LANES

    def own_parents(tail):
        return tail[at["high"] : at["high"] + c] * LANES + tail[at["low"] : at["low"] + c]

    cols = [columns(own_parents(tails[0]))]
    for side, (other, there, tail) in enumerate(near_tails(tails, me, regions)):
        first = halo * (1 - side)
        col = columns(tail[at["coarse"] : at["coarse"] + 1])[first : first + halo]
        halo_codes[side * halo : (side + 1) * halo, :] = jnp.where(there, other * coarse + col, -1)
        theirs = own_parents(tail).astype(F32)
        value = jnp.zeros((halo, LANES), F32)
        for i in range(c):
            value = value + jnp.where(col == lane_iota(halo, i * LANES), theirs[i : i + 1], 0.0)
        value = jnp.broadcast_to(jnp.sum(value, axis=1, keepdims=True), (halo, LANES)).astype(I32)
        cols.append(jnp.where(there, value, -1))
    cols.append(jnp.full((wide - coarse - 2 * halo, LANES), -1, I32))
    cols = jnp.concatenate(cols, axis=0)
    parents[...] = cols
    count = receivers.shape[0]
    needed = []
    for i in range(count):
        match = jnp.where(cols == receivers[i : i + 1, :], 1.0, 0.0)
        needed.append(jnp.max(match, axis=0, keepdims=True))
    needed = jnp.concatenate(needed, axis=0)
    upto = jnp.where(lax.broadcasted_iota(I32, (LANES, LANES), 0) <= lane_iota(LANES), 1.0, 0.0)
    inside = dot(needed.astype(BF16), upto.astype(BF16))
    sums = jnp.broadcast_to(inside[:, LANES - 1 :], (count, LANES))
    square = (count, count)
    before = lax.broadcasted_iota(I32, square, 1) < lax.broadcasted_iota(I32, square, 0)
    rank = dot(hot(before), sums.astype(BF16)) + inside - 1.0
    ranks[...] = jnp.where(needed > 0.0, rank, -1.0).astype(I32)
    codes[...] = senders[...] * TOP + receivers[...]
    number[0] = jnp.sum(needed).astype(I32)
    latents[...], found[...] = compact(0, ranks, codes, edges, size)


def parent_kernel(regions, halo, coarse, *refs):
    blocks, (table, parents) = refs[:regions], refs[regions:]
    me = lax.axis_index("region")
    fine = blocks[0].shape[0] - TAIL
    at = row_layout(fine, coarse)
    tails = [tail_of(block, fine) for block in blocks]
    f = fine // LANES

    def own_parents(tail):
        return tail[at["dest"] : at["dest"] + f] * coarse + tail[at["target"] : at["target"] + f]

    table[:fine, :] = blocks[0][:fine, :]
    parents[:fine, :] = columns(own_parents(tails[0]))
    for side, (other, there, tail) in enumerate(near_tails(tails, me, regions)):
        rows = slice(fine + side * halo, fine + (side + 1) * halo)
        first = halo * (1 - side)
        listed = tail[at["fine_high"] : at["fine_high"] + 1] * LANES + tail[at["fine_low"] : at["fine_low"] + 1]
        col = columns(listed)[first : first + halo]
        theirs = own_parents(tail).astype(F32)
        value = jnp.zeros((halo, LANES), F32)
        for i in range(f):
            value = value + jnp.where(col == lane_iota(halo, i * LANES), theirs[i : i + 1], 0.0)
        value = jnp.broadcast_to(jnp.sum(value, axis=1, keepdims=True), (halo, LANES)).astype(I32)
        parents[rows, :] = jnp.where(there, value, -1)
        total = jnp.zeros((halo, LANES), F32)
        for j, block in enumerate(blocks):
            here = jnp.logical_and(there, jnp.bitwise_xor(me, j) == other)
            total = total + dot(hot_rows(jnp.where(here, col, -1), fine), block[:fine, :])
        table[rows, :] = total.astype(BF16)


def pooled(col, blocks, coarse):
    c = coarse // LANES

    def add(block, sums):
        total, members = sums
        tail = tail_of(block, coarse)
        chosen = hot_codes(col, tail[:c] * LANES + tail[c : 2 * c])
        total = total + dot(chosen, block[:coarse, :])
        for i in range(c):
            members = members + chosen[:, i * LANES : (i + 1) * LANES].astype(F32)
        return total, members

    sums = (jnp.zeros((col.shape[0], LANES), F32),) * 2
    if isinstance(blocks, tuple):
        for block in blocks:
            sums = add(block, sums)
    else:
        sums = lax.fori_loop(0, blocks.shape[0], lambda n, sums: add(blocks.at[n], sums), sums)
    total, members = sums
    members = jnp.sum(members, axis=1, keepdims=True)
    return (total / jnp.maximum(members, 1.0)).astype(BF16)


def as_rows(col):
    return jnp.concatenate(
        [jnp.transpose(col[i : i + LANES])[:1] for i in range(0, col.shape[0], LANES)], axis=0
    )


def top_kernel(regions, halo, coarse, size, count, *refs):
    blocks, refs = refs[:count] if count > 1 else refs[0], refs[count:]
    parents, halo_codes, ranks, codes, latents, found, number, all_edges = refs[:8]
    senders, receivers, edges = refs[8:11]
    top_weights, weights = block_weights(refs[11:15], 2), block_weights(refs[11:15], 3)
    out, agg = refs[15:]
    me = lax.axis_index("region")
    subs = lax.axis_size("sub")
    own_sub = lambda j: blocks[j * subs] if count > 1 else blocks.at[j * subs]
    wide = parents.shape[0]
    mine = parents[...]
    top_own = pooled(mine, blocks, coarse)
    mine_rows = as_rows(mine)
    row_at = lax.broadcasted_iota(I32, (wide, LANES), 0)
    firsts = []
    for i in range(wide // LANES):
        earlier = jnp.logical_and(mine == mine_rows[i : i + 1], row_at < lane_iota(wide, i * LANES))
        seen = jnp.max(jnp.where(earlier, 1.0, 0.0), axis=0, keepdims=True)
        firsts.append(jnp.where(seen > 0.0, -2, mine_rows[i : i + 1]))
    firsts = jnp.concatenate(firsts, axis=0)
    first, second = top_weights[0][...], top_weights[1][...]
    agg[...] = jnp.zeros_like(agg)
    total = number[0]

    def one(at, edge, code):
        place = lax.broadcasted_iota(I32, (size, LANES), 0) + at
        send = jnp.right_shift(code, TOP.bit_length() - 1)
        recv = jnp.where(place < total, jnp.bitwise_and(code, TOP - 1), -3)
        from_send = pooled(send, blocks, coarse)
        from_recv = dot(hot_codes(recv, firsts), top_own).astype(BF16)
        joined = jnp.concatenate([from_send, from_recv, edge], axis=1)
        new = (edge.astype(F32) + perceptron(joined, first, second)).astype(BF16)
        agg[...] += dot(hot_codes(mine, as_rows(recv)), new)

    one(0, latents[...], found[...])

    def more(b, carry):
        edge, code = compact(b * size, ranks, codes, all_edges, size)
        one(b * size, edge, code)
        return carry

    lax.fori_loop(1, (total + size - 1) // size, more, 0)
    top_final = node_update(top_own, agg[...], top_weights[2][...], top_weights[3][...])
    wanted = halo_codes[...]
    near = jnp.zeros((2 * halo, LANES), F32)
    for j in range(regions):
        col = wanted - jnp.bitwise_xor(me, j) * coarse
        near = near + dot(hot_rows(col, coarse), own_sub(j)[:coarse, :])
    down = jnp.concatenate([own_sub(0)[:coarse, :].astype(F32), near], axis=0)
    table = (down + top_final[: coarse + 2 * halo].astype(F32)).astype(BF16)
    out[...] = message_pass(table, coarse, senders, receivers, edges, weights)


def last_kernel(regions, *refs):
    blocks, refs = refs[:regions], refs[regions:]
    down, parents, senders, receivers, edges, *weights, out = refs
    weights = block_weights(weights, 4)
    me = lax.axis_index("region")
    own, coarse = out.shape[0], blocks[0].shape[0]
    total = down[...].astype(F32)
    wanted = parents[...]
    for j, block in enumerate(blocks):
        col = wanted - jnp.bitwise_xor(me, j) * coarse
        total = total + dot(hot_rows(col, coarse), block[...])
    out[...] = message_pass(total.astype(BF16), own, senders, receivers, edges, weights)


def call(kernel, args, outs, scratch=(), scalars=(), scalar_outs=()):
    specs = [pl.BlockSpec(memory_space=pltpu.SMEM if i in scalars else pltpu.VMEM) for i in range(len(args))]
    out_specs = [pl.BlockSpec(memory_space=pltpu.SMEM if i in scalar_outs else pltpu.VMEM) for i in range(len(outs))]
    return pl.pallas_call(
        kernel,
        out_shape=[jax.ShapeDtypeStruct(shape, dtype) for shape, dtype in outs],
        in_specs=specs,
        out_specs=out_specs,
        scratch_shapes=list(scratch),
        compiler_params=pltpu.CompilerParams(vmem_limit_bytes=LIMIT),
    )(*args)


def over_region(rows):
    count = lax.axis_size("region")
    blocks = {0: rows}
    bit = count // 2
    while bit:
        for j in list(blocks):
            blocks[j + bit] = lax.ppermute(blocks[j], "region", [(i, i ^ bit) for i in range(count)])
        bit //= 2
    return [blocks[j] for j in range(count)]


def over_both(rows):
    regions, subs = lax.axis_size("region"), lax.axis_size("sub")
    turns = [rows] + [
        lax.ppermute(rows, "sub", [(i, (i + k) % subs) for i in range(subs)]) for k in range(1, subs)
    ]
    if regions * subs <= 16:
        spread = [over_region(turn) for turn in turns]
        return [spread[k][j] for j in range(regions) for k in range(subs)]
    blocks, bit = jnp.stack(turns), 1
    while bit < regions:
        there = lax.ppermute(blocks, "region", [(i, i ^ bit) for i in range(regions)])
        blocks, bit = jnp.concatenate([blocks, there]), 2 * bit
    return [blocks]


def on_device(
    node_feats,
    fine_senders,
    fine_receivers,
    fine_edges,
    halo_rows,
    coarse_senders,
    coarse_receivers,
    coarse_edges,
    coarse_halo_rows,
    pool_dest,
    pool_target,
    pool3_target,
    top_senders,
    top_receivers,
    top_edges,
    edge_in,
    edge_out,
    node_in,
    node_out,
):
    weights = (edge_in, edge_out, node_in, node_out)
    regions = lax.axis_size("region")
    fine, coarse = node_feats.shape[0], pool3_target.shape[0]
    halo, halo2 = halo_rows.shape[1], coarse_halo_rows.shape[1]
    rows = lambda a: a.reshape(-1, LANES)
    fine_send, fine_recv = rows(fine_senders), rows(fine_receivers)
    coarse_send, coarse_recv = rows(coarse_senders), rows(coarse_receivers)
    top_send, top_recv = rows(top_senders), rows(top_receivers)

    to_lower, to_higher = call(
        pick_kernel, [node_feats, halo_rows], [((halo, LANES), BF16)] * 2
    )
    up = [(i, i + 1) for i in range(regions - 1)]
    from_lower = lax.ppermute(to_higher, "region", up)
    from_higher = lax.ppermute(to_lower, "region", [(j, i) for i, j in up])

    parent3, listed = rows(pool3_target), halo_rows.reshape(1, -1)
    tail = jnp.concatenate(
        [
            rows(pool_dest),
            rows(pool_target),
            parent3 // LANES,
            parent3 % LANES,
            jnp.pad(coarse_halo_rows.reshape(1, -1), ((0, 0), (0, LANES - 2 * halo2))),
            listed // LANES,
            listed % LANES,
        ],
        axis=0,
    )
    tail = jnp.pad(tail, ((0, TAIL - tail.shape[0]), (0, 0))).astype(BF16)

    payload, fine_edges2 = call(
        fine_kernel,
        [node_feats, from_lower, from_higher, fine_send, fine_recv, fine_edges, tail, *weights],
        [((fine + TAIL, LANES), BF16), (fine_edges.shape, BF16)],
    )
    blocks = over_region(payload)
    payload2, coarse_edges2 = call(
        functools.partial(coarse_kernel, regions, halo2, coarse),
        blocks + [coarse_send, coarse_recv, coarse_edges, *weights],
        [((coarse + TAIL, LANES), BF16), (coarse_edges.shape, BF16)],
    )
    wide = -(-(coarse + 2 * halo2) // LANES) * LANES
    size = min(512, top_edges.shape[0])
    parents, halo_codes, ranks, codes, latents, found, number = call(
        functools.partial(listed_kernel, regions, halo2, coarse, wide, size),
        blocks + [top_send, top_recv, top_edges],
        [
            ((wide, LANES), I32),
            ((2 * halo2, LANES), I32),
            (top_send.shape, I32),
            (top_send.shape, I32),
            ((size, LANES), BF16),
            ((size, LANES), I32),
            ((1,), I32),
        ],
        scalar_outs=(6,),
    )
    fine_table, fine_parents = call(
        functools.partial(parent_kernel, regions, halo, coarse),
        blocks,
        [((fine + 2 * halo, LANES), BF16), ((fine + 2 * halo, LANES), I32)],
    )
    blocks2 = over_both(payload2)
    (coarse_final,) = call(
        functools.partial(top_kernel, regions, halo2, coarse, size, len(blocks2)),
        blocks2
        + [parents, halo_codes, ranks, codes, latents, found, number, top_edges]
        + [coarse_send, coarse_recv, coarse_edges2, *weights],
        [((coarse, LANES), BF16)],
        scratch=[pltpu.VMEM((wide, LANES), F32)],
        scalars=(len(blocks2) + 6,),
    )
    (fine_final,) = call(
        functools.partial(last_kernel, regions),
        over_region(coarse_final) + [fine_table, fine_parents, fine_send, fine_recv, fine_edges2, *weights],
        [((fine, LANES), BF16)],
    )
    return fine_final


def solution(mesh):
    spread = ("parts", "region", "sub")
    rows, flat = P(spread, None), P(spread)
    in_specs = (
        (rows, flat, flat, rows, rows, flat, flat, rows, rows, rows, flat, flat)
        + (P("parts"), P("parts"), P("parts", None))
        + (P(),) * 4
    )
    return jax.shard_map(on_device, mesh=mesh, in_specs=in_specs, out_specs=rows, check_vma=False)
```

```python
import functools

import jax
import jax.numpy as jnp
from jax import lax
from jax.experimental import pallas as pl
from jax.experimental.pallas import tpu as pltpu
from jax.sharding import PartitionSpec as P

EPSILON = 1e-05
TOP = 2048
LANES = 128
F32, BF16, I32 = jnp.float32, jnp.bfloat16, jnp.int32
TAIL = 16
LIMIT = 32 * 1024 * 1024


def dot(a, b):
    return jnp.dot(a, b, preferred_element_type=F32)


def lane_iota(rows, first=0):
    return lax.broadcasted_iota(I32, (rows, LANES), 1) + first


def column(row):
    return jnp.transpose(jnp.broadcast_to(row, (LANES, row.shape[1])))


def columns(rows):
    return jnp.concatenate([column(rows[i : i + 1]) for i in range(rows.shape[0])], axis=0)


def hot(mask):
    return jnp.where(mask, 1.0, 0.0).astype(BF16)


def hot_rows(col, count):
    return jnp.concatenate(
        [hot(col == lane_iota(col.shape[0], first)) for first in range(0, count, LANES)], axis=1
    )


def hot_cols(rows, count):
    place = lax.broadcasted_iota(I32, (count, LANES), 0)
    return jnp.concatenate([hot(place == rows[i : i + 1]) for i in range(rows.shape[0])], axis=1)


def hot_codes(col, rows):
    return jnp.concatenate([hot(col == rows[i : i + 1]) for i in range(rows.shape[0])], axis=1)


def normalize(values):
    centred = values - jnp.mean(values, axis=-1, keepdims=True)
    variance = jnp.mean(centred * centred, axis=-1, keepdims=True)
    return centred * lax.rsqrt(variance + EPSILON)


def perceptron(features, first, second):
    hidden = jnp.maximum(dot(features, first), 0.0).astype(BF16)
    return normalize(dot(hidden, second))


def node_update(nodes, summed, first, second):
    joined = jnp.concatenate([nodes, summed.astype(BF16)], axis=1)
    return (nodes.astype(F32) + perceptron(joined, first, second)).astype(BF16)


def message_pass(table, own, senders, receivers, edges, weights, new_edges=None, step=1024):
    nodes = table[:own]
    short = -table.shape[0] % LANES
    if short:
        table = jnp.concatenate([table, jnp.zeros((short, LANES), BF16)], axis=0)
    senders, receivers, edges = senders.get(), receivers.get(), edges.get()
    count = edges.shape[0]
    step = min(step, count)
    first, second = weights[0].get()[...], weights[1].get()[...]
    summed = jnp.zeros((own, LANES), F32)
    for at in range(0, count, step):
        rows = slice(at // LANES, (at + step) // LANES)
        send, recv = senders[rows, :], receivers[rows, :]
        from_send = dot(hot_rows(columns(send), table.shape[0]), table).astype(BF16)
        from_recv = dot(hot_rows(columns(recv), own), nodes).astype(BF16)
        edge = edges[at : at + step, :]
        joined = jnp.concatenate([from_send, from_recv, edge], axis=1)
        new = (edge.astype(F32) + perceptron(joined, first, second)).astype(BF16)
        if new_edges is not None:
            new_edges[at : at + step, :] = new
        summed = summed + dot(hot_cols(recv, own), new)
    return node_update(nodes, summed, weights[2].get()[...], weights[3].get()[...])


def tail_of(block, count):
    return block[count : count + TAIL, :].astype(F32).astype(I32)


def row_layout(fine, coarse):
    f, c = fine // LANES, coarse // LANES
    return {"dest": 0, "target": f, "high": 2 * f, "low": 2 * f + c, "coarse": 2 * f + 2 * c, "fine_high": 2 * f + 2 * c + 1, "fine_low": 2 * f + 2 * c + 2}


def near_tails(tails, me, count):
    out = []
    for other in (me - 1, me + 1):
        there = jnp.logical_and(other >= 0, other < count)
        near = jnp.where(there, jnp.bitwise_xor(me, other), 0)
        picked = sum(jnp.where(near == j, tail, 0) for j, tail in enumerate(tails))
        out.append((other, there, picked))
    return out


def pick_kernel(halo, coarse_halo, fine, coarse, nodes, rows, coarse_rows, dest, target, parent, lower, higher, lists):
    at = row_layout(fine, coarse)
    lists[...] = jnp.zeros_like(lists)
    listed, coarse_listed = rows.get()[...], coarse_rows.get()[...]
    for side in (0, 1):
        lists[at["coarse"] : at["coarse"] + 1, side * coarse_halo : (side + 1) * coarse_halo] = coarse_listed[side : side + 1]
        lanes = slice(side * halo, (side + 1) * halo)
        lists[at["fine_high"] : at["fine_high"] + 1, lanes] = jnp.right_shift(listed[side : side + 1], 7)
        lists[at["fine_low"] : at["fine_low"] + 1, lanes] = jnp.bitwise_and(listed[side : side + 1], LANES - 1)
    lists[at["dest"] : at["target"], :] = dest.get()[...]
    lists[at["target"] : at["high"], :] = target.get()[...]
    parents = parent.get()[...]
    lists[at["high"] : at["low"], :] = jnp.right_shift(parents, 7)
    lists[at["low"] : at["coarse"], :] = jnp.bitwise_and(parents, LANES - 1)
    tail = lists[...].astype(F32).astype(BF16)
    nodes = nodes.get()
    for side, out in ((0, lower), (1, higher)):
        col = column(listed[side : side + 1])
        out[:halo, :] = dot(hot_rows(col, fine), nodes[...]).astype(BF16)
        out[halo:, :] = tail


def fine_kernel(halo, from_lower, from_higher, own, nodes, senders, receivers, edges, *rest):
    *weights, payload, new_edges = rest
    nodes = nodes.get()
    fine = nodes.shape[0]
    table = jnp.concatenate([nodes[...], from_lower[:halo, :], from_higher[:halo, :]], axis=0)
    payload[:fine, :] = message_pass(table, fine, senders, receivers, edges, weights, new_edges)
    payload[fine:, :] = own[halo:, :]


def coarse_kernel(regions, halo, coarse, *refs):
    blocks, (_, _, senders, receivers, edges, *rest) = refs[:regions], refs[regions:]
    *weights, payload, new_edges = rest
    me = lax.axis_index("region")
    fine = blocks[0].shape[0] - TAIL
    at = row_layout(fine, coarse)
    tails = [tail_of(block, fine) for block in blocks]
    near = near_tails(tails, me, regions)
    codes = [me * coarse + lax.broadcasted_iota(I32, (coarse, LANES), 0)]
    for side, (other, there, tail) in enumerate(near):
        listed = tail[at["coarse"] : at["coarse"] + 1, :]
        first = halo * (1 - side)
        col = columns(listed)[first : first + halo]
        codes.append(jnp.where(there, other * coarse + col, -1))
    codes = jnp.concatenate(codes, axis=0)
    total = jnp.zeros((codes.shape[0], LANES), F32)
    members = jnp.zeros((codes.shape[0], LANES), F32)
    for block, tail in zip(blocks, tails):
        f = fine // LANES
        parent = tail[at["dest"] : at["dest"] + f] * coarse + tail[at["target"] : at["target"] + f]
        chosen = hot_codes(codes, parent)
        total = total + dot(chosen, block[:fine, :])
        for i in range(f):
            members = members + chosen[:, i * LANES : (i + 1) * LANES].astype(F32)
    members = jnp.sum(members, axis=1, keepdims=True)
    table = (total / jnp.maximum(members, 1.0)).astype(BF16)
    payload[:coarse, :] = message_pass(table, coarse, senders, receivers, edges, weights, new_edges)
    own_tail = tails[0]
    c = coarse // LANES
    payload[coarse:, :] = jnp.concatenate(
        [own_tail[at["high"] : at["high"] + 2 * c], jnp.zeros((TAIL - 2 * c, LANES), I32)], axis=0
    ).astype(F32).astype(BF16)


def compact(first, ranks, codes, edges, size, at_once=8):
    place = lax.broadcasted_iota(I32, (size, LANES), 0) + first

    def body(g, carry):
        latents, found = carry
        rank = ranks[pl.ds(pl.multiple_of(g * at_once, at_once), at_once), :]
        code = codes[pl.ds(pl.multiple_of(g * at_once, at_once), at_once), :]
        hots = []
        for i in range(at_once):
            mask = place == rank[i : i + 1]
            hots.append(hot(mask))
            found = found + jnp.where(mask, code[i : i + 1], 0)
        wide = at_once * LANES
        rows = edges[pl.ds(pl.multiple_of(g * wide, wide), wide), :]
        return latents + dot(jnp.concatenate(hots, axis=1), rows), found

    zero = jnp.zeros((size, LANES), F32), jnp.zeros((size, LANES), I32)
    latents, found = lax.fori_loop(0, ranks.shape[0] // at_once, body, zero)
    found = jnp.sum(found.astype(F32), axis=1, keepdims=True).astype(I32)
    return latents.astype(BF16), jnp.broadcast_to(found, (size, LANES))


def listed_kernel(regions, halo, fine, coarse, wide, *refs):
    own, lower, higher, senders, receivers, parents, halo_codes, ranks, codes, number = refs
    me = lax.axis_index("region")
    at = row_layout(fine, coarse)
    own_tail, lower_tail, higher_tail = (tail_of(ref, ref.shape[0] - TAIL) for ref in (own, lower, higher))
    near = ((me - 1, me > 0, lower_tail), (me + 1, me < regions - 1, higher_tail))
    c = coarse // LANES

    def own_parents(tail):
        return tail[at["high"] : at["high"] + c] * LANES + tail[at["low"] : at["low"] + c]

    cols = [columns(own_parents(own_tail))]
    for side, (other, there, tail) in enumerate(near):
        first = halo * (1 - side)
        col = columns(tail[at["coarse"] : at["coarse"] + 1])[first : first + halo]
        halo_codes[side * halo : (side + 1) * halo, :] = jnp.where(there, other * coarse + col, -1)
        theirs = own_parents(tail).astype(F32)
        value = jnp.zeros((halo, LANES), F32)
        for i in range(c):
            value = value + jnp.where(col == lane_iota(halo, i * LANES), theirs[i : i + 1], 0.0)
        value = jnp.broadcast_to(jnp.sum(value, axis=1, keepdims=True), (halo, LANES)).astype(I32)
        cols.append(jnp.where(there, value, -1))
    cols.append(jnp.full((wide - coarse - 2 * halo, LANES), -1, I32))
    cols = jnp.concatenate(cols, axis=0)
    parents[...] = cols
    receivers = receivers.get()
    count = receivers.shape[0]
    needed = []
    for i in range(count):
        match = jnp.where(cols == receivers[i : i + 1, :], 1.0, 0.0)
        needed.append(jnp.max(match, axis=0, keepdims=True))
    needed = jnp.concatenate(needed, axis=0)
    upto = jnp.where(lax.broadcasted_iota(I32, (LANES, LANES), 0) <= lane_iota(LANES), 1.0, 0.0)
    inside = dot(needed.astype(BF16), upto.astype(BF16))
    sums = jnp.broadcast_to(inside[:, LANES - 1 :], (count, LANES))
    square = (count, count)
    before = lax.broadcasted_iota(I32, square, 1) < lax.broadcasted_iota(I32, square, 0)
    rank = dot(hot(before), sums.astype(BF16)) + inside - 1.0
    ranks[...] = jnp.where(needed > 0.0, rank, -1.0).astype(I32)
    codes[...] = senders.get()[...] * TOP + receivers[...]
    number[0] = jnp.sum(needed).astype(I32)


def compact_kernel(size, ranks, codes, edges, latents, found):
    latents[...], found[...] = compact(0, ranks, codes, edges.get(), size)


def parent_kernel(regions, halo, coarse, *refs):
    blocks, (table, parents) = refs[:regions], refs[regions:]
    me = lax.axis_index("region")
    fine = blocks[0].shape[0] - TAIL
    at = row_layout(fine, coarse)
    tails = [tail_of(block, fine) for block in blocks]
    f = fine // LANES

    def own_parents(tail):
        return tail[at["dest"] : at["dest"] + f] * coarse + tail[at["target"] : at["target"] + f]

    table[:fine, :] = blocks[0][:fine, :]
    parents[:fine, :] = columns(own_parents(tails[0]))
    for side, (other, there, tail) in enumerate(near_tails(tails, me, regions)):
        rows = slice(fine + side * halo, fine + (side + 1) * halo)
        first = halo * (1 - side)
        listed = tail[at["fine_high"] : at["fine_high"] + 1] * LANES + tail[at["fine_low"] : at["fine_low"] + 1]
        col = columns(listed)[first : first + halo]
        theirs = own_parents(tail).astype(F32)
        value = jnp.zeros((halo, LANES), F32)
        for i in range(f):
            value = value + jnp.where(col == lane_iota(halo, i * LANES), theirs[i : i + 1], 0.0)
        value = jnp.broadcast_to(jnp.sum(value, axis=1, keepdims=True), (halo, LANES)).astype(I32)
        parents[rows, :] = jnp.where(there, value, -1)
        total = jnp.zeros((halo, LANES), F32)
        for j, block in enumerate(blocks):
            here = jnp.logical_and(there, jnp.bitwise_xor(me, j) == other)
            total = total + dot(hot_rows(jnp.where(here, col, -1), fine), block[:fine, :])
        table[rows, :] = total.astype(BF16)


def pooled(col, blocks, coarse):
    c = coarse // LANES

    def add(block, sums):
        total, members = sums
        tail = tail_of(block, coarse)
        chosen = hot_codes(col, tail[:c] * LANES + tail[c : 2 * c])
        total = total + dot(chosen, block[:coarse, :])
        for i in range(c):
            members = members + chosen[:, i * LANES : (i + 1) * LANES].astype(F32)
        return total, members

    sums = (jnp.zeros((col.shape[0], LANES), F32),) * 2
    if isinstance(blocks, tuple):
        for block in blocks:
            sums = add(block, sums)
    else:
        sums = lax.fori_loop(0, blocks.shape[0], lambda n, sums: add(blocks.at[n], sums), sums)
    total, members = sums
    members = jnp.sum(members, axis=1, keepdims=True)
    return (total / jnp.maximum(members, 1.0)).astype(BF16)


def as_rows(col):
    return jnp.concatenate(
        [jnp.transpose(col[i : i + LANES])[:1] for i in range(0, col.shape[0], LANES)], axis=0
    )


def top_kernel(regions, halo, coarse, size, count, *refs):
    blocks, refs = refs[:count] if count > 1 else refs[0], refs[count:]
    parents, halo_codes, ranks, codes, latents, found, number, all_edges = refs[:8]
    edges, senders, receivers = Here(refs[8]), *refs[9:11]
    top_weights, weights = refs[11:15], refs[15:19]
    out, agg, fallback, semaphore = refs[19:]
    me = lax.axis_index("region")
    subs = lax.axis_size("sub")
    own_sub = lambda j: blocks[j * subs] if count > 1 else blocks.at[j * subs]
    wide = parents.shape[0]
    mine = parents[...]
    top_own = pooled(mine, blocks, coarse)
    mine_rows = as_rows(mine)
    row_at = lax.broadcasted_iota(I32, (wide, LANES), 0)
    firsts = []
    for i in range(wide // LANES):
        earlier = jnp.logical_and(mine == mine_rows[i : i + 1], row_at < lane_iota(wide, i * LANES))
        seen = jnp.max(jnp.where(earlier, 1.0, 0.0), axis=0, keepdims=True)
        firsts.append(jnp.where(seen > 0.0, -2, mine_rows[i : i + 1]))
    firsts = jnp.concatenate(firsts, axis=0)
    first, second = top_weights[0].get()[...], top_weights[1].get()[...]
    agg[...] = jnp.zeros_like(agg)
    total = number[0]

    def one(at, edge, code):
        place = lax.broadcasted_iota(I32, (size, LANES), 0) + at
        send = jnp.right_shift(code, TOP.bit_length() - 1)
        recv = jnp.where(place < total, jnp.bitwise_and(code, TOP - 1), -3)
        from_send = pooled(send, blocks, coarse)
        from_recv = dot(hot_codes(recv, firsts), top_own).astype(BF16)
        joined = jnp.concatenate([from_send, from_recv, edge], axis=1)
        new = (edge.astype(F32) + perceptron(joined, first, second)).astype(BF16)
        agg[...] += dot(hot_codes(mine, as_rows(recv)), new)

    one(0, latents[...], found[...])

    def more(b, carry):
        copy = pltpu.make_async_copy(all_edges, fallback, semaphore.at[0])
        copy.start()
        copy.wait()
        edge, code = compact(b * size, ranks, codes, fallback, size)
        one(b * size, edge, code)
        return carry

    lax.fori_loop(1, (total + size - 1) // size, more, 0)
    top_final = node_update(top_own, agg[...], top_weights[2].get()[...], top_weights[3].get()[...])
    wanted = halo_codes[...]
    near = jnp.zeros((2 * halo, LANES), F32)
    for j in range(regions):
        col = wanted - jnp.bitwise_xor(me, j) * coarse
        near = near + dot(hot_rows(col, coarse), own_sub(j)[:coarse, :])
    down = jnp.concatenate([own_sub(0)[:coarse, :].astype(F32), near], axis=0)
    table = (down + top_final[: coarse + 2 * halo].astype(F32)).astype(BF16)
    out[...] = message_pass(table, coarse, senders, receivers, edges, weights)


def last_kernel(regions, *refs):
    blocks, refs = refs[:regions], refs[regions:]
    down, parents, edges, senders, receivers, *weights, out = refs
    edges = Here(edges)
    me = lax.axis_index("region")
    own, coarse = out.shape[0], blocks[0].shape[0]
    total = down[...].astype(F32)
    wanted = parents[...]
    for j, block in enumerate(blocks):
        col = wanted - jnp.bitwise_xor(me, j) * coarse
        total = total + dot(hot_rows(col, coarse), block[...])
    out[...] = message_pass(total.astype(BF16), own, senders, receivers, edges, weights)


class Here:
    def __init__(self, place):
        self.place = place

    def get(self):
        return self.place


class Arriving(Here):
    def __init__(self, source, place, semaphore):
        super().__init__(place)
        self.copy, self.waiting = pltpu.make_async_copy(source, place, semaphore), True
        self.copy.start()

    def get(self):
        if self.waiting:
            self.copy.wait()
            self.waiting = False
        return self.place


def call(kernel, args, outs, more=(), scratch=(), raw=(), scalars=(), scalar_outs=(), cost=1, far=False, limit=LIMIT):
    kinds = {i: pltpu.SMEM for i in scalars} | {i: pltpu.HBM for i in raw}
    specs = [pl.BlockSpec(memory_space=kinds.get(i, pltpu.VMEM)) for i in range(len(args))]
    specs += [pl.BlockSpec(memory_space=pltpu.HBM if far else pltpu.VMEM)] * len(more)
    out_specs = [pl.BlockSpec(memory_space=pltpu.SMEM if i in scalar_outs else pltpu.VMEM) for i in range(len(outs))]
    places = []
    if far:
        places = [pltpu.VMEM(array.shape, array.dtype) for array, _ in more]
        places.append(pltpu.SemaphoreType.DMA((len(more),)))
    n, k, o = len(args), len(more), len(outs)

    def body(*refs):
        given, sources, results, rest = refs[:n], refs[n : n + k], refs[n + k : n + k + o], refs[n + k + o :]
        if far:
            near, semaphores, rest = rest[:k], rest[k], rest[k + 1 :]
            operands = [Arriving(source, near[i], semaphores.at[i]) for i, source in enumerate(sources)]
        else:
            operands = [Here(ref if at is None else ref.at[at]) for ref, (_, at) in zip(sources, more)]
        kernel(*given, *operands, *results, *rest)

    return pl.pallas_call(
        body,
        out_shape=[jax.ShapeDtypeStruct(shape, dtype) for shape, dtype in outs],
        in_specs=specs,
        out_specs=out_specs,
        scratch_shapes=places + list(scratch),
        compiler_params=pltpu.CompilerParams(vmem_limit_bytes=limit),
        cost_estimate=pl.CostEstimate(flops=cost * 10**9, bytes_accessed=cost * 10**5, transcendentals=0),
    )(*args, *[array for array, _ in more])


def over_region(rows):
    count = lax.axis_size("region")
    blocks = {0: rows}
    bit = count // 2
    while bit:
        for j in list(blocks):
            blocks[j + bit] = lax.ppermute(blocks[j], "region", [(i, i ^ bit) for i in range(count)])
        bit //= 2
    return [blocks[j] for j in range(count)]


def over_both(rows):
    regions, subs = lax.axis_size("region"), lax.axis_size("sub")
    turns = [rows] + [
        lax.ppermute(rows, "sub", [(i, (i + k) % subs) for i in range(subs)]) for k in range(1, subs)
    ]
    if regions * subs <= 16:
        spread = [over_region(turn) for turn in turns]
        return [spread[k][j] for j in range(regions) for k in range(subs)]
    blocks, bit = jnp.stack(turns), 1
    while bit < regions:
        there = lax.ppermute(blocks, "region", [(i, i ^ bit) for i in range(regions)])
        blocks, bit = jnp.concatenate([blocks, there]), 2 * bit
    return [blocks]


def on_device(
    node_feats,
    fine_senders,
    fine_receivers,
    fine_edges,
    halo_rows,
    coarse_senders,
    coarse_receivers,
    coarse_edges,
    coarse_halo_rows,
    pool_dest,
    pool_target,
    pool3_target,
    top_senders,
    top_receivers,
    top_edges,
    edge_in,
    edge_out,
    node_in,
    node_out,
):
    weights = (edge_in, edge_out, node_in, node_out)
    regions = lax.axis_size("region")
    fine, coarse = node_feats.shape[0], pool3_target.shape[0]
    halo, halo2 = halo_rows.shape[1], coarse_halo_rows.shape[1]
    rows = lambda a: a.reshape(-1, LANES)
    fine_send, fine_recv = rows(fine_senders), rows(fine_receivers)
    coarse_send, coarse_recv = rows(coarse_senders), rows(coarse_receivers)
    top_send, top_recv = rows(top_senders), rows(top_receivers)

    level = lambda index: [(matrix, index) for matrix in weights]
    plain = lambda *arrays: [(array, None) for array in arrays]

    to_lower, to_higher = call(
        functools.partial(pick_kernel, halo, halo2, fine, coarse),
        [],
        [((halo + TAIL, LANES), BF16)] * 2,
        plain(node_feats, halo_rows, coarse_halo_rows, rows(pool_dest), rows(pool_target), rows(pool3_target)),
        scratch=[pltpu.VMEM((TAIL, LANES), I32)],
        far=True,
        limit=60 * 1024 * 1024,
    )
    up = [(i, i + 1) for i in range(regions - 1)]
    from_lower = lax.ppermute(to_higher, "region", up)
    from_higher = lax.ppermute(to_lower, "region", [(j, i) for i, j in up])
    payload, fine_edges2 = call(
        functools.partial(fine_kernel, halo),
        [from_lower, from_higher, to_lower],
        [((fine + TAIL, LANES), BF16), (fine_edges.shape, BF16)],
        plain(node_feats, fine_send, fine_recv, fine_edges) + level(0),
        cost=5,
    )
    blocks = over_region(payload)
    wide = -(-(coarse + 2 * halo2) // LANES) * LANES
    size = min(384, top_edges.shape[0])
    parents, halo_codes, ranks, codes, number = call(
        functools.partial(listed_kernel, regions, halo2, fine, coarse, wide),
        [to_lower, from_lower, from_higher],
        [
            ((wide, LANES), I32),
            ((2 * halo2, LANES), I32),
            (top_send.shape, I32),
            (top_send.shape, I32),
            ((1,), I32),
        ],
        plain(top_send, top_recv),
        scalar_outs=(4,),
        cost=3,
    )
    latents, found = call(
        functools.partial(compact_kernel, size),
        [ranks, codes],
        [((size, LANES), BF16), ((size, LANES), I32)],
        plain(top_edges),
        cost=3,
    )
    payload2, coarse_edges2 = call(
        functools.partial(coarse_kernel, regions, halo2, coarse),
        blocks + [number, found],
        [((coarse + TAIL, LANES), BF16), (coarse_edges.shape, BF16)],
        plain(coarse_send, coarse_recv, coarse_edges) + level(1),
        scalars=(regions,),
        cost=4,
    )
    fine_table, fine_parents = call(
        functools.partial(parent_kernel, regions, halo, coarse),
        blocks,
        [((fine + 2 * halo, LANES), BF16), ((fine + 2 * halo, LANES), I32)],
    )
    blocks2 = over_both(payload2)
    many = len(blocks2)
    (coarse_final,) = call(
        functools.partial(top_kernel, regions, halo2, coarse, size, many),
        blocks2 + [parents, halo_codes, ranks, codes, latents, found, number, top_edges, coarse_edges2],
        [((coarse, LANES), BF16)],
        plain(coarse_send, coarse_recv) + level(2) + level(3),
        scratch=[
            pltpu.VMEM((wide, LANES), F32),
            pltpu.VMEM(top_edges.shape, BF16),
            pltpu.SemaphoreType.DMA((1,)),
        ],
        scalars=(many + 6,),
        raw=(many + 7,),
        cost=6,
    )
    (fine_final,) = call(
        functools.partial(last_kernel, regions),
        over_region(coarse_final) + [fine_table, fine_parents, fine_edges2],
        [((fine, LANES), BF16)],
        plain(fine_send, fine_recv) + level(4),
        cost=6,
    )
    return fine_final


def solution(mesh):
    spread = ("parts", "region", "sub")
    rows, flat = P(spread, None), P(spread)
    in_specs = (
        (rows, flat, flat, rows, rows, flat, flat, rows, rows, rows, flat, flat)
        + (P("parts"), P("parts"), P("parts", None))
        + (P(),) * 4
    )
    return jax.shard_map(on_device, mesh=mesh, in_specs=in_specs, out_specs=rows, check_vma=False)
```

```python
import functools

import jax
import jax.numpy as jnp
from jax import lax
from jax.experimental import pallas as pl
from jax.experimental.pallas import tpu as pltpu
from jax.sharding import PartitionSpec as P

EPSILON = 1e-05
TOP = 2048
LANES = 128
F32, BF16, I32 = jnp.float32, jnp.bfloat16, jnp.int32
GROUP, SLOTS = 8, 64
CUT_BITS = 8
CUT = 1 << CUT_BITS
TAIL = 16
LIMIT = 32 * 1024 * 1024


def dot(a, b):
    return jnp.dot(a, b, preferred_element_type=F32)


def lane_iota(rows, first=0):
    return lax.broadcasted_iota(I32, (rows, LANES), 1) + first


def column(row):
    return jnp.transpose(jnp.broadcast_to(row, (LANES, row.shape[1])))


def columns(rows):
    return jnp.concatenate([column(rows[i : i + 1]) for i in range(rows.shape[0])], axis=0)


def hot(mask):
    return jnp.where(mask, 1.0, 0.0).astype(BF16)


def hot_rows(col, count):
    return jnp.concatenate(
        [hot(col == lane_iota(col.shape[0], first)) for first in range(0, count, LANES)], axis=1
    )


def hot_cols(rows, count):
    place = lax.broadcasted_iota(I32, (count, LANES), 0)
    return jnp.concatenate([hot(place == rows[i : i + 1]) for i in range(rows.shape[0])], axis=1)


def gather(row, block, blocks):
    wide = dot(hot_rows(row, blocks[0].shape[0]), jnp.concatenate(blocks, axis=1))
    out = jnp.zeros((row.shape[0], LANES), F32)
    for i in range(len(blocks)):
        out = jnp.where(block == i, wide[:, i * LANES : (i + 1) * LANES], out)
    return out


def cut(table):
    short = -table.shape[0] % CUT
    if short:
        table = jnp.concatenate([table, jnp.zeros((short, LANES), BF16)], axis=0)
    return [table[i : i + CUT] for i in range(0, table.shape[0], CUT)]


def gather_cut(col, blocks):
    return gather(jnp.bitwise_and(col, CUT - 1), jnp.right_shift(col, CUT_BITS), blocks).astype(BF16)


def segment_sum(rows, col, values, count):
    block = jnp.right_shift(col, CUT_BITS)
    wide = [values]
    if count > CUT:
        wide = [jnp.where(block == i, values.astype(F32), 0.0).astype(BF16) for i in range(count // CUT)]
    out = dot(hot_cols(jnp.bitwise_and(rows, CUT - 1), CUT), jnp.concatenate(wide, axis=1))
    return jnp.concatenate([out[:, i * LANES : (i + 1) * LANES] for i in range(len(wide))], axis=0)


def hot_codes(col, rows):
    return jnp.concatenate([hot(col == rows[i : i + 1]) for i in range(rows.shape[0])], axis=1)


def normalize(values):
    centred = values - jnp.mean(values, axis=-1, keepdims=True)
    variance = jnp.mean(centred * centred, axis=-1, keepdims=True)
    return centred * lax.rsqrt(variance + EPSILON)


def perceptron(features, first, second):
    hidden = jnp.maximum(dot(features, first), 0.0).astype(BF16)
    return normalize(dot(hidden, second))


def node_update(nodes, summed, first, second):
    joined = jnp.concatenate([nodes, summed.astype(BF16)], axis=1)
    return (nodes.astype(F32) + perceptron(joined, first, second)).astype(BF16)


def message_pass(table, own, senders, receivers, edges, weights, new_edges=None, step=1536):
    nodes = table[:own]
    all_blocks, own_blocks = cut(table), cut(nodes)
    senders, receivers, edges = senders.get(), receivers.get(), edges.get()
    count = edges.shape[0]
    step = min(step, count)
    first, second = weights[0].get()[...], weights[1].get()[...]
    summed = jnp.zeros((own, LANES), F32)
    for at in range(0, count, step):
        rows = slice(at // LANES, (at + step) // LANES)
        recv = receivers[rows, :]
        send_col, recv_col = columns(senders[rows, :]), columns(recv)
        from_send = gather_cut(send_col, all_blocks)
        from_recv = gather_cut(recv_col, own_blocks)
        edge = edges[at : at + step, :]
        joined = jnp.concatenate([from_send, from_recv, edge], axis=1)
        new = (edge.astype(F32) + perceptron(joined, first, second)).astype(BF16)
        if new_edges is not None:
            new_edges[at : at + step, :] = new
        summed = summed + segment_sum(recv, recv_col, new, own)
    return node_update(nodes, summed, weights[2].get()[...], weights[3].get()[...])


def tail_of(block, count):
    return block[count : count + TAIL, :].astype(F32).astype(I32)


def row_layout(fine, coarse):
    f, c = fine // LANES, coarse // LANES
    return {"dest": 0, "target": f, "high": 2 * f, "low": 2 * f + c, "coarse": 2 * f + 2 * c, "fine_high": 2 * f + 2 * c + 1, "fine_low": 2 * f + 2 * c + 2}


def near_tails(tails, me, count):
    out = []
    for other in (me - 1, me + 1):
        there = jnp.logical_and(other >= 0, other < count)
        near = jnp.where(there, jnp.bitwise_xor(me, other), 0)
        picked = sum(jnp.where(near == j, tail, 0) for j, tail in enumerate(tails))
        out.append((other, there, picked))
    return out


def pick_kernel(halo, coarse_halo, fine, coarse, nodes, rows, coarse_rows, dest, target, parent, paired, crossed, lists):
    at = row_layout(fine, coarse)
    lists[...] = jnp.zeros_like(lists)
    listed, coarse_listed = rows.get()[...], coarse_rows.get()[...]
    for side in (0, 1):
        lists[at["coarse"] : at["coarse"] + 1, side * coarse_halo : (side + 1) * coarse_halo] = coarse_listed[side : side + 1]
        lanes = slice(side * halo, (side + 1) * halo)
        lists[at["fine_high"] : at["fine_high"] + 1, lanes] = jnp.right_shift(listed[side : side + 1], 7)
        lists[at["fine_low"] : at["fine_low"] + 1, lanes] = jnp.bitwise_and(listed[side : side + 1], LANES - 1)
    lists[at["dest"] : at["target"], :] = dest.get()[...]
    lists[at["target"] : at["high"], :] = target.get()[...]
    parents = parent.get()[...]
    lists[at["high"] : at["low"], :] = jnp.right_shift(parents, 7)
    lists[at["low"] : at["coarse"], :] = jnp.bitwise_and(parents, LANES - 1)
    tail = lists[...].astype(F32).astype(BF16)
    nodes = nodes.get()
    odd = jnp.bitwise_and(lax.axis_index("region"), 1)
    for out, up in ((paired, 1 - odd), (crossed, odd)):
        col = column(jnp.where(up == 1, listed[1:2], listed[0:1]))
        out[:halo, :] = dot(hot_rows(col, fine), nodes[...]).astype(BF16)
        out[halo:, :] = tail


def lower_higher(paired, crossed):
    odd = jnp.bitwise_and(lax.axis_index("region"), 1) == 1
    paired, crossed = paired.astype(F32), crossed.astype(F32)
    return jnp.where(odd, paired, crossed).astype(BF16), jnp.where(odd, crossed, paired).astype(BF16)


def fine_kernel(halo, paired, crossed, own, nodes, senders, receivers, edges, *rest):
    *weights, payload, new_edges = rest
    nodes = nodes.get()
    fine = nodes.shape[0]
    table = jnp.concatenate([nodes[...], *lower_higher(paired[:halo, :], crossed[:halo, :])], axis=0)
    payload[:fine, :] = message_pass(table, fine, senders, receivers, edges, weights, new_edges)
    payload[fine:, :] = own[halo:, :]


def coarse_kernel(regions, halo, coarse, *refs):
    blocks, (senders, receivers, edges, *rest) = refs[:regions], refs[regions:]
    *weights, payload, new_edges = rest
    me = lax.axis_index("region")
    fine = blocks[0].shape[0] - TAIL
    at = row_layout(fine, coarse)
    tails = [tail_of(block, fine) for block in blocks]
    near = near_tails(tails, me, regions)
    codes = [me * coarse + lax.broadcasted_iota(I32, (coarse, LANES), 0)]
    for side, (other, there, tail) in enumerate(near):
        listed = tail[at["coarse"] : at["coarse"] + 1, :]
        first = halo * (1 - side)
        col = columns(listed)[first : first + halo]
        codes.append(jnp.where(there, other * coarse + col, -1))
    codes = jnp.concatenate(codes, axis=0)
    total = jnp.zeros((codes.shape[0], LANES), F32)
    members = jnp.zeros((codes.shape[0], LANES), F32)
    for block, tail in zip(blocks, tails):
        f = fine // LANES
        parent = tail[at["dest"] : at["dest"] + f] * coarse + tail[at["target"] : at["target"] + f]
        more, counted = sums_and_counts(hot_codes(codes, parent), block[:fine, :])
        total, members = total + more, members + counted
    table = (total / jnp.maximum(members, 1.0)).astype(BF16)
    payload[:coarse, :] = message_pass(table, coarse, senders, receivers, edges, weights, new_edges)
    own_tail = tails[0]
    c = coarse // LANES
    payload[coarse:, :] = jnp.concatenate(
        [own_tail[at["high"] : at["high"] + 2 * c], jnp.zeros((TAIL - 2 * c, LANES), I32)], axis=0
    ).astype(F32).astype(BF16)


def compact(first, ranks, codes, edges, size, at_once=8):
    place = lax.broadcasted_iota(I32, (size, LANES), 0) + first

    def body(g, carry):
        latents, found = carry
        rank = ranks[pl.ds(pl.multiple_of(g * at_once, at_once), at_once), :]
        code = codes[pl.ds(pl.multiple_of(g * at_once, at_once), at_once), :]
        hots = []
        for i in range(at_once):
            mask = place == rank[i : i + 1]
            hots.append(hot(mask))
            found = found + jnp.where(mask, code[i : i + 1], 0)
        wide = at_once * LANES
        rows = edges[pl.ds(pl.multiple_of(g * wide, wide), wide), :]
        return latents + dot(jnp.concatenate(hots, axis=1), rows), found

    zero = jnp.zeros((size, LANES), F32), jnp.zeros((size, LANES), I32)
    latents, found = lax.fori_loop(0, ranks.shape[0] // at_once, body, zero)
    found = jnp.sum(found.astype(F32), axis=1, keepdims=True).astype(I32)
    return latents.astype(BF16), jnp.broadcast_to(found, (size, LANES))


def below(rows, same):
    square = (rows, rows)
    return hot(same(lax.broadcasted_iota(I32, square, 0), lax.broadcasted_iota(I32, square, 1)))


def running(flags):
    upto = hot(lax.broadcasted_iota(I32, (LANES, LANES), 0) <= lane_iota(LANES))
    inside = dot(flags.astype(BF16), upto)
    return inside, jnp.broadcast_to(inside[:, LANES - 1 :], flags.shape)


def listed_kernel(regions, halo, fine, coarse, *refs):
    own, paired, crossed, senders, receivers, edges, parents, halo_rows, halo_blocks, ranks, codes, latents, found, number = refs
    me = lax.axis_index("region")
    at = row_layout(fine, coarse)
    start = own.shape[0] - TAIL
    lower, higher = lower_higher(paired[start:, :], crossed[start:, :])
    own_tail, lower_tail, higher_tail = (tail.astype(F32).astype(I32) for tail in (own[start:, :], lower, higher))
    near = ((me - 1, me > 0, lower_tail), (me + 1, me < regions - 1, higher_tail))
    c = coarse // LANES
    wide, size = parents.shape[0], latents.shape[0]

    def own_parents(tail):
        return tail[at["high"] : at["high"] + c] * LANES + tail[at["low"] : at["low"] + c]

    cols = [columns(own_parents(own_tail))]
    for side, (other, there, tail) in enumerate(near):
        first = halo * (1 - side)
        col = columns(tail[at["coarse"] : at["coarse"] + 1])[first : first + halo]
        halo_rows[side * halo : (side + 1) * halo, :] = col
        halo_blocks[side * halo : (side + 1) * halo, :] = jnp.full(col.shape, jnp.where(there, jnp.bitwise_xor(me, other), -1))
        theirs = own_parents(tail).astype(F32)
        value = jnp.zeros((halo, LANES), F32)
        for i in range(c):
            value = value + jnp.where(col == lane_iota(halo, i * LANES), theirs[i : i + 1], 0.0)
        value = jnp.broadcast_to(jnp.sum(value, axis=1, keepdims=True), (halo, LANES)).astype(I32)
        cols.append(jnp.where(there, value, -1))
    cols.append(jnp.full((wide - coarse - 2 * halo, LANES), -1, I32))
    cols = jnp.concatenate(cols, axis=0)
    parents[...] = cols

    high_count = TOP // LANES
    rows = as_rows(cols)
    tops = dot(
        hot_cols(jnp.right_shift(rows, 7), high_count), hot_rows(jnp.bitwise_and(cols, LANES - 1), LANES)
    )
    tops = jnp.minimum(tops, 1.0).astype(BF16)
    receivers = receivers.get()
    count = receivers.shape[0]
    high = lax.broadcasted_iota(I32, (high_count, LANES), 0)
    needed = []
    for i in range(0, count, 8):
        recv = receivers[i : i + 8, :]
        match = dot(tops, hot_cols(jnp.bitwise_and(recv, LANES - 1), LANES))
        for k in range(8):
            mine = jnp.where(high == jnp.right_shift(recv[k : k + 1], 7), match[:, k * LANES : (k + 1) * LANES], 0.0)
            needed.append(jnp.sum(mine, axis=0, keepdims=True))
    needed = jnp.concatenate(needed, axis=0)

    group_of = lambda i: jnp.right_shift(i, GROUP.bit_length() - 1)
    inside, sums = running(needed)
    sums = sums.astype(BF16)
    local = dot(below(count, lambda i, j: jnp.logical_and(j < i, group_of(i) == group_of(j))), sums) + inside - 1.0
    in_group = dot(below(count, lambda i, j: group_of(i) == group_of(j)), sums)
    used = jnp.minimum(in_group, float(SLOTS))
    before = dot(below(count, lambda i, j: group_of(j) < group_of(i)), (used / GROUP).astype(BF16))
    placed = jnp.logical_and(local < SLOTS, local + before < size)
    others = jnp.where(placed, 0.0, needed)
    inside, sums = running(others)
    rank = dot(below(count, lambda i, j: j < i), sums.astype(BF16)) + inside - 1.0
    ranks[...] = jnp.where(others > 0.0, rank, -1.0).astype(I32)
    number[1] = jnp.sum(others).astype(I32)
    number[0] = jnp.sum(needed).astype(I32) - number[1]
    codes[...] = senders.get()[...] * TOP + receivers[...]

    slot = jnp.where(needed > 0.0, local, -1.0).astype(I32)
    place = lax.broadcasted_iota(I32, (SLOTS, LANES), 0)
    edges = edges.get()
    lane = lane_iota(SLOTS)
    slots, targets = [], []
    for first in range(0, count, GROUP):
        hots, code = [], jnp.zeros((SLOTS, LANES), F32)
        for i in range(first, first + GROUP):
            mask = place == slot[i : i + 1]
            hots.append(hot(mask))
            code = code + jnp.where(mask, codes[i : i + 1, :].astype(F32), 0.0)
        code = jnp.broadcast_to(jnp.sum(code, axis=1, keepdims=True), (SLOTS, LANES)).astype(I32)
        parts = jnp.where(
            lane == 0,
            jnp.right_shift(code, 16),
            jnp.where(lane == 1, jnp.bitwise_and(jnp.right_shift(code, 8), 255), jnp.bitwise_and(code, 255)),
        )
        parts = jnp.where(lane < 3, parts, 0).astype(F32).astype(BF16)
        packed = dot(jnp.concatenate(hots, axis=1), edges[first * LANES : (first + GROUP) * LANES, :]).astype(BF16)
        slots.append(jnp.concatenate([packed, parts], axis=1))
        target = before[first : first + 1] + lane_iota(1).astype(F32)
        targets.append(jnp.where(lane_iota(1).astype(F32) < used[first : first + 1], target, -1.0).astype(I32)[:, :SLOTS])
    per = LANES // SLOTS
    targets = [jnp.concatenate(targets[i : i + per], axis=1) for i in range(0, len(targets), per)]
    packed = dot(hot_cols(jnp.concatenate(targets, axis=0), size), jnp.concatenate(slots, axis=0))
    latents[...] = packed[:, :LANES].astype(BF16)
    parts = packed[:, LANES:]
    lane = lane_iota(size)
    code = jnp.where(lane == 0, parts * 65536.0, jnp.where(lane == 1, parts * 256.0, parts))
    found[...] = jnp.broadcast_to(jnp.sum(code, axis=1, keepdims=True), (size, LANES)).astype(I32)


def parent_kernel(regions, halo, coarse, *refs):
    blocks, (table, parent_rows, parent_blocks) = refs[:regions], refs[regions:]
    me = lax.axis_index("region")
    fine = blocks[0].shape[0] - TAIL
    at = row_layout(fine, coarse)
    tails = [tail_of(block, fine) for block in blocks]
    f = fine // LANES

    def own_parents(tail):
        return tail[at["dest"] : at["dest"] + f] * coarse + tail[at["target"] : at["target"] + f]

    table[:fine, :] = blocks[0][:fine, :]
    owner = lambda tail: tail[at["dest"] : at["dest"] + f]
    parent_rows[:fine, :] = columns(tails[0][at["target"] : at["target"] + f])
    parent_blocks[:fine, :] = jnp.bitwise_xor(columns(owner(tails[0])), me)
    for side, (other, there, tail) in enumerate(near_tails(tails, me, regions)):
        rows = slice(fine + side * halo, fine + (side + 1) * halo)
        first = halo * (1 - side)
        listed = tail[at["fine_high"] : at["fine_high"] + 1] * LANES + tail[at["fine_low"] : at["fine_low"] + 1]
        col = columns(listed)[first : first + halo]
        theirs = own_parents(tail).astype(F32)
        value = jnp.zeros((halo, LANES), F32)
        for i in range(f):
            value = value + jnp.where(col == lane_iota(halo, i * LANES), theirs[i : i + 1], 0.0)
        value = jnp.broadcast_to(jnp.sum(value, axis=1, keepdims=True), (halo, LANES)).astype(I32)
        parent_rows[rows, :] = jnp.bitwise_and(value, coarse - 1)
        block = jnp.bitwise_xor(jnp.right_shift(value, coarse.bit_length() - 1), me)
        parent_blocks[rows, :] = jnp.where(there, block, -1)
        total = jnp.zeros((halo, LANES), F32)
        for j, block in enumerate(blocks):
            here = jnp.logical_and(there, jnp.bitwise_xor(me, j) == other)
            total = total + dot(hot_rows(jnp.where(here, col, -1), fine), block[:fine, :])
        table[rows, :] = total.astype(BF16)


def sums_and_counts(chosen, rows):
    both = dot(chosen, jnp.concatenate([rows, jnp.ones(rows.shape, BF16)], axis=1))
    return both[:, :LANES], both[:, LANES:]


def pooled(col, blocks, coarse):
    c = coarse // LANES

    def add(block, sums):
        tail = tail_of(block, coarse)
        total, members = sums_and_counts(hot_codes(col, tail[:c] * LANES + tail[c : 2 * c]), block[:coarse, :])
        return sums[0] + total, sums[1] + members

    sums = (jnp.zeros((col.shape[0], LANES), F32),) * 2
    if isinstance(blocks, tuple):
        for block in blocks:
            sums = add(block, sums)
    else:
        sums = lax.fori_loop(0, blocks.shape[0], lambda n, sums: add(blocks.at[n], sums), sums)
    total, members = sums
    return (total / jnp.maximum(members, 1.0)).astype(BF16)


def as_rows(col):
    return jnp.concatenate(
        [jnp.transpose(col[i : i + LANES])[:1] for i in range(0, col.shape[0], LANES)], axis=0
    )


def top_kernel(regions, halo, coarse, size, count, *refs):
    subs = lax.axis_size("sub")
    if count > 1:
        rows = coarse + TAIL
        there = [refs[count - 1].at[i * rows : (i + 1) * rows] for i in range(count - 1)]
        blocks = tuple((there if j % 2 else refs)[j // 2 * subs + k] for j in range(regions) for k in range(subs))
    else:
        blocks = refs[0]
    refs = refs[count:]
    parents, halo_rows, halo_blocks, ranks, codes, latents, found, number, all_edges, edges = refs[:10]
    senders, receivers = refs[10:12]
    top_weights, weights = refs[12:16], refs[16:20]
    out, agg, fallback, semaphore = refs[20:]
    me = lax.axis_index("region")
    own_sub = lambda j: blocks[j * subs] if count > 1 else blocks.at[j * subs]
    wide = parents.shape[0]
    mine = parents[...]
    top_own = pooled(mine, blocks, coarse)
    mine_rows = as_rows(mine)
    row_at = lax.broadcasted_iota(I32, (wide, LANES), 0)
    firsts = []
    for i in range(wide // LANES):
        earlier = jnp.logical_and(mine == mine_rows[i : i + 1], row_at < lane_iota(wide, i * LANES))
        seen = jnp.max(jnp.where(earlier, 1.0, 0.0), axis=0, keepdims=True)
        firsts.append(jnp.where(seen > 0.0, -2, mine_rows[i : i + 1]))
    firsts = jnp.concatenate(firsts, axis=0)
    first, second = top_weights[0].get()[...], top_weights[1].get()[...]
    agg[...] = jnp.zeros_like(agg)

    def one(edge, code, first_place, total):
        place = lax.broadcasted_iota(I32, (size, LANES), 0) + first_place
        send = jnp.right_shift(code, TOP.bit_length() - 1)
        recv = jnp.where(place < total, jnp.bitwise_and(code, TOP - 1), -3)
        from_send = pooled(send, blocks, coarse)
        from_recv = dot(hot_codes(recv, firsts), top_own).astype(BF16)
        joined = jnp.concatenate([from_send, from_recv, edge], axis=1)
        new = (edge.astype(F32) + perceptron(joined, first, second)).astype(BF16)
        agg[...] += dot(hot_codes(mine, as_rows(recv)), new)

    one(latents[...], found[...], 0, number[0])

    def more(b, carry):
        copy = pltpu.make_async_copy(all_edges, fallback, semaphore.at[0])
        copy.start()
        copy.wait()
        edge, code = compact(b * size, ranks, codes, fallback, size)
        one(edge, code, b * size, number[1])
        return carry

    lax.fori_loop(0, (number[1] + size - 1) // size, more, 0)
    top_final = node_update(top_own, agg[...], top_weights[2].get()[...], top_weights[3].get()[...])
    near = gather(halo_rows[...], halo_blocks[...], [own_sub(j)[:coarse, :] for j in range(regions)])
    down = jnp.concatenate([own_sub(0)[:coarse, :].astype(F32), near], axis=0)
    table = (down + top_final[: coarse + 2 * halo].astype(F32)).astype(BF16)
    out[...] = message_pass(table, coarse, senders, receivers, Here(edges), weights)


def last_kernel(regions, *refs):
    blocks, refs = refs[:regions], refs[regions:]
    down, parent_rows, parent_blocks, edges, senders, receivers, *weights, out = refs
    parent = gather(parent_rows[...], parent_blocks[...], [block[...] for block in blocks])
    table = (down[...].astype(F32) + parent).astype(BF16)
    out[...] = message_pass(table, out.shape[0], senders, receivers, Here(edges), weights)


class Here:
    def __init__(self, place):
        self.place = place

    def get(self):
        return self.place


class Arriving(Here):
    def __init__(self, source, place, semaphore):
        super().__init__(place)
        self.copy, self.waiting = pltpu.make_async_copy(source, place, semaphore), True
        self.copy.start()

    def get(self):
        if self.waiting:
            self.copy.wait()
            self.waiting = False
        return self.place


def call(kernel, args, outs, more=(), scratch=(), raw=(), scalars=(), scalar_outs=(), cost=1, far=False, limit=LIMIT):
    kinds = {i: pltpu.SMEM for i in scalars} | {i: pltpu.HBM for i in raw}
    specs = [pl.BlockSpec(memory_space=kinds.get(i, pltpu.VMEM)) for i in range(len(args))]
    specs += [pl.BlockSpec(memory_space=pltpu.HBM if far else pltpu.VMEM)] * len(more)
    out_specs = [pl.BlockSpec(memory_space=pltpu.SMEM if i in scalar_outs else pltpu.VMEM) for i in range(len(outs))]
    places = []
    if far:
        places = [pltpu.VMEM(array.shape, array.dtype) for array, _ in more]
        places.append(pltpu.SemaphoreType.DMA((len(more),)))
    n, k, o = len(args), len(more), len(outs)

    def body(*refs):
        given, sources, results, rest = refs[:n], refs[n : n + k], refs[n + k : n + k + o], refs[n + k + o :]
        if far:
            near, semaphores, rest = rest[:k], rest[k], rest[k + 1 :]
            operands = [Arriving(source, near[i], semaphores.at[i]) for i, source in enumerate(sources)]
        else:
            operands = [Here(ref if at is None else ref.at[at]) for ref, (_, at) in zip(sources, more)]
        kernel(*given, *operands, *results, *rest)

    return pl.pallas_call(
        body,
        out_shape=[jax.ShapeDtypeStruct(shape, dtype) for shape, dtype in outs],
        in_specs=specs,
        out_specs=out_specs,
        scratch_shapes=places + list(scratch),
        compiler_params=pltpu.CompilerParams(vmem_limit_bytes=limit),
        cost_estimate=pl.CostEstimate(flops=cost * 10**9, bytes_accessed=cost * 10**5, transcendentals=0),
    )(*args, *[array for array, _ in more])


def over_region(rows, beside=None):
    count = lax.axis_size("region")
    blocks = {0: rows}
    bit = count // 2
    while bit:
        going = dict(blocks)
        if beside is not None and len(going) > 1:
            far = max(going)
            going[far], beside = lax.optimization_barrier((going[far], beside))
        for j in blocks:
            going[j + bit] = lax.ppermute(going[j], "region", [(i, i ^ bit) for i in range(count)])
        blocks = going
        bit //= 2
    blocks = [blocks[j] for j in range(count)]
    return blocks if beside is None else (blocks, beside)


def over_both(rows):
    regions, subs = lax.axis_size("region"), lax.axis_size("sub")
    swap = lambda array, axis, bits: lax.ppermute(array, axis, [(i, i ^ bits) for i in range(lax.axis_size(axis))])
    turns = [rows] + [swap(rows, "sub", k) for k in range(1, subs)]
    if regions * subs <= 16:
        blocks = {0: turns}
        bit = regions // 2
        while bit > 1:
            for j in list(blocks):
                blocks[j + bit] = [swap(block, "region", bit) for block in blocks[j]]
            bit //= 2
        here = [block for j in range(0, regions, 2) for block in blocks[j]]
        return here + [swap(jnp.concatenate(here), "region", 1)]
    blocks, bit = jnp.stack(turns), 1
    while bit < regions:
        blocks, bit = jnp.concatenate([blocks, swap(blocks, "region", bit)]), 2 * bit
    return [blocks]


def on_device(
    node_feats,
    fine_senders,
    fine_receivers,
    fine_edges,
    halo_rows,
    coarse_senders,
    coarse_receivers,
    coarse_edges,
    coarse_halo_rows,
    pool_dest,
    pool_target,
    pool3_target,
    top_senders,
    top_receivers,
    top_edges,
    edge_in,
    edge_out,
    node_in,
    node_out,
):
    weights = (edge_in, edge_out, node_in, node_out)
    regions = lax.axis_size("region")
    fine, coarse = node_feats.shape[0], pool3_target.shape[0]
    halo, halo2 = halo_rows.shape[1], coarse_halo_rows.shape[1]
    rows = lambda a: a.reshape(-1, LANES)
    fine_send, fine_recv = rows(fine_senders), rows(fine_receivers)
    coarse_send, coarse_recv = rows(coarse_senders), rows(coarse_receivers)
    top_send, top_recv = rows(top_senders), rows(top_receivers)

    level = lambda index: [(matrix, index) for matrix in weights]
    plain = lambda *arrays: [(array, None) for array in arrays]

    to_pair, to_other = call(
        functools.partial(pick_kernel, halo, halo2, fine, coarse),
        [],
        [((halo + TAIL, LANES), BF16)] * 2,
        plain(node_feats, halo_rows, coarse_halo_rows, rows(pool_dest), rows(pool_target), rows(pool3_target)),
        scratch=[pltpu.VMEM((TAIL, LANES), I32)],
        far=True,
        limit=60 * 1024 * 1024,
    )
    pairs = lambda first: [(i, j) for low in range(first, regions - 1, 2) for i, j in ((low, low + 1), (low + 1, low))]
    paired = lax.ppermute(to_pair, "region", pairs(0))
    crossed = lax.ppermute(to_other, "region", pairs(1))
    payload, fine_edges2 = call(
        functools.partial(fine_kernel, halo),
        [paired, crossed, to_pair],
        [((fine + TAIL, LANES), BF16), (fine_edges.shape, BF16)],
        plain(node_feats, fine_send, fine_recv, fine_edges) + level(0),
        cost=5,
    )
    wide = -(-(coarse + 2 * halo2) // LANES) * LANES
    size = min(384, top_edges.shape[0])
    selected = call(
        functools.partial(listed_kernel, regions, halo2, fine, coarse),
        [to_pair, paired, crossed],
        [
            ((wide, LANES), I32),
            ((2 * halo2, LANES), I32),
            ((2 * halo2, LANES), I32),
            (top_send.shape, I32),
            (top_send.shape, I32),
            ((size, LANES), BF16),
            ((size, LANES), I32),
            ((2,), I32),
        ],
        plain(top_send, top_recv, top_edges),
        scalar_outs=(7,),
        cost=3,
    )
    blocks, selected = over_region(payload, selected)
    payload2, coarse_edges2 = call(
        functools.partial(coarse_kernel, regions, halo2, coarse),
        blocks,
        [((coarse + TAIL, LANES), BF16), (coarse_edges.shape, BF16)],
        plain(coarse_send, coarse_recv, coarse_edges) + level(1),
        cost=4,
    )
    table_shape = (fine + 2 * halo, LANES)
    fine_table, parent_rows, parent_blocks = call(
        functools.partial(parent_kernel, regions, halo, coarse),
        blocks,
        [(table_shape, BF16), (table_shape, I32), (table_shape, I32)],
    )
    blocks2 = over_both(payload2)
    many = len(blocks2)
    (coarse_final,) = call(
        functools.partial(top_kernel, regions, halo2, coarse, size, many),
        blocks2 + [*selected, top_edges, coarse_edges2],
        [((coarse, LANES), BF16)],
        plain(coarse_send, coarse_recv) + level(2) + level(3),
        scratch=[
            pltpu.VMEM((wide, LANES), F32),
            pltpu.VMEM(top_edges.shape, BF16),
            pltpu.SemaphoreType.DMA((1,)),
        ],
        scalars=(many + 7,),
        raw=(many + 8,),
        cost=6,
    )
    (fine_final,) = call(
        functools.partial(last_kernel, regions),
        over_region(coarse_final) + [fine_table, parent_rows, parent_blocks, fine_edges2],
        [((fine, LANES), BF16)],
        plain(fine_send, fine_recv) + level(4),
        cost=6,
    )
    return fine_final


def solution(mesh):
    spread = ("parts", "region", "sub")
    rows, flat = P(spread, None), P(spread)
    in_specs = (
        (rows, flat, flat, rows, rows, flat, flat, rows, rows, rows, flat, flat)
        + (P("parts"), P("parts"), P("parts", None))
        + (P(),) * 4
    )
    return jax.shard_map(on_device, mesh=mesh, in_specs=in_specs, out_specs=rows, check_vma=False)
```

```python
import functools

import jax
import jax.numpy as jnp
from jax import lax
from jax.experimental import pallas as pl
from jax.experimental.pallas import tpu as pltpu
from jax.sharding import PartitionSpec as P

EPSILON = 1e-05
TOP = 2048
LANES = 128
F32, BF16, I32, I16 = jnp.float32, jnp.bfloat16, jnp.int32, jnp.int16
GROUP, SLOTS = 8, 64
STEP = 3072
CUT_BITS = 8
CUT = 1 << CUT_BITS
TAIL = 16
LIMIT = 32 * 1024 * 1024


def dot(a, b):
    return jnp.dot(a, b, preferred_element_type=F32)


def lane_iota(rows, first=0):
    return lax.broadcasted_iota(I32, (rows, LANES), 1) + first


def column(row):
    return jnp.transpose(jnp.broadcast_to(row, (LANES, row.shape[1])))


def columns(rows):
    return jnp.concatenate([column(rows[i : i + 1]) for i in range(rows.shape[0])], axis=0)


def hot(mask):
    return jnp.where(mask, jnp.ones(mask.shape, BF16), jnp.zeros(mask.shape, BF16))


def short(row, count):
    return jnp.concatenate([jnp.broadcast_to(row, (16, LANES)).astype(I16)] * (count // 16), axis=0)


def hot_rows(col, count, start=0):
    col = col.astype(I16)
    places = [lane_iota(16, first) for first in range(start, start + count, LANES)]
    return jnp.concatenate([hot(col == short(place[:1], col.shape[0])) for place in places], axis=1)


def hot_cols(rows, count):
    return hot_codes(lax.broadcasted_iota(I32, (count, LANES), 0), rows)


def hot_codes(col, rows):
    col = col.astype(I16)
    return jnp.concatenate([hot(col == short(rows[i : i + 1], col.shape[0])) for i in range(rows.shape[0])], axis=1)


def gather(row, block, blocks, all_there=False):
    wide = dot(hot_rows(row, blocks[0].shape[0]), jnp.concatenate(blocks, axis=1))
    if block is None:
        return wide
    out = wide[:, :LANES] if all_there else jnp.zeros((row.shape[0], LANES), F32)
    for i in range(1 if all_there else 0, len(blocks)):
        out = jnp.where(block == i, wide[:, i * LANES : (i + 1) * LANES], out)
    return out


def cut(table):
    short = -table.shape[0] % CUT
    if short:
        table = jnp.concatenate([table, jnp.zeros((short, LANES), BF16)], axis=0)
    return [table[i : i + CUT] for i in range(0, table.shape[0], CUT)]


def segment_sum(rows, block, values):
    chosen = hot_cols(jnp.bitwise_and(rows, CUT - 1), CUT)
    if block is None:
        return dot(chosen, values)
    upper = values * jnp.where(block == 1, 1.0, 0.0).astype(BF16)
    out = dot(chosen, jnp.concatenate([values - upper, upper], axis=1))
    return jnp.concatenate([out[:, :LANES], out[:, LANES:]], axis=0)


def centre(second):
    exact = second.astype(F32)
    return (exact - jnp.mean(exact, axis=1, keepdims=True)).astype(BF16)


def perceptron(before, centred_second):
    out = dot(jnp.maximum(before, 0.0).astype(BF16), centred_second)
    return out * lax.rsqrt(jnp.mean(out * out, axis=-1, keepdims=True) + EPSILON)


def node_update(nodes, summed, first, second):
    joined = jnp.concatenate([nodes, summed.astype(BF16)], axis=1)
    return (nodes.astype(F32) + perceptron(dot(joined, first), centre(second))).astype(BF16)


def project(blocks, matrix):
    return [dot(block, matrix).astype(BF16) for block in blocks]


def edge_columns(own, count):
    shape = (count, LANES)
    if own == 2 * CUT:
        return [(shape, I16), (shape, I16), (shape, I32), (shape, I16), (shape, I32)]
    return [(shape, I16), (shape, I32), (shape, I16)]


def fill_columns(own, senders, receivers, outs):
    send, recv = columns(senders), columns(receivers)
    low, high = jnp.bitwise_and(send, CUT - 1), jnp.right_shift(send, CUT_BITS)
    if own == 2 * CUT:
        low = jnp.where(send < own, low, -1)
        values = [send, low, high, jnp.bitwise_and(recv, CUT - 1), jnp.right_shift(recv, CUT_BITS)]
    else:
        values = [low, high, recv]
    for value, out in zip(values, outs):
        out[...] = value.astype(out.dtype)


def from_own(cols, nodes, first):
    _, low, high, recv_low, recv_high = cols
    blocks = cut(nodes)
    sent, received = project(blocks, first[:LANES]), project(blocks, first[LANES : 2 * LANES])
    return lambda rows: (
        gather(low[rows, :], high[rows, :], sent, True) + gather(recv_low[rows, :], recv_high[rows, :], received, True)
    )


def from_halo(cols, halo, own, first):
    sent = dot(halo, first[:LANES]).astype(BF16)
    return lambda rows: dot(hot_rows(cols[0][rows, :], LANES, own), sent)


def from_table(cols, table, first):
    low, high, recv = cols
    sent = project(cut(table), first[:LANES])
    received = project([table[:CUT]], first[LANES : 2 * LANES])
    return lambda rows: gather(low[rows, :], high[rows, :], sent, True) + gather(recv[rows, :], None, received)


def finish(before_at, nodes, receivers, block, edges, weights, new_edges=None, step=STEP):
    second = centre(weights[1].get()[...])
    receivers = receivers.get()
    summed = 0.0
    for at in range(0, edges.shape[0], step):
        rows = slice(at, min(at + step, edges.shape[0]))
        edge = edges[rows, :]
        new = (edge.astype(F32) + perceptron(before_at(rows), second)).astype(BF16)
        if new_edges is not None:
            new_edges[rows, :] = new
        recv = receivers[rows.start // LANES : rows.stop // LANES, :]
        summed = summed + segment_sum(recv, None if block is None else block[rows, :], new)
    return node_update(nodes, summed, weights[2].get()[...], weights[3].get()[...])


def tail_of(block, count):
    return block[count : count + TAIL, :].astype(F32).astype(I32)


def row_layout(fine, coarse):
    f, c = fine // LANES, coarse // LANES
    return {"dest": 0, "target": f, "high": 2 * f, "low": 2 * f + c, "coarse": 2 * f + 2 * c, "fine_high": 2 * f + 2 * c + 1, "fine_low": 2 * f + 2 * c + 2}


def near_tails(tails, me, count):
    out = []
    for other in (me - 1, me + 1):
        there = jnp.logical_and(other >= 0, other < count)
        near = jnp.where(there, jnp.bitwise_xor(me, other), 0)
        picked = sum(jnp.where(near == j, tail, 0) for j, tail in enumerate(tails))
        out.append((other, there, picked))
    return out


def pick_kernel(halo, coarse_halo, fine, coarse, nodes, rows, coarse_rows, dest, target, parent, paired, crossed, own_tail, lists):
    at = row_layout(fine, coarse)
    lists[...] = jnp.zeros_like(lists)
    listed, coarse_listed = rows.get()[...], coarse_rows.get()[...]
    for side in (0, 1):
        lists[at["coarse"] : at["coarse"] + 1, side * coarse_halo : (side + 1) * coarse_halo] = coarse_listed[side : side + 1]
        lanes = slice(side * halo, (side + 1) * halo)
        lists[at["fine_high"] : at["fine_high"] + 1, lanes] = jnp.right_shift(listed[side : side + 1], 7)
        lists[at["fine_low"] : at["fine_low"] + 1, lanes] = jnp.bitwise_and(listed[side : side + 1], LANES - 1)
    lists[at["dest"] : at["target"], :] = dest.get()[...]
    lists[at["target"] : at["high"], :] = target.get()[...]
    parents = parent.get()[...]
    lists[at["high"] : at["low"], :] = jnp.right_shift(parents, 7)
    lists[at["low"] : at["coarse"], :] = jnp.bitwise_and(parents, LANES - 1)
    tail = lists[...].astype(F32).astype(BF16)
    nodes = nodes.get()
    odd = jnp.bitwise_and(lax.axis_index("region"), 1)
    for out, up in ((paired, 1 - odd), (crossed, odd)):
        col = column(jnp.where(up == 1, listed[1:2], listed[0:1]))
        out[:halo, :] = dot(hot_rows(col, fine), nodes[...]).astype(BF16)
        out[halo:, :] = tail
    own_tail[...] = tail


def lower_higher(paired, crossed):
    odd = jnp.bitwise_and(lax.axis_index("region"), 1) == 1
    paired, crossed = paired.astype(F32), crossed.astype(F32)
    return jnp.where(odd, paired, crossed).astype(BF16), jnp.where(odd, crossed, paired).astype(BF16)


def ready_kernel(nodes, senders, receivers, edges, first, _1, _2, _3, *outs):
    *cols, before = outs
    nodes, first = nodes.get()[...], first.get()[...]
    fill_columns(nodes.shape[0], senders.get()[...], receivers.get()[...], cols)
    edges, inner = edges.get(), from_own(cols, nodes, first)
    for at in range(0, edges.shape[0], STEP):
        rows = slice(at, min(at + STEP, edges.shape[0]))
        before[rows, :] = dot(edges[rows, :], first[2 * LANES :]) + inner(rows)


def fine_kernel(halo, paired, crossed, tail, before, *refs):
    cols, (nodes, receivers, edges, *weights), (payload, new_edges) = refs[:5], refs[5:12], refs[12:]
    nodes = nodes.get()[...]
    fine = nodes.shape[0]
    outer = jnp.concatenate(lower_higher(paired[:halo, :], crossed[:halo, :]), axis=0)
    outside = from_halo(cols, outer, fine, weights[0].get()[...])
    payload[:fine, :] = finish(lambda rows: before[rows, :] + outside(rows), nodes, receivers, cols[-1], edges.get(), weights, new_edges)
    payload[fine:, :] = tail[...]


def columns_kernel(own, senders, receivers, edges, first, *outs):
    *cols, before = outs
    fill_columns(own, senders.get()[...], receivers.get()[...], cols)
    before[...] = dot(edges.get()[...], first.get()[2 * LANES :, :])


def edge_kernel(edges, first, before):
    before[...] = dot(edges[...], first.get()[2 * LANES :, :])


def coarse_kernel(regions, halo, coarse, *refs):
    blocks, (before, *rest) = refs[:regions], refs[regions:]
    cols, (receivers, edges, *weights), (payload, new_edges) = rest[:3], rest[3:9], rest[9:]
    me = lax.axis_index("region")
    fine = blocks[0].shape[0] - TAIL
    at = row_layout(fine, coarse)
    tails = [tail_of(block, fine) for block in blocks]
    near = near_tails(tails, me, regions)
    codes = [me * coarse + lax.broadcasted_iota(I32, (coarse, LANES), 0)]
    for side, (other, there, tail) in enumerate(near):
        listed = tail[at["coarse"] : at["coarse"] + 1, :]
        first = halo * (1 - side)
        col = columns(listed)[first : first + halo]
        codes.append(jnp.where(there, other * coarse + col, -1))
    codes = jnp.concatenate(codes, axis=0)
    half = codes.shape[0] // 2
    parts = []
    for part in (codes[:half], codes[half:]):
        total, members = 0.0, 0.0
        for block, tail in zip(blocks, tails):
            f = fine // LANES
            parent = tail[at["dest"] : at["dest"] + f] * coarse + tail[at["target"] : at["target"] + f]
            more, counted = sums_and_counts(hot_codes(part, parent), block[:fine, :])
            total, members = total + more, members + counted
        parts.append((total / jnp.maximum(members, 1.0)).astype(BF16))
    table = jnp.concatenate(parts, axis=0)
    inner = from_table(cols, table, weights[0].get()[...])
    payload[:coarse, :] = finish(lambda rows: before[rows, :] + inner(rows), table[:coarse], receivers, None, edges.get(), weights, new_edges)
    own_tail = tails[0]
    c = coarse // LANES
    payload[coarse:, :] = jnp.concatenate(
        [own_tail[at["high"] : at["high"] + 2 * c], jnp.zeros((TAIL - 2 * c, LANES), I32)], axis=0
    ).astype(F32).astype(BF16)


def compact(first, ranks, codes, edges, size, at_once=8):
    place = lax.broadcasted_iota(I32, (size, LANES), 0) + first

    def body(g, carry):
        latents, found = carry
        rank = ranks[pl.ds(pl.multiple_of(g * at_once, at_once), at_once), :]
        code = codes[pl.ds(pl.multiple_of(g * at_once, at_once), at_once), :]
        for i in range(at_once):
            found = found + jnp.where(place == rank[i : i + 1], code[i : i + 1], 0)
        wide = at_once * LANES
        rows = edges[pl.ds(pl.multiple_of(g * wide, wide), wide), :]
        return latents + dot(hot_codes(place, rank), rows), found

    zero = jnp.zeros((size, LANES), F32), jnp.zeros((size, LANES), I32)
    latents, found = lax.fori_loop(0, ranks.shape[0] // at_once, body, zero)
    found = jnp.sum(found.astype(F32), axis=1, keepdims=True).astype(I32)
    return latents.astype(BF16), jnp.broadcast_to(found, (size, LANES))


def below(rows, same):
    square = (rows, rows)
    mask = same(lax.broadcasted_iota(I32, square, 0), lax.broadcasted_iota(I32, square, 1))
    return jnp.where(mask, 1.0, 0.0).astype(BF16)


def running(flags):
    upto = jnp.where(lax.broadcasted_iota(I32, (LANES, LANES), 0) <= lane_iota(LANES), 1.0, 0.0).astype(BF16)
    inside = dot(flags.astype(BF16), upto)
    return inside, jnp.broadcast_to(inside[:, LANES - 1 :], flags.shape)


def listed_kernel(regions, halo, fine, coarse, *refs):
    own, paired, crossed, senders, receivers, edges, parents, firsts, halo_rows, halo_blocks, ranks, codes = refs[:12]
    latents, send, recv, recv_rows = refs[12:]
    me = lax.axis_index("region")
    at = row_layout(fine, coarse)
    start = paired.shape[0] - TAIL
    lower, higher = lower_higher(paired[start:, :], crossed[start:, :])
    own_tail, lower_tail, higher_tail = (tail.astype(F32).astype(I32) for tail in (own[...], lower, higher))
    near = ((me - 1, me > 0, lower_tail), (me + 1, me < regions - 1, higher_tail))
    c = coarse // LANES
    wide, size = parents.shape[0], latents.shape[0]

    def own_parents(tail):
        return tail[at["high"] : at["high"] + c] * LANES + tail[at["low"] : at["low"] + c]

    cols = [columns(own_parents(own_tail))]
    for side, (other, there, tail) in enumerate(near):
        first = halo * (1 - side)
        col = columns(tail[at["coarse"] : at["coarse"] + 1])[first : first + halo]
        halo_rows[side * halo : (side + 1) * halo, :] = col
        halo_blocks[side * halo : (side + 1) * halo, :] = jnp.full(col.shape, jnp.where(there, jnp.bitwise_xor(me, other), -1))
        theirs = own_parents(tail).astype(F32)
        value = jnp.zeros((halo, LANES), F32)
        for i in range(c):
            value = value + jnp.where(col == lane_iota(halo, i * LANES), theirs[i : i + 1], 0.0)
        value = jnp.broadcast_to(jnp.sum(value, axis=1, keepdims=True), (halo, LANES)).astype(I32)
        cols.append(jnp.where(there, value, -1))
    cols.append(jnp.full((wide - coarse - 2 * halo, LANES), -1, I32))
    cols = jnp.concatenate(cols, axis=0)
    parents[...] = cols

    high_count = TOP // LANES
    rows = as_rows(cols)
    row_at = lax.broadcasted_iota(I32, (wide, LANES), 0)
    for i in range(wide // LANES):
        earlier = jnp.logical_and(cols == rows[i : i + 1], row_at < lane_iota(wide, i * LANES))
        seen = jnp.max(jnp.where(earlier, 1.0, 0.0), axis=0, keepdims=True)
        firsts[i : i + 1, :] = jnp.where(seen > 0.0, -2, rows[i : i + 1])
    tops = dot(
        hot_cols(jnp.right_shift(rows, 7), high_count), hot_rows(jnp.bitwise_and(cols, LANES - 1), LANES)
    )
    tops = jnp.minimum(tops, 1.0).astype(BF16)
    receivers = receivers.get()
    count = receivers.shape[0]
    high = lax.broadcasted_iota(I32, (high_count, LANES), 0)
    needed = []
    for i in range(0, count, 8):
        some = receivers[i : i + 8, :]
        match = dot(tops, hot_cols(jnp.bitwise_and(some, LANES - 1), LANES))
        for k in range(8):
            mine = jnp.where(high == jnp.right_shift(some[k : k + 1], 7), match[:, k * LANES : (k + 1) * LANES], 0.0)
            needed.append(jnp.sum(mine, axis=0, keepdims=True))
    needed = jnp.concatenate(needed, axis=0)

    group_of = lambda i: jnp.right_shift(i, GROUP.bit_length() - 1)
    inside, sums = running(needed)
    sums = sums.astype(BF16)
    local = dot(below(count, lambda i, j: jnp.logical_and(j < i, group_of(i) == group_of(j))), sums) + inside - 1.0
    in_group = dot(below(count, lambda i, j: group_of(i) == group_of(j)), sums)
    used = jnp.minimum(in_group, float(SLOTS))
    before = dot(below(count, lambda i, j: group_of(j) < group_of(i)), (used / GROUP).astype(BF16))
    placed = jnp.logical_and(local < SLOTS, local + before < size)
    others = jnp.where(placed, 0.0, needed)
    inside, sums = running(others)
    rank = dot(below(count, lambda i, j: j < i), sums.astype(BF16)) + inside - 1.0
    ranks[...] = jnp.where(others > 0.0, rank, -1.0).astype(I32)
    total = jnp.sum(jnp.sum(needed - others, axis=0, keepdims=True), axis=1, keepdims=True).astype(I32)
    codes[...] = senders.get()[...] * TOP + receivers[...]

    slot = jnp.where(needed > 0.0, local, -1.0).astype(I32)
    place = lax.broadcasted_iota(I32, (SLOTS, LANES), 0)
    edges = edges.get()
    lane = lane_iota(SLOTS)
    slots, targets = [], []
    for first in range(0, count, GROUP):
        code = jnp.zeros((SLOTS, LANES), F32)
        for i in range(first, first + GROUP):
            code = code + jnp.where(place == slot[i : i + 1], codes[i : i + 1, :].astype(F32), 0.0)
        code = jnp.broadcast_to(jnp.sum(code, axis=1, keepdims=True), (SLOTS, LANES)).astype(I32)
        parts = jnp.where(
            lane == 0,
            jnp.right_shift(code, 16),
            jnp.where(lane == 1, jnp.bitwise_and(jnp.right_shift(code, 8), 255), jnp.bitwise_and(code, 255)),
        )
        parts = jnp.where(lane < 3, parts, 0).astype(F32).astype(BF16)
        chosen = hot_cols(slot[first : first + GROUP], SLOTS)
        packed = dot(chosen, edges[first * LANES : (first + GROUP) * LANES, :]).astype(BF16)
        slots.append(jnp.concatenate([packed, parts], axis=1))
        target = before[first : first + 1] + lane_iota(1).astype(F32)
        targets.append(jnp.where(lane_iota(1).astype(F32) < used[first : first + 1], target, -1.0).astype(I32)[:, :SLOTS])
    per = LANES // SLOTS
    targets = [jnp.concatenate(targets[i : i + per], axis=1) for i in range(0, len(targets), per)]
    packed = dot(hot_cols(jnp.concatenate(targets, axis=0), size), jnp.concatenate(slots, axis=0))
    latents[...] = packed[:, :LANES].astype(BF16)
    parts = packed[:, LANES:]
    lane = lane_iota(size)
    code = jnp.where(lane == 0, parts * 65536.0, jnp.where(lane == 1, parts * 256.0, parts))
    code = jnp.broadcast_to(jnp.sum(code, axis=1, keepdims=True), (size, LANES)).astype(I32)
    send[...], recv[...] = ends(code, 0, total)
    recv_rows[...] = as_rows(recv[...])


def ends(code, first_place, total):
    place = lax.broadcasted_iota(I32, code.shape, 0) + first_place
    recv = jnp.where(place < total, jnp.bitwise_and(code, TOP - 1), -3)
    return jnp.right_shift(code, TOP.bit_length() - 1), recv


def parent_kernel(regions, halo, coarse, *refs):
    blocks, (table, parent_rows, parent_blocks) = refs[:regions], refs[regions:]
    me = lax.axis_index("region")
    fine = blocks[0].shape[0] - TAIL
    at = row_layout(fine, coarse)
    tails = [tail_of(block, fine) for block in blocks]
    f = fine // LANES

    def own_parents(tail):
        return tail[at["dest"] : at["dest"] + f] * coarse + tail[at["target"] : at["target"] + f]

    table[:fine, :] = blocks[0][:fine, :]
    owner = lambda tail: tail[at["dest"] : at["dest"] + f]
    parent_rows[:fine, :] = columns(tails[0][at["target"] : at["target"] + f])
    parent_blocks[:fine, :] = jnp.bitwise_xor(columns(owner(tails[0])), me)
    for side, (other, there, tail) in enumerate(near_tails(tails, me, regions)):
        rows = slice(fine + side * halo, fine + (side + 1) * halo)
        first = halo * (1 - side)
        listed = tail[at["fine_high"] : at["fine_high"] + 1] * LANES + tail[at["fine_low"] : at["fine_low"] + 1]
        col = columns(listed)[first : first + halo]
        theirs = own_parents(tail).astype(F32)
        value = jnp.zeros((halo, LANES), F32)
        for i in range(f):
            value = value + jnp.where(col == lane_iota(halo, i * LANES), theirs[i : i + 1], 0.0)
        value = jnp.broadcast_to(jnp.sum(value, axis=1, keepdims=True), (halo, LANES)).astype(I32)
        parent_rows[rows, :] = jnp.bitwise_and(value, coarse - 1)
        block = jnp.bitwise_xor(jnp.right_shift(value, coarse.bit_length() - 1), me)
        parent_blocks[rows, :] = jnp.where(there, block, -1)
        total = jnp.zeros((halo, LANES), F32)
        for j, block in enumerate(blocks):
            here = jnp.logical_and(there, jnp.bitwise_xor(me, j) == other)
            total = total + dot(hot_rows(jnp.where(here, col, -1), fine), block[:fine, :])
        table[rows, :] = total.astype(BF16)


def sums_and_counts(chosen, rows):
    both = dot(chosen, jnp.concatenate([rows, jnp.ones(rows.shape, BF16)], axis=1))
    return both[:, :LANES], both[:, LANES:]


def pooled(cols, blocks, coarse):
    c = coarse // LANES

    def add(block, sums):
        tail = tail_of(block, coarse)
        parent = tail[:c] * LANES + tail[c : 2 * c]
        more = [sums_and_counts(hot_codes(col, parent), block[:coarse, :]) for col in cols]
        return tuple((total + a, members + b) for (total, members), (a, b) in zip(sums, more))

    sums = tuple((jnp.zeros(col.shape, F32),) * 2 for col in cols)
    if isinstance(blocks, tuple):
        for block in blocks:
            sums = add(block, sums)
    else:
        sums = lax.fori_loop(0, blocks.shape[0], lambda n, sums: add(blocks.at[n], sums), sums)
    return [(total / jnp.maximum(members, 1.0)).astype(BF16) for total, members in sums]


def as_rows(col):
    return jnp.concatenate(
        [jnp.transpose(col[i : i + LANES])[:1] for i in range(0, col.shape[0], LANES)], axis=0
    )


def top_kernel(regions, halo, coarse, size, count, *refs):
    subs = lax.axis_size("sub")
    if count > 1:
        rows = coarse + TAIL
        there = [refs[count - 1].at[i * rows : (i + 1) * rows] for i in range(count - 1)]
        blocks = tuple((there if j % 2 else refs)[j // 2 * subs + k] for j in range(regions) for k in range(subs))
    else:
        blocks = refs[0]
    refs = refs[count:]
    parents, firsts, halo_rows, halo_blocks, ranks, codes, latents, send, recv, recv_rows, all_edges = refs[:11]
    edges, before3, *cols = refs[11:16]
    receivers, top_weights, weights = refs[16], refs[17:21], refs[21:25]
    out, agg, fallback, semaphore = refs[25:]
    me = lax.axis_index("region")
    own_sub = lambda j: blocks[j * subs] if count > 1 else blocks.at[j * subs]
    mine, firsts = parents[...], firsts[...]
    top_own, from_send = pooled([mine, send[...]], blocks, coarse)
    first, second = top_weights[0].get()[...], centre(top_weights[1].get()[...])
    received = dot(top_own, first[LANES : 2 * LANES]).astype(BF16)
    others = jnp.concatenate([first[:LANES], first[2 * LANES :]], axis=0)

    def one(edge, from_send, recv, recv_rows):
        before = dot(jnp.concatenate([from_send, edge], axis=1), others) + dot(hot_codes(recv, firsts), received)
        new = (edge.astype(F32) + perceptron(before, second)).astype(BF16)
        return dot(hot_codes(mine, recv_rows), new)

    agg[...] = one(latents[...], from_send, recv[...], recv_rows[...])

    def more(b, carry):
        copy = pltpu.make_async_copy(all_edges, fallback, semaphore.at[0])
        copy.start()
        copy.wait()
        edge, code = compact(b * size, ranks, codes, fallback, size)
        send, recv = ends(code, b * size, left)
        (from_send,) = pooled([send], blocks, coarse)
        agg[...] += one(edge, from_send, recv, as_rows(recv))
        return carry

    left = jnp.max(ranks[...]) + 1
    lax.fori_loop(0, (left + size - 1) // size, more, 0)
    top_final = node_update(top_own, agg[...], top_weights[2].get()[...], top_weights[3].get()[...])
    near = gather(halo_rows[...], halo_blocks[...], [own_sub(j)[:coarse, :] for j in range(regions)])
    down = jnp.concatenate([own_sub(0)[:coarse, :].astype(F32), near], axis=0)
    table = (down + top_final[: coarse + 2 * halo].astype(F32)).astype(BF16)
    inner = from_table(cols, table, weights[0].get()[...])
    out[...] = finish(lambda rows: before3[rows, :] + inner(rows), table[:coarse], receivers, None, edges, weights)


def last_kernel(regions, *refs):
    blocks, (down, parent_rows, parent_blocks, edges, before, *rest) = refs[:regions], refs[regions:]
    cols, receivers, weights, out = rest[:5], rest[5], rest[6:10], rest[10]
    own = out.shape[0]
    parent = gather(parent_rows[...], parent_blocks[...], [block[...] for block in blocks])
    table = (down[...].astype(F32) + parent).astype(BF16)
    first = weights[0].get()[...]
    inner, outside = from_own(cols, table[:own], first), from_halo(cols, table[own:], own, first)
    out[...] = finish(lambda rows: before[rows, :] + inner(rows) + outside(rows), table[:own], receivers, cols[-1], edges, weights)


class Here:
    def __init__(self, place):
        self.place = place

    def get(self):
        return self.place


class Arriving(Here):
    def __init__(self, source, place, semaphore):
        super().__init__(place)
        self.copy, self.waiting = pltpu.make_async_copy(source, place, semaphore), True
        self.copy.start()

    def get(self):
        if self.waiting:
            self.copy.wait()
            self.waiting = False
        return self.place


def call(kernel, args, outs, more=(), scratch=(), raw=(), cost=1, far=False, limit=LIMIT):
    specs = [pl.BlockSpec(memory_space=pltpu.HBM if i in raw else pltpu.VMEM) for i in range(len(args))]
    specs += [pl.BlockSpec(memory_space=pltpu.HBM if far else pltpu.VMEM)] * len(more)
    out_specs = [pl.BlockSpec(memory_space=pltpu.VMEM)] * len(outs)
    places = []
    if far:
        places = [pltpu.VMEM(array.shape, array.dtype) for array, _ in more]
        places.append(pltpu.SemaphoreType.DMA((len(more),)))
    n, k, o = len(args), len(more), len(outs)

    def body(*refs):
        given, sources, results, rest = refs[:n], refs[n : n + k], refs[n + k : n + k + o], refs[n + k + o :]
        if far:
            near, semaphores, rest = rest[:k], rest[k], rest[k + 1 :]
            operands = [Arriving(source, near[i], semaphores.at[i]) for i, source in enumerate(sources)]
        else:
            operands = [Here(ref if at is None else ref.at[at]) for ref, (_, at) in zip(sources, more)]
        kernel(*given, *operands, *results, *rest)

    return pl.pallas_call(
        body,
        out_shape=[jax.ShapeDtypeStruct(shape, dtype) for shape, dtype in outs],
        in_specs=specs,
        out_specs=out_specs,
        scratch_shapes=places + list(scratch),
        compiler_params=pltpu.CompilerParams(vmem_limit_bytes=limit),
        cost_estimate=pl.CostEstimate(flops=cost * 10**9, bytes_accessed=cost * 10**5, transcendentals=0),
    )(*args, *[array for array, _ in more])


def over_region(rows, beside=None):
    count = lax.axis_size("region")
    blocks = {0: rows}
    bit = count // 2
    while bit:
        going = dict(blocks)
        if beside is not None and len(going) > 1:
            far = max(going)
            going[far], beside = lax.optimization_barrier((going[far], beside))
        for j in blocks:
            going[j + bit] = lax.ppermute(going[j], "region", [(i, i ^ bit) for i in range(count)])
        blocks = going
        bit //= 2
    blocks = [blocks[j] for j in range(count)]
    return blocks if beside is None else (blocks, beside)


def over_both(rows, beside):
    regions, subs = lax.axis_size("region"), lax.axis_size("sub")
    swap = lambda array, axis, bits: lax.ppermute(array, axis, [(i, i ^ bits) for i in range(lax.axis_size(axis))])
    turns = [rows] + [swap(rows, "sub", k) for k in range(1, subs)]
    if regions * subs <= 16:
        turns[-1], beside = lax.optimization_barrier((turns[-1], beside))
        blocks = {0: turns}
        bit = regions // 2
        while bit > 1:
            for j in list(blocks):
                blocks[j + bit] = [swap(block, "region", bit) for block in blocks[j]]
            bit //= 2
        here = [block for j in range(0, regions, 2) for block in blocks[j]]
        return here + [swap(jnp.concatenate(here), "region", 1)], beside
    blocks, bit = jnp.stack(turns), 1
    while bit < regions:
        blocks, bit = jnp.concatenate([blocks, swap(blocks, "region", bit)]), 2 * bit
    return [blocks], beside


def on_device(
    node_feats,
    fine_senders,
    fine_receivers,
    fine_edges,
    halo_rows,
    coarse_senders,
    coarse_receivers,
    coarse_edges,
    coarse_halo_rows,
    pool_dest,
    pool_target,
    pool3_target,
    top_senders,
    top_receivers,
    top_edges,
    edge_in,
    edge_out,
    node_in,
    node_out,
):
    weights = (edge_in, edge_out, node_in, node_out)
    regions = lax.axis_size("region")
    fine, coarse = node_feats.shape[0], pool3_target.shape[0]
    halo, halo2 = halo_rows.shape[1], coarse_halo_rows.shape[1]
    rows = lambda a: a.reshape(-1, LANES)
    fine_send, fine_recv = rows(fine_senders), rows(fine_receivers)
    coarse_send, coarse_recv = rows(coarse_senders), rows(coarse_receivers)
    top_send, top_recv = rows(top_senders), rows(top_receivers)

    level = lambda index: [(matrix, index) for matrix in weights]
    plain = lambda *arrays: [(array, None) for array in arrays]

    to_pair, to_other, tail = call(
        functools.partial(pick_kernel, halo, halo2, fine, coarse),
        [],
        [((halo + TAIL, LANES), BF16)] * 2 + [((TAIL, LANES), BF16)],
        plain(node_feats, halo_rows, coarse_halo_rows, rows(pool_dest), rows(pool_target), rows(pool3_target)),
        scratch=[pltpu.VMEM((TAIL, LANES), I32)],
        far=True,
        limit=60 * 1024 * 1024,
    )
    pairs = lambda first: [(i, j) for low in range(first, regions - 1, 2) for i, j in ((low, low + 1), (low + 1, low))]
    paired = lax.ppermute(to_pair, "region", pairs(0))
    crossed = lax.ppermute(to_other, "region", pairs(1))
    one = lambda index: [(edge_in, index)]
    fine_cols, coarse_cols = edge_columns(fine, fine_edges.shape[0]), edge_columns(coarse, coarse_edges.shape[0])
    late_send, tail = lax.optimization_barrier((fine_send, tail))
    *fine_cols, before = call(
        ready_kernel,
        [],
        fine_cols + [(fine_edges.shape, F32)],
        plain(node_feats, late_send, fine_recv, fine_edges) + level(0),
        cost=2,
    )
    payload, fine_edges2 = call(
        functools.partial(fine_kernel, halo),
        [paired, crossed, tail, before, *fine_cols],
        [((fine + TAIL, LANES), BF16), (fine_edges.shape, BF16)],
        plain(node_feats, fine_recv, fine_edges) + level(0),
        cost=3,
    )
    wide = -(-(coarse + 2 * halo2) // LANES) * LANES
    size = min(384, top_edges.shape[0])
    listed_shapes = [
        ((wide, LANES), I32),
        ((wide // LANES, LANES), I32),
        ((2 * halo2, LANES), I32),
        ((2 * halo2, LANES), I32),
        (top_send.shape, I32),
        (top_send.shape, I32),
        ((size, LANES), BF16),
        ((size, LANES), I32),
        ((size, LANES), I32),
        ((size // LANES, LANES), I32),
    ]
    selected = call(
        functools.partial(listed_kernel, regions, halo2, fine, coarse),
        [tail, paired, crossed],
        listed_shapes,
        plain(top_send, top_recv, top_edges),
        cost=3,
    )
    payload, late_edges = lax.optimization_barrier((payload, coarse_edges))
    *coarse_cols, before = call(
        functools.partial(columns_kernel, coarse),
        [],
        coarse_cols + [(coarse_edges.shape, F32)],
        plain(coarse_send, coarse_recv, late_edges) + one(1),
    )
    blocks, selected = over_region(payload, selected)
    payload2, coarse_edges2 = call(
        functools.partial(coarse_kernel, regions, halo2, coarse),
        blocks + [before, *coarse_cols],
        [((coarse + TAIL, LANES), BF16), (coarse_edges.shape, BF16)],
        plain(coarse_recv, coarse_edges) + level(1),
        cost=3,
    )
    table_shape = (fine + 2 * halo, LANES)
    table = call(
        functools.partial(parent_kernel, regions, halo, coarse),
        blocks,
        [(table_shape, BF16), (table_shape, I32), (table_shape, I32)],
    )
    before = call(edge_kernel, [coarse_edges2], [(coarse_edges.shape, F32)], one(3))
    blocks2, (table, before) = over_both(payload2, (table, before))
    many = len(blocks2)
    (coarse_final,) = call(
        functools.partial(top_kernel, regions, halo2, coarse, size, many),
        blocks2 + [*selected, top_edges, coarse_edges2, *before, *coarse_cols],
        [((coarse, LANES), BF16)],
        plain(coarse_recv) + level(2) + level(3),
        scratch=[
            pltpu.VMEM((wide, LANES), F32),
            pltpu.VMEM(top_edges.shape, BF16),
            pltpu.SemaphoreType.DMA((1,)),
        ],
        raw=(many + len(selected),),
        cost=6,
    )
    before = call(edge_kernel, [fine_edges2], [(fine_edges.shape, F32)], one(4))
    blocks3, before = over_region(coarse_final, before)
    (fine_final,) = call(
        functools.partial(last_kernel, regions),
        blocks3 + [*table, fine_edges2, *before, *fine_cols],
        [((fine, LANES), BF16)],
        plain(fine_recv) + level(4),
        cost=3,
    )
    return fine_final


def solution(mesh):
    spread = ("parts", "region", "sub")
    rows, flat = P(spread, None), P(spread)
    in_specs = (
        (rows, flat, flat, rows, rows, flat, flat, rows, rows, rows, flat, flat)
        + (P("parts"), P("parts"), P("parts", None))
        + (P(),) * 4
    )
    return jax.shard_map(on_device, mesh=mesh, in_specs=in_specs, out_specs=rows, check_vma=False)
```

```python
import functools

import jax
import jax.numpy as jnp
from jax import lax
from jax.experimental import pallas as pl
from jax.experimental.pallas import tpu as pltpu
from jax.sharding import PartitionSpec as P

EPSILON = 1e-05
TOP = 2048
LANES = 128
F32, BF16, I32, I16 = jnp.float32, jnp.bfloat16, jnp.int32, jnp.int16
GROUP, SLOTS = 8, 64
STEP = 3072
CUT_BITS = 8
CUT = 1 << CUT_BITS
TAIL = 16
LIMIT = 32 * 1024 * 1024


def dot(a, b):
    return jnp.dot(a, b, preferred_element_type=F32)


def lane_iota(rows, first=0):
    return lax.broadcasted_iota(I32, (rows, LANES), 1) + first


def column(row):
    return jnp.transpose(jnp.broadcast_to(row, (LANES, row.shape[1])))


def columns(rows):
    return jnp.concatenate([column(rows[i : i + 1]) for i in range(rows.shape[0])], axis=0)


def hot(mask):
    return jnp.where(mask, jnp.ones(mask.shape, BF16), jnp.zeros(mask.shape, BF16))


def short(row, count):
    return jnp.concatenate([jnp.broadcast_to(row, (16, LANES)).astype(I16)] * (count // 16), axis=0)


def hot_rows(col, count, start=0):
    col = col.astype(I16)
    places = [lane_iota(16, first) for first in range(start, start + count, LANES)]
    return jnp.concatenate([hot(col == short(place[:1], col.shape[0])) for place in places], axis=1)


def hot_cols(rows, count):
    return hot_codes(lax.broadcasted_iota(I32, (count, LANES), 0), rows)


def hot_codes(col, rows):
    col = col.astype(I16)
    return jnp.concatenate([hot(col == short(rows[i : i + 1], col.shape[0])) for i in range(rows.shape[0])], axis=1)


def gather(row, block, blocks, all_there=False):
    return pick(hot_rows(row, blocks[0].shape[0]), block, blocks, all_there)


def pick(hots, block, blocks, all_there=False):
    wide = dot(hots, jnp.concatenate(blocks, axis=1))
    if block is None:
        return wide
    out = wide[:, :LANES] if all_there else jnp.zeros((hots.shape[0], LANES), F32)
    for i in range(1 if all_there else 0, len(blocks)):
        out = jnp.where(block == i, wide[:, i * LANES : (i + 1) * LANES], out)
    return out


def cut(table):
    short = -table.shape[0] % CUT
    if short:
        table = jnp.concatenate([table, jnp.zeros((short, LANES), BF16)], axis=0)
    return [table[i : i + CUT] for i in range(0, table.shape[0], CUT)]


def segment_sum(rows, block, values):
    chosen = hot_cols(jnp.bitwise_and(rows, CUT - 1), CUT)
    if block is None:
        return jnp.concatenate([dot(chosen[: CUT // 2], values), dot(chosen[CUT // 2 :], values)], axis=0)
    upper = values * block
    wide = jnp.concatenate([values - upper, upper], axis=1)
    out = jnp.concatenate([dot(chosen[: CUT // 2], wide), dot(chosen[CUT // 2 :], wide)], axis=0)
    return jnp.concatenate([out[:, :LANES], out[:, LANES:]], axis=0)


def centre(second):
    exact = second.astype(F32)
    return (exact - jnp.mean(exact, axis=1, keepdims=True)).astype(BF16)


def perceptron(before, centred_second):
    out = dot(jnp.maximum(before.astype(BF16), 0.0), centred_second)
    return out * lax.rsqrt(jnp.mean(out * out, axis=-1, keepdims=True) + EPSILON)


def node_update(nodes, summed, first, second):
    joined = jnp.concatenate([nodes, summed.astype(BF16)], axis=1)
    return (nodes.astype(F32) + perceptron(dot(joined, first), centre(second))).astype(BF16)


def project(blocks, matrix):
    return [dot(block, matrix).astype(BF16) for block in blocks]


def edge_columns(own, count):
    shape = (count, LANES)
    if own == 2 * CUT:
        return [(shape, I16), (shape, I16), (shape, I32), (shape, I16), (shape, I32), (shape, BF16)]
    return [(shape, I16), (shape, I32), (shape, I16)]


def fill_columns(own, senders, receivers, outs):
    send, recv = columns(senders), columns(receivers)
    low, high = jnp.bitwise_and(send, CUT - 1), jnp.right_shift(send, CUT_BITS)
    if own == 2 * CUT:
        low = jnp.where(send < own, low, -1)
        recv_high = jnp.right_shift(recv, CUT_BITS)
        values = [send, low, high, jnp.bitwise_and(recv, CUT - 1), recv_high, recv_high.astype(F32)]
    else:
        values = [low, high, recv]
    for value, out in zip(values, outs):
        out[...] = value.astype(out.dtype)


def from_own(cols, nodes, first):
    _, low, high, recv_low, recv_high, _ = cols
    blocks = cut(nodes)
    sent, received = project(blocks, first[:LANES]), project(blocks, first[LANES : 2 * LANES])
    return lambda rows: (
        gather(low[rows, :], high[rows, :], sent, True) + gather(recv_low[rows, :], recv_high[rows, :], received, True)
    )


def from_halo(cols, halo, own, first):
    sent = dot(halo, first[:LANES]).astype(BF16)
    return lambda rows: dot(hot_rows(cols[0][rows, :], LANES, own), sent)


def from_table(cols, table, first):
    low, high, recv = cols
    sent = project(cut(table), first[:LANES])
    received = project([table[:CUT]], first[LANES : 2 * LANES])
    return lambda rows: gather(low[rows, :], high[rows, :], sent, True) + gather(recv[rows, :], None, received)


def finish(before_at, nodes, receivers, block, edges, weights, new_edges=None, step=STEP):
    second = centre(weights[1].get()[...])
    receivers = receivers.get()
    summed = 0.0
    for at in range(0, edges.shape[0], step):
        rows = slice(at, min(at + step, edges.shape[0]))
        edge = edges[rows, :]
        new = (edge.astype(F32) + perceptron(before_at(rows), second)).astype(BF16)
        if new_edges is not None:
            new_edges[rows, :] = new
        recv = receivers[rows.start // LANES : rows.stop // LANES, :]
        summed = summed + segment_sum(recv, None if block is None else block[rows, :], new)
    return node_update(nodes, summed, weights[2].get()[...], weights[3].get()[...])


def tail_of(block, count):
    return block[count : count + TAIL, :].astype(F32).astype(I32)


def row_layout(fine, coarse):
    f, c = fine // LANES, coarse // LANES
    return {"dest": 0, "target": f, "high": 2 * f, "low": 2 * f + c, "coarse": 2 * f + 2 * c, "fine_high": 2 * f + 2 * c + 1, "fine_low": 2 * f + 2 * c + 2}


def near_tails(tails, me, count):
    out = []
    for other in (me - 1, me + 1):
        there = jnp.logical_and(other >= 0, other < count)
        near = jnp.where(there, jnp.bitwise_xor(me, other), 0)
        picked = sum(jnp.where(near == j, tail, 0) for j, tail in enumerate(tails))
        out.append((other, there, picked))
    return out


def pick_kernel(halo, coarse_halo, fine, coarse, nodes, rows, coarse_rows, dest, target, parent, paired, crossed, own_tail, lists):
    at = row_layout(fine, coarse)
    lists[...] = jnp.zeros_like(lists)
    listed, coarse_listed = rows.get()[...], coarse_rows.get()[...]
    for side in (0, 1):
        lists[at["coarse"] : at["coarse"] + 1, side * coarse_halo : (side + 1) * coarse_halo] = coarse_listed[side : side + 1]
        lanes = slice(side * halo, (side + 1) * halo)
        lists[at["fine_high"] : at["fine_high"] + 1, lanes] = jnp.right_shift(listed[side : side + 1], 7)
        lists[at["fine_low"] : at["fine_low"] + 1, lanes] = jnp.bitwise_and(listed[side : side + 1], LANES - 1)
    lists[at["dest"] : at["target"], :] = dest.get()[...]
    lists[at["target"] : at["high"], :] = target.get()[...]
    parents = parent.get()[...]
    lists[at["high"] : at["low"], :] = jnp.right_shift(parents, 7)
    lists[at["low"] : at["coarse"], :] = jnp.bitwise_and(parents, LANES - 1)
    tail = lists[...].astype(F32).astype(BF16)
    nodes = nodes.get()
    odd = jnp.bitwise_and(lax.axis_index("region"), 1)
    for out, up in ((paired, 1 - odd), (crossed, odd)):
        col = column(jnp.where(up == 1, listed[1:2], listed[0:1]))
        out[:halo, :] = dot(hot_rows(col, fine), nodes[...]).astype(BF16)
        out[halo:, :] = tail
    own_tail[...] = tail


def lower_higher(paired, crossed):
    odd = jnp.bitwise_and(lax.axis_index("region"), 1) == 1
    paired, crossed = paired.astype(F32), crossed.astype(F32)
    return jnp.where(odd, paired, crossed).astype(BF16), jnp.where(odd, crossed, paired).astype(BF16)


def ready_kernel(nodes, senders, receivers, edges, first, _1, _2, _3, *outs):
    *cols, before = outs
    nodes, first = nodes.get()[...], first.get()[...]
    fill_columns(nodes.shape[0], senders.get()[...], receivers.get()[...], cols)
    edges, inner = edges.get(), from_own(cols, nodes, first)
    for at in range(0, edges.shape[0], STEP):
        rows = slice(at, min(at + STEP, edges.shape[0]))
        before[rows, :] = dot(edges[rows, :], first[2 * LANES :]) + inner(rows)


def fine_kernel(halo, paired, crossed, tail, before, *refs):
    cols, (nodes, receivers, edges, *weights), (payload, new_edges) = refs[:6], refs[6:13], refs[13:]
    nodes = nodes.get()[...]
    fine = nodes.shape[0]
    outer = jnp.concatenate(lower_higher(paired[:halo, :], crossed[:halo, :]), axis=0)
    outside = from_halo(cols, outer, fine, weights[0].get()[...])
    payload[:fine, :] = finish(lambda rows: before[rows, :] + outside(rows), nodes, receivers, cols[-1], edges.get(), weights, new_edges)
    payload[fine:, :] = tail[...]


def columns_kernel(own, senders, receivers, edges, first, *outs):
    *cols, before = outs
    fill_columns(own, senders.get()[...], receivers.get()[...], cols)
    before[...] = dot(edges.get()[...], first.get()[2 * LANES :, :])


def edge_kernel(edges, first, before):
    before[...] = dot(edges[...], first.get()[2 * LANES :, :])


def coarse_kernel(regions, halo, coarse, *refs):
    blocks, (before, *rest) = refs[:regions], refs[regions:]
    cols, (receivers, edges, *weights), (payload, new_edges) = rest[:3], rest[3:9], rest[9:]
    me = lax.axis_index("region")
    fine = blocks[0].shape[0] - TAIL
    at = row_layout(fine, coarse)
    tails = [tail_of(block, fine) for block in blocks]
    near = near_tails(tails, me, regions)
    codes = [me * coarse + lax.broadcasted_iota(I32, (coarse, LANES), 0)]
    for side, (other, there, tail) in enumerate(near):
        listed = tail[at["coarse"] : at["coarse"] + 1, :]
        first = halo * (1 - side)
        col = columns(listed)[first : first + halo]
        codes.append(jnp.where(there, other * coarse + col, -1))
    codes = jnp.concatenate(codes, axis=0)
    half = codes.shape[0] // 2
    parts = []
    for part in (codes[:half], codes[half:]):
        total, members = 0.0, 0.0
        for block, tail in zip(blocks, tails):
            f = fine // LANES
            parent = tail[at["dest"] : at["dest"] + f] * coarse + tail[at["target"] : at["target"] + f]
            more, counted = sums_and_counts(hot_codes(part, parent), block[:fine, :])
            total, members = total + more, members + counted
        parts.append((total / jnp.maximum(members, 1.0)).astype(BF16))
    table = jnp.concatenate(parts, axis=0)
    inner = from_table(cols, table, weights[0].get()[...])
    payload[:coarse, :] = finish(lambda rows: before[rows, :] + inner(rows), table[:coarse], receivers, None, edges.get(), weights, new_edges)
    own_tail = tails[0]
    c = coarse // LANES
    payload[coarse:, :] = jnp.concatenate(
        [own_tail[at["high"] : at["high"] + 2 * c], jnp.zeros((TAIL - 2 * c, LANES), I32)], axis=0
    ).astype(F32).astype(BF16)


def compact(first, ranks, codes, edges, size, at_once=8):
    place = lax.broadcasted_iota(I32, (size, LANES), 0) + first

    def body(g, carry):
        latents, found = carry
        rank = ranks[pl.ds(pl.multiple_of(g * at_once, at_once), at_once), :]
        code = codes[pl.ds(pl.multiple_of(g * at_once, at_once), at_once), :]
        for i in range(at_once):
            found = found + jnp.where(place == rank[i : i + 1], code[i : i + 1], 0)
        wide = at_once * LANES
        rows = edges[pl.ds(pl.multiple_of(g * wide, wide), wide), :]
        return latents + dot(hot_codes(place, rank), rows), found

    zero = jnp.zeros((size, LANES), F32), jnp.zeros((size, LANES), I32)
    latents, found = lax.fori_loop(0, ranks.shape[0] // at_once, body, zero)
    found = jnp.sum(found.astype(F32), axis=1, keepdims=True).astype(I32)
    return latents.astype(BF16), jnp.broadcast_to(found, (size, LANES))


def below(rows, same):
    square = (rows, rows)
    mask = same(lax.broadcasted_iota(I32, square, 0), lax.broadcasted_iota(I32, square, 1))
    return jnp.where(mask, 1.0, 0.0).astype(BF16)


def running(flags):
    upto = jnp.where(lax.broadcasted_iota(I32, (LANES, LANES), 0) <= lane_iota(LANES), 1.0, 0.0).astype(BF16)
    inside = dot(flags.astype(BF16), upto)
    return inside, jnp.broadcast_to(inside[:, LANES - 1 :], flags.shape)


def listed_kernel(regions, halo, fine, coarse, *refs):
    own, paired, crossed, senders, receivers, edges, parents, firsts, halo_rows, halo_blocks, ranks, codes = refs[:12]
    latents, send, recv, recv_rows = refs[12:]
    me = lax.axis_index("region")
    at = row_layout(fine, coarse)
    start = paired.shape[0] - TAIL
    lower, higher = lower_higher(paired[start:, :], crossed[start:, :])
    own_tail, lower_tail, higher_tail = (tail.astype(F32).astype(I32) for tail in (own[...], lower, higher))
    near = ((me - 1, me > 0, lower_tail), (me + 1, me < regions - 1, higher_tail))
    c = coarse // LANES
    wide, size = parents.shape[0], latents.shape[0]

    def own_parents(tail):
        return tail[at["high"] : at["high"] + c] * LANES + tail[at["low"] : at["low"] + c]

    cols = [columns(own_parents(own_tail))]
    for side, (other, there, tail) in enumerate(near):
        first = halo * (1 - side)
        col = columns(tail[at["coarse"] : at["coarse"] + 1])[first : first + halo]
        halo_rows[side * halo : (side + 1) * halo, :] = col
        halo_blocks[side * halo : (side + 1) * halo, :] = jnp.full(col.shape, jnp.where(there, jnp.bitwise_xor(me, other), -1))
        theirs = own_parents(tail).astype(F32)
        value = jnp.zeros((halo, LANES), F32)
        for i in range(c):
            value = value + jnp.where(col == lane_iota(halo, i * LANES), theirs[i : i + 1], 0.0)
        value = jnp.broadcast_to(jnp.sum(value, axis=1, keepdims=True), (halo, LANES)).astype(I32)
        cols.append(jnp.where(there, value, -1))
    cols.append(jnp.full((wide - coarse - 2 * halo, LANES), -1, I32))
    cols = jnp.concatenate(cols, axis=0)
    parents[...] = cols

    high_count = TOP // LANES
    rows = as_rows(cols)
    row_at = lax.broadcasted_iota(I32, (wide, LANES), 0)
    for i in range(wide // LANES):
        earlier = jnp.logical_and(cols == rows[i : i + 1], row_at < lane_iota(wide, i * LANES))
        seen = jnp.max(jnp.where(earlier, 1.0, 0.0), axis=0, keepdims=True)
        firsts[i : i + 1, :] = jnp.where(seen > 0.0, -2, rows[i : i + 1])
    tops = dot(
        hot_cols(jnp.right_shift(rows, 7), high_count), hot_rows(jnp.bitwise_and(cols, LANES - 1), LANES)
    )
    tops = jnp.minimum(tops, 1.0).astype(BF16)
    receivers = receivers.get()
    count = receivers.shape[0]
    high = lax.broadcasted_iota(I32, (high_count, LANES), 0)
    needed = []
    for i in range(0, count, 8):
        some = receivers[i : i + 8, :]
        match = dot(tops, hot_cols(jnp.bitwise_and(some, LANES - 1), LANES))
        for k in range(8):
            mine = jnp.where(high == jnp.right_shift(some[k : k + 1], 7), match[:, k * LANES : (k + 1) * LANES], 0.0)
            needed.append(jnp.sum(mine, axis=0, keepdims=True))
    needed = jnp.concatenate(needed, axis=0)

    group_of = lambda i: jnp.right_shift(i, GROUP.bit_length() - 1)
    inside, sums = running(needed)
    sums = sums.astype(BF16)
    local = dot(below(count, lambda i, j: jnp.logical_and(j < i, group_of(i) == group_of(j))), sums) + inside - 1.0
    in_group = dot(below(count, lambda i, j: group_of(i) == group_of(j)), sums)
    used = jnp.minimum(in_group, float(SLOTS))
    before = dot(below(count, lambda i, j: group_of(j) < group_of(i)), (used / GROUP).astype(BF16))
    placed = jnp.logical_and(local < SLOTS, local + before < size)
    others = jnp.where(placed, 0.0, needed)
    inside, sums = running(others)
    rank = dot(below(count, lambda i, j: j < i), sums.astype(BF16)) + inside - 1.0
    ranks[...] = jnp.where(others > 0.0, rank, -1.0).astype(I32)
    total = jnp.sum(jnp.sum(needed - others, axis=0, keepdims=True), axis=1, keepdims=True).astype(I32)
    codes[...] = senders.get()[...] * TOP + receivers[...]

    slot = jnp.where(needed > 0.0, local, -1.0).astype(I32)
    place = lax.broadcasted_iota(I32, (SLOTS, LANES), 0)
    edges = edges.get()
    lane = lane_iota(SLOTS)
    slots, targets = [], []
    for first in range(0, count, GROUP):
        code = jnp.zeros((SLOTS, LANES), F32)
        for i in range(first, first + GROUP):
            code = code + jnp.where(place == slot[i : i + 1], codes[i : i + 1, :].astype(F32), 0.0)
        code = jnp.broadcast_to(jnp.sum(code, axis=1, keepdims=True), (SLOTS, LANES)).astype(I32)
        parts = jnp.where(
            lane == 0,
            jnp.right_shift(code, 16),
            jnp.where(lane == 1, jnp.bitwise_and(jnp.right_shift(code, 8), 255), jnp.bitwise_and(code, 255)),
        )
        parts = jnp.where(lane < 3, parts, 0).astype(F32).astype(BF16)
        chosen = hot_cols(slot[first : first + GROUP], SLOTS)
        packed = dot(chosen, edges[first * LANES : (first + GROUP) * LANES, :]).astype(BF16)
        slots.append(jnp.concatenate([packed, parts], axis=1))
        target = before[first : first + 1] + lane_iota(1).astype(F32)
        targets.append(jnp.where(lane_iota(1).astype(F32) < used[first : first + 1], target, -1.0).astype(I32)[:, :SLOTS])
    per = LANES // SLOTS
    targets = [jnp.concatenate(targets[i : i + per], axis=1) for i in range(0, len(targets), per)]
    packed = dot(hot_cols(jnp.concatenate(targets, axis=0), size), jnp.concatenate(slots, axis=0))
    latents[...] = packed[:, :LANES].astype(BF16)
    parts = packed[:, LANES:]
    lane = lane_iota(size)
    code = jnp.where(lane == 0, parts * 65536.0, jnp.where(lane == 1, parts * 256.0, parts))
    code = jnp.broadcast_to(jnp.sum(code, axis=1, keepdims=True), (size, LANES)).astype(I32)
    send[...], recv[...] = ends(code, 0, total)
    recv_rows[...] = as_rows(recv[...])


def ends(code, first_place, total):
    place = lax.broadcasted_iota(I32, code.shape, 0) + first_place
    recv = jnp.where(place < total, jnp.bitwise_and(code, TOP - 1), -3)
    return jnp.right_shift(code, TOP.bit_length() - 1), recv


def parent_kernel(regions, halo, coarse, *refs):
    blocks, (table, parent_hots, parent_blocks) = refs[:regions], refs[regions:]
    me = lax.axis_index("region")
    fine = blocks[0].shape[0] - TAIL
    at = row_layout(fine, coarse)
    tails = [tail_of(block, fine) for block in blocks]
    f = fine // LANES

    def own_parents(tail):
        return tail[at["dest"] : at["dest"] + f] * coarse + tail[at["target"] : at["target"] + f]

    table[:fine, :] = blocks[0][:fine, :]
    owner = lambda tail: tail[at["dest"] : at["dest"] + f]
    parent_hots[:fine, :] = hot_rows(columns(tails[0][at["target"] : at["target"] + f]), coarse)
    parent_blocks[:fine, :] = jnp.bitwise_xor(columns(owner(tails[0])), me)
    for side, (other, there, tail) in enumerate(near_tails(tails, me, regions)):
        rows = slice(fine + side * halo, fine + (side + 1) * halo)
        first = halo * (1 - side)
        listed = tail[at["fine_high"] : at["fine_high"] + 1] * LANES + tail[at["fine_low"] : at["fine_low"] + 1]
        col = columns(listed)[first : first + halo]
        theirs = own_parents(tail).astype(F32)
        value = jnp.zeros((halo, LANES), F32)
        for i in range(f):
            value = value + jnp.where(col == lane_iota(halo, i * LANES), theirs[i : i + 1], 0.0)
        value = jnp.broadcast_to(jnp.sum(value, axis=1, keepdims=True), (halo, LANES)).astype(I32)
        parent_hots[rows, :] = hot_rows(jnp.bitwise_and(value, coarse - 1), coarse)
        block = jnp.bitwise_xor(jnp.right_shift(value, coarse.bit_length() - 1), me)
        parent_blocks[rows, :] = jnp.where(there, block, -1)
        total = jnp.zeros((halo, LANES), F32)
        for j, block in enumerate(blocks):
            here = jnp.logical_and(there, jnp.bitwise_xor(me, j) == other)
            total = total + dot(hot_rows(jnp.where(here, col, -1), fine), block[:fine, :])
        table[rows, :] = total.astype(BF16)


def sums_and_counts(chosen, rows):
    both = dot(chosen, jnp.concatenate([rows, jnp.ones(rows.shape, BF16)], axis=1))
    return both[:, :LANES], both[:, LANES:]


def add_blocks(cols, blocks, coarse, sums):
    c = coarse // LANES

    def add(block, sums):
        tail = tail_of(block, coarse)
        parent = tail[:c] * LANES + tail[c : 2 * c]
        more = [sums_and_counts(hot_codes(col, parent), block[:coarse, :]) for col in cols]
        return tuple((total + a, members + b) for (total, members), (a, b) in zip(sums, more))

    if isinstance(blocks, tuple):
        for block in blocks:
            sums = add(block, sums)
        return sums
    return lax.fori_loop(0, blocks.shape[0], lambda n, sums: add(blocks.at[n], sums), sums)


def nothing(cols):
    return tuple((jnp.zeros(col.shape, F32),) * 2 for col in cols)


def means(sums):
    return [(total / jnp.maximum(members, 1.0)).astype(BF16) for total, members in sums]


def half_kernel(coarse, *refs):
    blocks, (parents, send, *outs) = refs[:-6], refs[-6:]
    cols = [parents[...], send[...]]
    for i, value in enumerate(sum(add_blocks(cols, blocks, coarse, nothing(cols)), ())):
        outs[i][...] = value


def as_rows(col):
    return jnp.concatenate(
        [jnp.transpose(col[i : i + LANES])[:1] for i in range(0, col.shape[0], LANES)], axis=0
    )


def top_kernel(regions, halo, coarse, size, count, *refs):
    subs = lax.axis_size("sub")
    if count > 1:
        rows = coarse + TAIL
        there = tuple(refs[count - 1].at[i * rows : (i + 1) * rows] for i in range(count - 1))
        blocks = tuple((there if j % 2 else refs)[j // 2 * subs + k] for j in range(regions) for k in range(subs))
        begun = [ref[...] for ref in refs[count : count + 4]]
        begun, refs = ((begun[0], begun[1]), (begun[2], begun[3])), refs[count + 4 :]
    else:
        there = blocks = refs[0]
        begun, refs = None, refs[count:]
    parents, firsts, halo_rows, halo_blocks, ranks, codes, latents, send, recv, recv_rows, all_edges = refs[:11]
    edges, before3, *cols = refs[11:16]
    receivers, top_weights, weights = refs[16], refs[17:21], refs[21:25]
    out, agg, fallback, semaphore = refs[25:]
    me = lax.axis_index("region")
    own_sub = lambda j: blocks[j * subs] if count > 1 else blocks.at[j * subs]
    mine, firsts = parents[...], firsts[...]
    cols_here = [mine, send[...]]
    top_own, from_send = means(add_blocks(cols_here, there, coarse, nothing(cols_here) if begun is None else begun))
    first, second = top_weights[0].get()[...], centre(top_weights[1].get()[...])
    received = dot(top_own, first[LANES : 2 * LANES]).astype(BF16)
    others = jnp.concatenate([first[:LANES], first[2 * LANES :]], axis=0)

    def one(edge, from_send, recv, recv_rows):
        before = dot(jnp.concatenate([from_send, edge], axis=1), others) + dot(hot_codes(recv, firsts), received)
        new = (edge.astype(F32) + perceptron(before, second)).astype(BF16)
        return dot(hot_codes(mine, recv_rows), new)

    agg[...] = one(latents[...], from_send, recv[...], recv_rows[...])

    def more(b, carry):
        copy = pltpu.make_async_copy(all_edges, fallback, semaphore.at[0])
        copy.start()
        copy.wait()
        edge, code = compact(b * size, ranks, codes, fallback, size)
        send, recv = ends(code, b * size, left)
        (from_send,) = means(add_blocks([send], blocks, coarse, nothing([send])))
        agg[...] += one(edge, from_send, recv, as_rows(recv))
        return carry

    left = jnp.max(ranks[...]) + 1
    lax.fori_loop(0, (left + size - 1) // size, more, 0)
    top_final = node_update(top_own, agg[...], top_weights[2].get()[...], top_weights[3].get()[...])
    near = gather(halo_rows[...], halo_blocks[...], [own_sub(j)[:coarse, :] for j in range(regions)])
    down = jnp.concatenate([own_sub(0)[:coarse, :].astype(F32), near], axis=0)
    table = (down + top_final[: coarse + 2 * halo].astype(F32)).astype(BF16)
    inner = from_table(cols, table, weights[0].get()[...])
    out[...] = finish(lambda rows: before3[rows, :] + inner(rows), table[:coarse], receivers, None, edges, weights)


def last_kernel(regions, *refs):
    blocks, (down, parent_hots, parent_blocks, edges, before, *rest) = refs[:regions], refs[regions:]
    cols, receivers, weights, out = rest[:6], rest[6], rest[7:11], rest[11]
    own = out.shape[0]
    parent = pick(parent_hots[...], parent_blocks[...], [block[...] for block in blocks])
    table = (down[...].astype(F32) + parent).astype(BF16)
    first = weights[0].get()[...]
    inner, outside = from_own(cols, table[:own], first), from_halo(cols, table[own:], own, first)
    out[...] = finish(lambda rows: before[rows, :] + inner(rows) + outside(rows), table[:own], receivers, cols[-1], edges, weights)


class Here:
    def __init__(self, place):
        self.place = place

    def get(self):
        return self.place


class Arriving(Here):
    def __init__(self, source, place, semaphore):
        super().__init__(place)
        self.copy, self.waiting = pltpu.make_async_copy(source, place, semaphore), True
        self.copy.start()

    def get(self):
        if self.waiting:
            self.copy.wait()
            self.waiting = False
        return self.place


def call(kernel, args, outs, more=(), scratch=(), raw=(), cost=1, far=False, limit=LIMIT):
    specs = [pl.BlockSpec(memory_space=pltpu.HBM if i in raw else pltpu.VMEM) for i in range(len(args))]
    specs += [pl.BlockSpec(memory_space=pltpu.HBM if far else pltpu.VMEM)] * len(more)
    out_specs = [pl.BlockSpec(memory_space=pltpu.VMEM)] * len(outs)
    places = []
    if far:
        places = [pltpu.VMEM(array.shape, array.dtype) for array, _ in more]
        places.append(pltpu.SemaphoreType.DMA((len(more),)))
    n, k, o = len(args), len(more), len(outs)

    def body(*refs):
        given, sources, results, rest = refs[:n], refs[n : n + k], refs[n + k : n + k + o], refs[n + k + o :]
        if far:
            near, semaphores, rest = rest[:k], rest[k], rest[k + 1 :]
            operands = [Arriving(source, near[i], semaphores.at[i]) for i, source in enumerate(sources)]
        else:
            operands = [Here(ref if at is None else ref.at[at]) for ref, (_, at) in zip(sources, more)]
        kernel(*given, *operands, *results, *rest)

    return pl.pallas_call(
        body,
        out_shape=[jax.ShapeDtypeStruct(shape, dtype) for shape, dtype in outs],
        in_specs=specs,
        out_specs=out_specs,
        scratch_shapes=places + list(scratch),
        compiler_params=pltpu.CompilerParams(vmem_limit_bytes=limit),
        cost_estimate=pl.CostEstimate(flops=cost * 10**9, bytes_accessed=cost * 10**5, transcendentals=0),
    )(*args, *[array for array, _ in more])


def over_region(rows, beside=None):
    count = lax.axis_size("region")
    blocks = {0: rows}
    bit = count // 2
    while bit:
        going = dict(blocks)
        if beside is not None and len(going) > 1:
            far = max(going)
            going[far], beside = lax.optimization_barrier((going[far], beside))
        for j in blocks:
            going[j + bit] = lax.ppermute(going[j], "region", [(i, i ^ bit) for i in range(count)])
        blocks = going
        bit //= 2
    blocks = [blocks[j] for j in range(count)]
    return blocks if beside is None else (blocks, beside)


def over_both(rows, beside):
    regions, subs = lax.axis_size("region"), lax.axis_size("sub")
    swap = lambda array, axis, bits: lax.ppermute(array, axis, [(i, i ^ bits) for i in range(lax.axis_size(axis))])
    turns = [rows] + [swap(rows, "sub", k) for k in range(1, subs)]
    if regions * subs <= 16:
        turns[1], beside = lax.optimization_barrier((turns[1], beside))
        blocks = {0: turns}
        bit = regions // 2
        while bit > 1:
            for j in list(blocks):
                blocks[j + bit] = [swap(block, "region", bit) for block in blocks[j]]
            bit //= 2
        here = [block for j in range(0, regions, 2) for block in blocks[j]]
        return here + [swap(jnp.concatenate(here), "region", 1)], beside
    blocks, bit = jnp.stack(turns), 1
    while bit < regions:
        blocks, bit = jnp.concatenate([blocks, swap(blocks, "region", bit)]), 2 * bit
    return [blocks], beside


def on_device(
    node_feats,
    fine_senders,
    fine_receivers,
    fine_edges,
    halo_rows,
    coarse_senders,
    coarse_receivers,
    coarse_edges,
    coarse_halo_rows,
    pool_dest,
    pool_target,
    pool3_target,
    top_senders,
    top_receivers,
    top_edges,
    edge_in,
    edge_out,
    node_in,
    node_out,
):
    weights = (edge_in, edge_out, node_in, node_out)
    regions = lax.axis_size("region")
    fine, coarse = node_feats.shape[0], pool3_target.shape[0]
    halo, halo2 = halo_rows.shape[1], coarse_halo_rows.shape[1]
    rows = lambda a: a.reshape(-1, LANES)
    fine_send, fine_recv = rows(fine_senders), rows(fine_receivers)
    coarse_send, coarse_recv = rows(coarse_senders), rows(coarse_receivers)
    top_send, top_recv = rows(top_senders), rows(top_receivers)

    level = lambda index: [(matrix, index) for matrix in weights]
    plain = lambda *arrays: [(array, None) for array in arrays]

    to_pair, to_other, tail = call(
        functools.partial(pick_kernel, halo, halo2, fine, coarse),
        [],
        [((halo + TAIL, LANES), BF16)] * 2 + [((TAIL, LANES), BF16)],
        plain(node_feats, halo_rows, coarse_halo_rows, rows(pool_dest), rows(pool_target), rows(pool3_target)),
        scratch=[pltpu.VMEM((TAIL, LANES), I32)],
        far=True,
        limit=60 * 1024 * 1024,
    )
    pairs = lambda first: [(i, j) for low in range(first, regions - 1, 2) for i, j in ((low, low + 1), (low + 1, low))]
    paired = lax.ppermute(to_pair, "region", pairs(0))
    crossed = lax.ppermute(to_other, "region", pairs(1))
    one = lambda index: [(edge_in, index)]
    fine_cols, coarse_cols = edge_columns(fine, fine_edges.shape[0]), edge_columns(coarse, coarse_edges.shape[0])
    late_send, tail = lax.optimization_barrier((fine_send, tail))
    *fine_cols, before = call(
        ready_kernel,
        [],
        fine_cols + [(fine_edges.shape, F32)],
        plain(node_feats, late_send, fine_recv, fine_edges) + level(0),
        cost=2,
    )
    payload, fine_edges2 = call(
        functools.partial(fine_kernel, halo),
        [paired, crossed, tail, before, *fine_cols],
        [((fine + TAIL, LANES), BF16), (fine_edges.shape, BF16)],
        plain(node_feats, fine_recv, fine_edges) + level(0),
        cost=3,
    )
    wide = -(-(coarse + 2 * halo2) // LANES) * LANES
    size = min(384, top_edges.shape[0])
    listed_shapes = [
        ((wide, LANES), I32),
        ((wide // LANES, LANES), I32),
        ((2 * halo2, LANES), I32),
        ((2 * halo2, LANES), I32),
        (top_send.shape, I32),
        (top_send.shape, I32),
        ((size, LANES), BF16),
        ((size, LANES), I32),
        ((size, LANES), I32),
        ((size // LANES, LANES), I32),
    ]
    selected = call(
        functools.partial(listed_kernel, regions, halo2, fine, coarse),
        [tail, paired, crossed],
        listed_shapes,
        plain(top_send, top_recv, top_edges),
        cost=3,
    )
    payload, late_edges = lax.optimization_barrier((payload, coarse_edges))
    *coarse_cols, before = call(
        functools.partial(columns_kernel, coarse),
        [],
        coarse_cols + [(coarse_edges.shape, F32)],
        plain(coarse_send, coarse_recv, late_edges) + one(1),
    )
    blocks, selected = over_region(payload, selected)
    payload2, coarse_edges2 = call(
        functools.partial(coarse_kernel, regions, halo2, coarse),
        blocks + [before, *coarse_cols],
        [((coarse + TAIL, LANES), BF16), (coarse_edges.shape, BF16)],
        plain(coarse_recv, coarse_edges) + level(1),
        cost=3,
    )
    table_shape = (fine + 2 * halo, LANES)
    table = call(
        functools.partial(parent_kernel, regions, halo, coarse),
        blocks,
        [(table_shape, BF16), ((table_shape[0], coarse), BF16), (table_shape, I32)],
    )
    before = call(edge_kernel, [coarse_edges2], [(coarse_edges.shape, F32)], one(3))
    blocks2, (table, before) = over_both(payload2, (table, before))
    many = len(blocks2)
    begun = []
    if many > 1:
        begun = call(
            functools.partial(half_kernel, coarse),
            blocks2[:-1] + [selected[0], selected[7]],
            [((wide, LANES), F32)] * 2 + [((size, LANES), F32)] * 2,
        )
    (coarse_final,) = call(
        functools.partial(top_kernel, regions, halo2, coarse, size, many),
        blocks2 + [*begun, *selected, top_edges, coarse_edges2, *before, *coarse_cols],
        [((coarse, LANES), BF16)],
        plain(coarse_recv) + level(2) + level(3),
        scratch=[
            pltpu.VMEM((wide, LANES), F32),
            pltpu.VMEM(top_edges.shape, BF16),
            pltpu.SemaphoreType.DMA((1,)),
        ],
        raw=(many + len(begun) + len(selected),),
        cost=6,
    )
    before = call(edge_kernel, [fine_edges2], [(fine_edges.shape, F32)], one(4))
    blocks3, before = over_region(coarse_final, before)
    (fine_final,) = call(
        functools.partial(last_kernel, regions),
        blocks3 + [*table, fine_edges2, *before, *fine_cols],
        [((fine, LANES), BF16)],
        plain(fine_recv) + level(4),
        cost=3,
    )
    return fine_final


def solution(mesh):
    spread = ("parts", "region", "sub")
    rows, flat = P(spread, None), P(spread)
    in_specs = (
        (rows, flat, flat, rows, rows, flat, flat, rows, rows, rows, flat, flat)
        + (P("parts"), P("parts"), P("parts", None))
        + (P(),) * 4
    )
    return jax.shard_map(on_device, mesh=mesh, in_specs=in_specs, out_specs=rows, check_vma=False)
```

```python
import functools

import jax
import jax.numpy as jnp
from jax import lax
from jax.experimental import pallas as pl
from jax.experimental.pallas import tpu as pltpu
from jax.sharding import PartitionSpec as P

EPSILON = 1e-05
TOP = 2048
LANES = 128
F32, BF16, I32, I16 = jnp.float32, jnp.bfloat16, jnp.int32, jnp.int16
GROUP, SLOTS = 8, 64
STEP = 3072
CUT_BITS = 8
CUT = 1 << CUT_BITS
TAIL = 16
LIMIT = 32 * 1024 * 1024


def dot(a, b):
    return jnp.dot(a, b, preferred_element_type=F32)


def lane_iota(rows, first=0):
    return lax.broadcasted_iota(I32, (rows, LANES), 1) + first


def column(row):
    return jnp.transpose(jnp.broadcast_to(row, (LANES, row.shape[1])))


def columns(rows):
    return jnp.concatenate([column(rows[i : i + 1]) for i in range(rows.shape[0])], axis=0)


def hot(mask):
    return jnp.where(mask, jnp.ones(mask.shape, BF16), jnp.zeros(mask.shape, BF16))


def short(row, count):
    return jnp.concatenate([jnp.broadcast_to(row, (16, LANES)).astype(I16)] * (count // 16), axis=0)


def hot_rows(col, count, start=0):
    col = col.astype(I16)
    places = [lane_iota(16, first) for first in range(start, start + count, LANES)]
    return jnp.concatenate([hot(col == short(place[:1], col.shape[0])) for place in places], axis=1)


def hot_cols(rows, count):
    return hot_codes(lax.broadcasted_iota(I32, (count, LANES), 0), rows)


def hot_codes(col, rows):
    col = col.astype(I16)
    return jnp.concatenate([hot(col == short(rows[i : i + 1], col.shape[0])) for i in range(rows.shape[0])], axis=1)


def gather(row, block, blocks, all_there=False):
    return pick(hot_rows(row, blocks[0].shape[0]), block, blocks, all_there)


def pick(hots, block, blocks, all_there=False):
    wide = dot(hots, jnp.concatenate(blocks, axis=1))
    if block is None:
        return wide
    out = wide[:, :LANES] if all_there else jnp.zeros((hots.shape[0], LANES), F32)
    for i in range(1 if all_there else 0, len(blocks)):
        out = jnp.where(block == i, wide[:, i * LANES : (i + 1) * LANES], out)
    return out


def cut(table):
    short = -table.shape[0] % CUT
    if short:
        table = jnp.concatenate([table, jnp.zeros((short, LANES), BF16)], axis=0)
    return [table[i : i + CUT] for i in range(0, table.shape[0], CUT)]


def segment_sum(rows, block, values):
    chosen = hot_cols(jnp.bitwise_and(rows, CUT - 1), CUT)
    if block is None:
        return jnp.concatenate([dot(chosen[: CUT // 2], values), dot(chosen[CUT // 2 :], values)], axis=0)
    upper = values * block
    wide = jnp.concatenate([values - upper, upper], axis=1)
    out = jnp.concatenate([dot(chosen[: CUT // 2], wide), dot(chosen[CUT // 2 :], wide)], axis=0)
    return jnp.concatenate([out[:, :LANES], out[:, LANES:]], axis=0)


def centre(second):
    exact = second.astype(F32)
    return (exact - jnp.mean(exact, axis=1, keepdims=True)).astype(BF16)


def perceptron(before, centred_second):
    out = dot(jnp.maximum(before.astype(BF16), 0.0), centred_second)
    return out * lax.rsqrt(jnp.mean(out * out, axis=-1, keepdims=True) + EPSILON)


def node_update(nodes, summed, first, second):
    before = dot(nodes, first[:LANES]) + dot(summed.astype(BF16), first[LANES:])
    return (nodes.astype(F32) + perceptron(before, centre(second))).astype(BF16)


def project(blocks, matrix):
    return [dot(block, matrix).astype(BF16) for block in blocks]


def edge_columns(own, count):
    shape = (count, LANES)
    if own == 2 * CUT:
        return [(shape, I16), (shape, I16), (shape, I32), (shape, I16), (shape, I32), (shape, BF16)]
    return [(shape, I16), (shape, I32), (shape, I16)]


def fill_columns(own, senders, receivers, outs):
    send, recv = columns(senders), columns(receivers)
    low, high = jnp.bitwise_and(send, CUT - 1), jnp.right_shift(send, CUT_BITS)
    if own == 2 * CUT:
        low = jnp.where(send < own, low, -1)
        recv_high = jnp.right_shift(recv, CUT_BITS)
        values = [send, low, high, jnp.bitwise_and(recv, CUT - 1), recv_high, recv_high.astype(F32)]
    else:
        values = [low, high, recv]
    for value, out in zip(values, outs):
        out[...] = value.astype(out.dtype)


def from_own(cols, nodes, first):
    _, low, high, recv_low, recv_high, _ = cols
    blocks = cut(nodes)
    sent, received = project(blocks, first[:LANES]), project(blocks, first[LANES : 2 * LANES])
    return lambda rows: (
        gather(low[rows, :], high[rows, :], sent, True) + gather(recv_low[rows, :], recv_high[rows, :], received, True)
    )


def from_halo(cols, halo, own, first):
    sent = dot(halo, first[:LANES]).astype(BF16)
    return lambda rows: dot(hot_rows(cols[0][rows, :], LANES, own), sent)


def from_table(cols, table, first):
    low, high, recv = cols
    sent = project(cut(table), first[:LANES])
    received = project([table[:CUT]], first[LANES : 2 * LANES])
    return lambda rows: gather(low[rows, :], high[rows, :], sent, True) + gather(recv[rows, :], None, received)


def finish(before_at, nodes, receivers, block, edges, weights, new_edges=None, step=STEP):
    second = centre(weights[1].get()[...])
    receivers = receivers.get()
    summed = 0.0
    for at in range(0, edges.shape[0], step):
        rows = slice(at, min(at + step, edges.shape[0]))
        edge = edges[rows, :]
        new = (edge.astype(F32) + perceptron(before_at(rows), second)).astype(BF16)
        if new_edges is not None:
            new_edges[rows, :] = new
        recv = receivers[rows.start // LANES : rows.stop // LANES, :]
        summed = summed + segment_sum(recv, None if block is None else block[rows, :], new)
    return node_update(nodes, summed, weights[2].get()[...], weights[3].get()[...])


def tail_of(block, count):
    return block[count : count + TAIL, :].astype(F32).astype(I32)


def row_layout(fine, coarse):
    f, c = fine // LANES, coarse // LANES
    return {"dest": 0, "target": f, "high": 2 * f, "low": 2 * f + c, "coarse": 2 * f + 2 * c, "fine_high": 2 * f + 2 * c + 1, "fine_low": 2 * f + 2 * c + 2}


def near_tails(tails, me, count):
    out = []
    for other in (me - 1, me + 1):
        there = jnp.logical_and(other >= 0, other < count)
        near = jnp.where(there, jnp.bitwise_xor(me, other), 0)
        picked = sum(jnp.where(near == j, tail, 0) for j, tail in enumerate(tails))
        out.append((other, there, picked))
    return out


def pick_kernel(halo, coarse_halo, fine, coarse, nodes, rows, coarse_rows, dest, target, parent, paired, crossed, own_tail, lists):
    at = row_layout(fine, coarse)
    lists[...] = jnp.zeros_like(lists)
    listed, coarse_listed = rows.get()[...], coarse_rows.get()[...]
    for side in (0, 1):
        lists[at["coarse"] : at["coarse"] + 1, side * coarse_halo : (side + 1) * coarse_halo] = coarse_listed[side : side + 1]
        lanes = slice(side * halo, (side + 1) * halo)
        lists[at["fine_high"] : at["fine_high"] + 1, lanes] = jnp.right_shift(listed[side : side + 1], 7)
        lists[at["fine_low"] : at["fine_low"] + 1, lanes] = jnp.bitwise_and(listed[side : side + 1], LANES - 1)
    lists[at["dest"] : at["target"], :] = dest.get()[...]
    lists[at["target"] : at["high"], :] = target.get()[...]
    parents = parent.get()[...]
    lists[at["high"] : at["low"], :] = jnp.right_shift(parents, 7)
    lists[at["low"] : at["coarse"], :] = jnp.bitwise_and(parents, LANES - 1)
    tail = lists[...].astype(F32).astype(BF16)
    nodes = nodes.get()
    odd = jnp.bitwise_and(lax.axis_index("region"), 1)
    for out, up in ((paired, 1 - odd), (crossed, odd)):
        col = column(jnp.where(up == 1, listed[1:2], listed[0:1]))
        out[:halo, :] = dot(hot_rows(col, fine), nodes[...]).astype(BF16)
        out[halo:, :] = tail
    own_tail[...] = tail


def lower_higher(paired, crossed):
    odd = jnp.bitwise_and(lax.axis_index("region"), 1) == 1
    paired, crossed = paired.astype(F32), crossed.astype(F32)
    return jnp.where(odd, paired, crossed).astype(BF16), jnp.where(odd, crossed, paired).astype(BF16)


def ready_kernel(nodes, senders, receivers, edges, first, _1, _2, _3, *outs):
    *cols, before = outs
    nodes, first = nodes.get()[...], first.get()[...]
    fill_columns(nodes.shape[0], senders.get()[...], receivers.get()[...], cols)
    edges, inner = edges.get(), from_own(cols, nodes, first)
    for at in range(0, edges.shape[0], STEP):
        rows = slice(at, min(at + STEP, edges.shape[0]))
        before[rows, :] = dot(edges[rows, :], first[2 * LANES :]) + inner(rows)


def fine_kernel(halo, paired, crossed, tail, before, *refs):
    cols, (nodes, receivers, edges, *weights), (payload, new_edges) = refs[:6], refs[6:13], refs[13:]
    nodes = nodes.get()[...]
    fine = nodes.shape[0]
    outer = jnp.concatenate(lower_higher(paired[:halo, :], crossed[:halo, :]), axis=0)
    outside = from_halo(cols, outer, fine, weights[0].get()[...])
    payload[:fine, :] = finish(lambda rows: before[rows, :] + outside(rows), nodes, receivers, cols[-1], edges.get(), weights, new_edges)
    payload[fine:, :] = tail[...]


def columns_kernel(own, senders, receivers, edges, first, *outs):
    *cols, before = outs
    fill_columns(own, senders.get()[...], receivers.get()[...], cols)
    before[...] = dot(edges.get()[...], first.get()[2 * LANES :, :])


def edge_kernel(edges, first, before):
    before[...] = dot(edges[...], first.get()[2 * LANES :, :])


def coarse_kernel(regions, halo, coarse, *refs):
    blocks, (before, *rest) = refs[:regions], refs[regions:]
    cols, (receivers, edges, *weights), (payload, new_edges) = rest[:3], rest[3:9], rest[9:]
    me = lax.axis_index("region")
    fine = blocks[0].shape[0] - TAIL
    at = row_layout(fine, coarse)
    tails = [tail_of(block, fine) for block in blocks]
    near = near_tails(tails, me, regions)
    codes = [me * coarse + lax.broadcasted_iota(I32, (coarse, LANES), 0)]
    for side, (other, there, tail) in enumerate(near):
        listed = tail[at["coarse"] : at["coarse"] + 1, :]
        first = halo * (1 - side)
        col = columns(listed)[first : first + halo]
        codes.append(jnp.where(there, other * coarse + col, -1))
    codes = jnp.concatenate(codes, axis=0)
    half = codes.shape[0] // 2
    parts = []
    for part in (codes[:half], codes[half:]):
        total, members = 0.0, 0.0
        for block, tail in zip(blocks, tails):
            f = fine // LANES
            parent = tail[at["dest"] : at["dest"] + f] * coarse + tail[at["target"] : at["target"] + f]
            more, counted = sums_and_counts(hot_codes(part, parent), block[:fine, :])
            total, members = total + more, members + counted
        parts.append((total / jnp.maximum(members, 1.0)).astype(BF16))
    table = jnp.concatenate(parts, axis=0)
    inner = from_table(cols, table, weights[0].get()[...])
    payload[:coarse, :] = finish(lambda rows: before[rows, :] + inner(rows), table[:coarse], receivers, None, edges.get(), weights, new_edges)
    own_tail = tails[0]
    c = coarse // LANES
    payload[coarse:, :] = jnp.concatenate(
        [own_tail[at["high"] : at["high"] + 2 * c], jnp.zeros((TAIL - 2 * c, LANES), I32)], axis=0
    ).astype(F32).astype(BF16)


def compact(first, ranks, codes, edges, size, at_once=8):
    place = lax.broadcasted_iota(I32, (size, LANES), 0) + first

    def body(g, carry):
        latents, found = carry
        rank = ranks[pl.ds(pl.multiple_of(g * at_once, at_once), at_once), :]
        code = codes[pl.ds(pl.multiple_of(g * at_once, at_once), at_once), :]
        for i in range(at_once):
            found = found + jnp.where(place == rank[i : i + 1], code[i : i + 1], 0)
        wide = at_once * LANES
        rows = edges[pl.ds(pl.multiple_of(g * wide, wide), wide), :]
        return latents + dot(hot_codes(place, rank), rows), found

    zero = jnp.zeros((size, LANES), F32), jnp.zeros((size, LANES), I32)
    latents, found = lax.fori_loop(0, ranks.shape[0] // at_once, body, zero)
    found = jnp.sum(found.astype(F32), axis=1, keepdims=True).astype(I32)
    return latents.astype(BF16), jnp.broadcast_to(found, (size, LANES))


def below(rows, same):
    square = (rows, rows)
    mask = same(lax.broadcasted_iota(I32, square, 0), lax.broadcasted_iota(I32, square, 1))
    return jnp.where(mask, 1.0, 0.0).astype(BF16)


def running(flags):
    upto = jnp.where(lax.broadcasted_iota(I32, (LANES, LANES), 0) <= lane_iota(LANES), 1.0, 0.0).astype(BF16)
    inside = dot(flags.astype(BF16), upto)
    return inside, jnp.broadcast_to(inside[:, LANES - 1 :], flags.shape)


def listed_kernel(regions, halo, fine, coarse, *refs):
    own, paired, crossed, senders, receivers, edges, parents, firsts, halo_rows, halo_blocks, ranks, codes = refs[:12]
    latents, send, recv, recv_rows = refs[12:]
    me = lax.axis_index("region")
    at = row_layout(fine, coarse)
    start = paired.shape[0] - TAIL
    lower, higher = lower_higher(paired[start:, :], crossed[start:, :])
    own_tail, lower_tail, higher_tail = (tail.astype(F32).astype(I32) for tail in (own[...], lower, higher))
    near = ((me - 1, me > 0, lower_tail), (me + 1, me < regions - 1, higher_tail))
    c = coarse // LANES
    wide, size = parents.shape[0], latents.shape[0]

    def own_parents(tail):
        return tail[at["high"] : at["high"] + c] * LANES + tail[at["low"] : at["low"] + c]

    cols = [columns(own_parents(own_tail))]
    for side, (other, there, tail) in enumerate(near):
        first = halo * (1 - side)
        col = columns(tail[at["coarse"] : at["coarse"] + 1])[first : first + halo]
        halo_rows[side * halo : (side + 1) * halo, :] = col
        halo_blocks[side * halo : (side + 1) * halo, :] = jnp.full(col.shape, jnp.where(there, jnp.bitwise_xor(me, other), -1))
        theirs = own_parents(tail).astype(F32)
        value = jnp.zeros((halo, LANES), F32)
        for i in range(c):
            value = value + jnp.where(col == lane_iota(halo, i * LANES), theirs[i : i + 1], 0.0)
        value = jnp.broadcast_to(jnp.sum(value, axis=1, keepdims=True), (halo, LANES)).astype(I32)
        cols.append(jnp.where(there, value, -1))
    cols.append(jnp.full((wide - coarse - 2 * halo, LANES), -1, I32))
    cols = jnp.concatenate(cols, axis=0)
    parents[...] = cols

    high_count = TOP // LANES
    rows = as_rows(cols)
    row_at = lax.broadcasted_iota(I32, (wide, LANES), 0)
    for i in range(wide // LANES):
        earlier = jnp.logical_and(cols == rows[i : i + 1], row_at < lane_iota(wide, i * LANES))
        seen = jnp.max(jnp.where(earlier, 1.0, 0.0), axis=0, keepdims=True)
        firsts[i : i + 1, :] = jnp.where(seen > 0.0, -2, rows[i : i + 1])
    tops = dot(
        hot_cols(jnp.right_shift(rows, 7), high_count), hot_rows(jnp.bitwise_and(cols, LANES - 1), LANES)
    )
    tops = jnp.minimum(tops, 1.0).astype(BF16)
    receivers = receivers.get()
    count = receivers.shape[0]
    high = lax.broadcasted_iota(I32, (high_count, LANES), 0)
    needed = []
    for i in range(0, count, 8):
        some = receivers[i : i + 8, :]
        match = dot(tops, hot_cols(jnp.bitwise_and(some, LANES - 1), LANES))
        for k in range(8):
            mine = jnp.where(high == jnp.right_shift(some[k : k + 1], 7), match[:, k * LANES : (k + 1) * LANES], 0.0)
            needed.append(jnp.sum(mine, axis=0, keepdims=True))
    needed = jnp.concatenate(needed, axis=0)

    group_of = lambda i: jnp.right_shift(i, GROUP.bit_length() - 1)
    inside, sums = running(needed)
    sums = sums.astype(BF16)
    local = dot(below(count, lambda i, j: jnp.logical_and(j < i, group_of(i) == group_of(j))), sums) + inside - 1.0
    in_group = dot(below(count, lambda i, j: group_of(i) == group_of(j)), sums)
    used = jnp.minimum(in_group, float(SLOTS))
    before = dot(below(count, lambda i, j: group_of(j) < group_of(i)), (used / GROUP).astype(BF16))
    placed = jnp.logical_and(local < SLOTS, local + before < size)
    others = jnp.where(placed, 0.0, needed)
    inside, sums = running(others)
    rank = dot(below(count, lambda i, j: j < i), sums.astype(BF16)) + inside - 1.0
    ranks[...] = jnp.where(others > 0.0, rank, -1.0).astype(I32)
    total = jnp.sum(jnp.sum(needed - others, axis=0, keepdims=True), axis=1, keepdims=True).astype(I32)
    codes[...] = senders.get()[...] * TOP + receivers[...]

    slot = jnp.where(needed > 0.0, local, -1.0).astype(I32)
    place = lax.broadcasted_iota(I32, (SLOTS, LANES), 0)
    edges = edges.get()
    lane = lane_iota(SLOTS)
    slots, targets = [], []
    for first in range(0, count, GROUP):
        code = jnp.zeros((SLOTS, LANES), F32)
        for i in range(first, first + GROUP):
            code = code + jnp.where(place == slot[i : i + 1], codes[i : i + 1, :].astype(F32), 0.0)
        code = jnp.broadcast_to(jnp.sum(code, axis=1, keepdims=True), (SLOTS, LANES)).astype(I32)
        parts = jnp.where(
            lane == 0,
            jnp.right_shift(code, 16),
            jnp.where(lane == 1, jnp.bitwise_and(jnp.right_shift(code, 8), 255), jnp.bitwise_and(code, 255)),
        )
        parts = jnp.where(lane < 3, parts, 0).astype(F32).astype(BF16)
        chosen = hot_cols(slot[first : first + GROUP], SLOTS)
        packed = dot(chosen, edges[first * LANES : (first + GROUP) * LANES, :]).astype(BF16)
        slots.append(jnp.concatenate([packed, parts], axis=1))
        target = before[first : first + 1] + lane_iota(1).astype(F32)
        targets.append(jnp.where(lane_iota(1).astype(F32) < used[first : first + 1], target, -1.0).astype(I32)[:, :SLOTS])
    per = LANES // SLOTS
    targets = [jnp.concatenate(targets[i : i + per], axis=1) for i in range(0, len(targets), per)]
    packed = dot(hot_cols(jnp.concatenate(targets, axis=0), size), jnp.concatenate(slots, axis=0))
    latents[...] = packed[:, :LANES].astype(BF16)
    parts = packed[:, LANES:]
    lane = lane_iota(size)
    code = jnp.where(lane == 0, parts * 65536.0, jnp.where(lane == 1, parts * 256.0, parts))
    code = jnp.broadcast_to(jnp.sum(code, axis=1, keepdims=True), (size, LANES)).astype(I32)
    send[...], recv[...] = ends(code, 0, total)
    recv_rows[...] = as_rows(recv[...])


def ends(code, first_place, total):
    place = lax.broadcasted_iota(I32, code.shape, 0) + first_place
    recv = jnp.where(place < total, jnp.bitwise_and(code, TOP - 1), -3)
    return jnp.right_shift(code, TOP.bit_length() - 1), recv


def parent_kernel(regions, halo, coarse, *refs):
    blocks, (table, parent_hots, parent_blocks) = refs[:regions], refs[regions:]
    me = lax.axis_index("region")
    fine = blocks[0].shape[0] - TAIL
    at = row_layout(fine, coarse)
    tails = [tail_of(block, fine) for block in blocks]
    f = fine // LANES

    def own_parents(tail):
        return tail[at["dest"] : at["dest"] + f] * coarse + tail[at["target"] : at["target"] + f]

    table[:fine, :] = blocks[0][:fine, :]
    owner = lambda tail: tail[at["dest"] : at["dest"] + f]
    parent_hots[:fine, :] = hot_rows(columns(tails[0][at["target"] : at["target"] + f]), coarse)
    parent_blocks[:fine, :] = jnp.bitwise_xor(columns(owner(tails[0])), me)
    for side, (other, there, tail) in enumerate(near_tails(tails, me, regions)):
        rows = slice(fine + side * halo, fine + (side + 1) * halo)
        first = halo * (1 - side)
        listed = tail[at["fine_high"] : at["fine_high"] + 1] * LANES + tail[at["fine_low"] : at["fine_low"] + 1]
        col = columns(listed)[first : first + halo]
        theirs = own_parents(tail).astype(F32)
        value = jnp.zeros((halo, LANES), F32)
        for i in range(f):
            value = value + jnp.where(col == lane_iota(halo, i * LANES), theirs[i : i + 1], 0.0)
        value = jnp.broadcast_to(jnp.sum(value, axis=1, keepdims=True), (halo, LANES)).astype(I32)
        parent_hots[rows, :] = hot_rows(jnp.bitwise_and(value, coarse - 1), coarse)
        block = jnp.bitwise_xor(jnp.right_shift(value, coarse.bit_length() - 1), me)
        parent_blocks[rows, :] = jnp.where(there, block, -1)
        total = jnp.zeros((halo, LANES), F32)
        for j, block in enumerate(blocks):
            here = jnp.logical_and(there, jnp.bitwise_xor(me, j) == other)
            total = total + dot(hot_rows(jnp.where(here, col, -1), fine), block[:fine, :])
        table[rows, :] = total.astype(BF16)


def sums_and_counts(chosen, rows):
    both = dot(chosen, jnp.concatenate([rows, jnp.ones(rows.shape, BF16)], axis=1))
    return both[:, :LANES], both[:, LANES:]


def add_blocks(cols, blocks, coarse, sums):
    c = coarse // LANES

    def add(block, sums):
        tail = tail_of(block, coarse)
        parent = tail[:c] * LANES + tail[c : 2 * c]
        more = [sums_and_counts(hot_codes(col, parent), block[:coarse, :]) for col in cols]
        return tuple((total + a, members + b) for (total, members), (a, b) in zip(sums, more))

    if isinstance(blocks, tuple):
        for block in blocks:
            sums = add(block, sums)
        return sums
    return lax.fori_loop(0, blocks.shape[0], lambda n, sums: add(blocks.at[n], sums), sums)


def nothing(cols):
    return tuple((jnp.zeros(col.shape, F32),) * 2 for col in cols)


def means(sums):
    return [(total / jnp.maximum(members, 1.0)).astype(BF16) for total, members in sums]


def half_kernel(coarse, *refs):
    blocks, (parents, send, *outs) = refs[:-6], refs[-6:]
    cols = [parents[...], send[...]]
    for i, value in enumerate(sum(add_blocks(cols, blocks, coarse, nothing(cols)), ())):
        outs[i][...] = value


def as_rows(col):
    return jnp.concatenate(
        [jnp.transpose(col[i : i + LANES])[:1] for i in range(0, col.shape[0], LANES)], axis=0
    )


def top_kernel(regions, halo, coarse, size, count, *refs):
    subs = lax.axis_size("sub")
    if count > 1:
        rows = coarse + TAIL
        there = tuple(refs[count - 1].at[i * rows : (i + 1) * rows] for i in range(count - 1))
        blocks = tuple((there if j % 2 else refs)[j // 2 * subs + k] for j in range(regions) for k in range(subs))
        begun = [ref[...] for ref in refs[count : count + 4]]
        begun, refs = ((begun[0], begun[1]), (begun[2], begun[3])), refs[count + 4 :]
    else:
        there = blocks = refs[0]
        begun, refs = None, refs[count:]
    parents, firsts, halo_rows, halo_blocks, ranks, codes, latents, send, recv, recv_rows, all_edges = refs[:11]
    edges, before3, *cols = refs[11:16]
    receivers, top_weights, weights = refs[16], refs[17:21], refs[21:25]
    out, agg, fallback, semaphore = refs[25:]
    me = lax.axis_index("region")
    own_sub = lambda j: blocks[j * subs] if count > 1 else blocks.at[j * subs]
    mine, firsts = parents[...], firsts[...]
    cols_here = [mine, send[...]]
    top_own, from_send = means(add_blocks(cols_here, there, coarse, nothing(cols_here) if begun is None else begun))
    near = gather(halo_rows[...], halo_blocks[...], [own_sub(j)[:coarse, :] for j in range(regions)])
    down = jnp.concatenate([own_sub(0)[:coarse, :].astype(F32), near], axis=0)
    first, second = top_weights[0].get()[...], centre(top_weights[1].get()[...])
    received = dot(top_own, first[LANES : 2 * LANES]).astype(BF16)
    others = jnp.concatenate([first[:LANES], first[2 * LANES :]], axis=0)

    def one(edge, from_send, recv, recv_rows):
        before = dot(jnp.concatenate([from_send, edge], axis=1), others) + dot(hot_codes(recv, firsts), received)
        new = (edge.astype(F32) + perceptron(before, second)).astype(BF16)
        return dot(hot_codes(mine, recv_rows), new)

    agg[...] = one(latents[...], from_send, recv[...], recv_rows[...])

    def more(b, carry):
        copy = pltpu.make_async_copy(all_edges, fallback, semaphore.at[0])
        copy.start()
        copy.wait()
        edge, code = compact(b * LANES, ranks, codes, fallback, LANES)
        send, recv = ends(code, b * LANES, left)
        (from_send,) = means(add_blocks([send], blocks, coarse, nothing([send])))
        agg[...] += one(edge, from_send, recv, as_rows(recv))
        return carry

    left = jnp.max(ranks[...]) + 1
    lax.fori_loop(0, (left + LANES - 1) // LANES, more, 0)
    top_final = node_update(top_own, agg[...], top_weights[2].get()[...], top_weights[3].get()[...])
    table = (down + top_final[: coarse + 2 * halo].astype(F32)).astype(BF16)
    inner = from_table(cols, table, weights[0].get()[...])
    out[...] = finish(lambda rows: before3[rows, :] + inner(rows), table[:coarse], receivers, None, edges, weights)


def last_kernel(regions, *refs):
    blocks, (down, parent_hots, parent_blocks, edges, before, *rest) = refs[:regions], refs[regions:]
    cols, receivers, weights, out = rest[:6], rest[6], rest[7:11], rest[11]
    own = out.shape[0]
    parent = pick(parent_hots[...], parent_blocks[...], [block[...] for block in blocks])
    table = (down[...].astype(F32) + parent).astype(BF16)
    first = weights[0].get()[...]
    inner, outside = from_own(cols, table[:own], first), from_halo(cols, table[own:], own, first)
    out[...] = finish(lambda rows: before[rows, :] + inner(rows) + outside(rows), table[:own], receivers, cols[-1], edges, weights)


class Here:
    def __init__(self, place):
        self.place = place

    def get(self):
        return self.place


class Arriving(Here):
    def __init__(self, source, place, semaphore):
        super().__init__(place)
        self.copy, self.waiting = pltpu.make_async_copy(source, place, semaphore), True
        self.copy.start()

    def get(self):
        if self.waiting:
            self.copy.wait()
            self.waiting = False
        return self.place


def call(kernel, args, outs, more=(), scratch=(), raw=(), cost=1, far=False, limit=LIMIT):
    specs = [pl.BlockSpec(memory_space=pltpu.HBM if i in raw else pltpu.VMEM) for i in range(len(args))]
    specs += [pl.BlockSpec(memory_space=pltpu.HBM if far else pltpu.VMEM)] * len(more)
    out_specs = [pl.BlockSpec(memory_space=pltpu.VMEM)] * len(outs)
    places = []
    if far:
        places = [pltpu.VMEM(array.shape, array.dtype) for array, _ in more]
        places.append(pltpu.SemaphoreType.DMA((len(more),)))
    n, k, o = len(args), len(more), len(outs)

    def body(*refs):
        given, sources, results, rest = refs[:n], refs[n : n + k], refs[n + k : n + k + o], refs[n + k + o :]
        if far:
            near, semaphores, rest = rest[:k], rest[k], rest[k + 1 :]
            operands = [Arriving(source, near[i], semaphores.at[i]) for i, source in enumerate(sources)]
        else:
            operands = [Here(ref if at is None else ref.at[at]) for ref, (_, at) in zip(sources, more)]
        kernel(*given, *operands, *results, *rest)

    return pl.pallas_call(
        body,
        out_shape=[jax.ShapeDtypeStruct(shape, dtype) for shape, dtype in outs],
        in_specs=specs,
        out_specs=out_specs,
        scratch_shapes=places + list(scratch),
        compiler_params=pltpu.CompilerParams(vmem_limit_bytes=limit),
        cost_estimate=pl.CostEstimate(flops=cost * 10**9, bytes_accessed=cost * 10**5, transcendentals=0),
    )(*args, *[array for array, _ in more])


def over_region(rows, beside=None):
    count = lax.axis_size("region")
    blocks = {0: rows}
    bit = count // 2
    while bit:
        going = dict(blocks)
        if beside is not None and len(going) > 1:
            for j in (0, max(going)):
                going[j], beside = lax.optimization_barrier((going[j], beside))
        for j in blocks:
            going[j + bit] = lax.ppermute(going[j], "region", [(i, i ^ bit) for i in range(count)])
        blocks = going
        bit //= 2
    blocks = [blocks[j] for j in range(count)]
    return blocks if beside is None else (blocks, beside)


def over_both(rows, beside):
    regions, subs = lax.axis_size("region"), lax.axis_size("sub")
    swap = lambda array, axis, bits: lax.ppermute(array, axis, [(i, i ^ bits) for i in range(lax.axis_size(axis))])
    turns = [rows] + [swap(rows, "sub", k) for k in range(1, subs)]
    if regions * subs <= 16:
        turns[1], beside = lax.optimization_barrier((turns[1], beside))
        blocks = {0: turns}
        bit = regions // 2
        while bit > 1:
            for j in list(blocks):
                blocks[j + bit] = [swap(block, "region", bit) for block in blocks[j]]
            bit //= 2
        here = [block for j in range(0, regions, 2) for block in blocks[j]]
        return here + [swap(jnp.concatenate(here), "region", 1)], beside
    blocks, bit = jnp.stack(turns), 1
    while bit < regions:
        blocks, bit = jnp.concatenate([blocks, swap(blocks, "region", bit)]), 2 * bit
    return [blocks], beside


def on_device(
    node_feats,
    fine_senders,
    fine_receivers,
    fine_edges,
    halo_rows,
    coarse_senders,
    coarse_receivers,
    coarse_edges,
    coarse_halo_rows,
    pool_dest,
    pool_target,
    pool3_target,
    top_senders,
    top_receivers,
    top_edges,
    edge_in,
    edge_out,
    node_in,
    node_out,
):
    weights = (edge_in, edge_out, node_in, node_out)
    regions = lax.axis_size("region")
    fine, coarse = node_feats.shape[0], pool3_target.shape[0]
    halo, halo2 = halo_rows.shape[1], coarse_halo_rows.shape[1]
    rows = lambda a: a.reshape(-1, LANES)
    fine_send, fine_recv = rows(fine_senders), rows(fine_receivers)
    coarse_send, coarse_recv = rows(coarse_senders), rows(coarse_receivers)
    top_send, top_recv = rows(top_senders), rows(top_receivers)

    level = lambda index: [(matrix, index) for matrix in weights]
    plain = lambda *arrays: [(array, None) for array in arrays]

    to_pair, to_other, tail = call(
        functools.partial(pick_kernel, halo, halo2, fine, coarse),
        [],
        [((halo + TAIL, LANES), BF16)] * 2 + [((TAIL, LANES), BF16)],
        plain(node_feats, halo_rows, coarse_halo_rows, rows(pool_dest), rows(pool_target), rows(pool3_target)),
        scratch=[pltpu.VMEM((TAIL, LANES), I32)],
        far=True,
        limit=60 * 1024 * 1024,
    )
    pairs = lambda first: [(i, j) for low in range(first, regions - 1, 2) for i, j in ((low, low + 1), (low + 1, low))]
    paired = lax.ppermute(to_pair, "region", pairs(0))
    crossed = lax.ppermute(to_other, "region", pairs(1))
    one = lambda index: [(edge_in, index)]
    fine_cols, coarse_cols = edge_columns(fine, fine_edges.shape[0]), edge_columns(coarse, coarse_edges.shape[0])
    late_send, tail = lax.optimization_barrier((fine_send, tail))
    *fine_cols, before = call(
        ready_kernel,
        [],
        fine_cols + [(fine_edges.shape, F32)],
        plain(node_feats, late_send, fine_recv, fine_edges) + level(0),
        cost=2,
    )
    payload, fine_edges2 = call(
        functools.partial(fine_kernel, halo),
        [paired, crossed, tail, before, *fine_cols],
        [((fine + TAIL, LANES), BF16), (fine_edges.shape, BF16)],
        plain(node_feats, fine_recv, fine_edges) + level(0),
        cost=3,
    )
    wide = -(-(coarse + 2 * halo2) // LANES) * LANES
    size = min(384, top_edges.shape[0])
    listed_shapes = [
        ((wide, LANES), I32),
        ((wide // LANES, LANES), I32),
        ((2 * halo2, LANES), I32),
        ((2 * halo2, LANES), I32),
        (top_send.shape, I32),
        (top_send.shape, I32),
        ((size, LANES), BF16),
        ((size, LANES), I32),
        ((size, LANES), I32),
        ((size // LANES, LANES), I32),
    ]
    selected = call(
        functools.partial(listed_kernel, regions, halo2, fine, coarse),
        [tail, paired, crossed],
        listed_shapes,
        plain(top_send, top_recv, top_edges),
        cost=3,
    )
    payload, late_edges = lax.optimization_barrier((payload, coarse_edges))
    *coarse_cols, before = call(
        functools.partial(columns_kernel, coarse),
        [],
        coarse_cols + [(coarse_edges.shape, F32)],
        plain(coarse_send, coarse_recv, late_edges) + one(1),
    )
    blocks, selected = over_region(payload, selected)
    payload2, coarse_edges2 = call(
        functools.partial(coarse_kernel, regions, halo2, coarse),
        blocks + [before, *coarse_cols],
        [((coarse + TAIL, LANES), BF16), (coarse_edges.shape, BF16)],
        plain(coarse_recv, coarse_edges) + level(1),
        cost=3,
    )
    table_shape = (fine + 2 * halo, LANES)
    table = call(
        functools.partial(parent_kernel, regions, halo, coarse),
        blocks,
        [(table_shape, BF16), ((table_shape[0], coarse), BF16), (table_shape, I32)],
    )
    before = call(edge_kernel, [coarse_edges2], [(coarse_edges.shape, F32)], one(3))
    blocks2, (table, before) = over_both(payload2, (table, before))
    many = len(blocks2)
    begun = []
    if many > 1:
        begun = call(
            functools.partial(half_kernel, coarse),
            blocks2[:-1] + [selected[0], selected[7]],
            [((wide, LANES), F32)] * 2 + [((size, LANES), F32)] * 2,
        )
    (coarse_final,) = call(
        functools.partial(top_kernel, regions, halo2, coarse, size, many),
        blocks2 + [*begun, *selected, top_edges, coarse_edges2, *before, *coarse_cols],
        [((coarse, LANES), BF16)],
        plain(coarse_recv) + level(2) + level(3),
        scratch=[
            pltpu.VMEM((wide, LANES), F32),
            pltpu.VMEM(top_edges.shape, BF16),
            pltpu.SemaphoreType.DMA((1,)),
        ],
        raw=(many + len(begun) + len(selected),),
        cost=6,
    )
    before = call(edge_kernel, [fine_edges2], [(fine_edges.shape, F32)], one(4))
    blocks3, before = over_region(coarse_final, before)
    (fine_final,) = call(
        functools.partial(last_kernel, regions),
        blocks3 + [*table, fine_edges2, *before, *fine_cols],
        [((fine, LANES), BF16)],
        plain(fine_recv) + level(4),
        cost=3,
    )
    return fine_final


def solution(mesh):
    spread = ("parts", "region", "sub")
    rows, flat = P(spread, None), P(spread)
    in_specs = (
        (rows, flat, flat, rows, rows, flat, flat, rows, rows, rows, flat, flat)
        + (P("parts"), P("parts"), P("parts", None))
        + (P(),) * 4
    )
    return jax.shard_map(on_device, mesh=mesh, in_specs=in_specs, out_specs=rows, check_vma=False)
```

```python
import functools

import jax
import jax.numpy as jnp
from jax import lax
from jax.experimental import pallas as pl
from jax.experimental.pallas import tpu as pltpu
from jax.sharding import PartitionSpec as P

EPSILON = 1e-05
TOP = 2048
LANES = 128
F32, BF16, I32, I16 = jnp.float32, jnp.bfloat16, jnp.int32, jnp.int16
GROUP, SLOTS = 8, 64
STEP = 3072
CUT_BITS = 8
CUT = 1 << CUT_BITS
TAIL = 16
LIMIT = 32 * 1024 * 1024


def dot(a, b):
    return jnp.dot(a, b, preferred_element_type=F32)


def lane_iota(rows, first=0):
    return lax.broadcasted_iota(I32, (rows, LANES), 1) + first


def column(row):
    return jnp.transpose(jnp.broadcast_to(row, (LANES, row.shape[1])))


def columns(rows):
    return jnp.concatenate([column(rows[i : i + 1]) for i in range(rows.shape[0])], axis=0)


def hot(mask):
    return jnp.where(mask, jnp.ones(mask.shape, BF16), jnp.zeros(mask.shape, BF16))


def short(row, count):
    return jnp.concatenate([jnp.broadcast_to(row, (16, LANES)).astype(I16)] * (count // 16), axis=0)


def hot_rows(col, count, start=0):
    col = col.astype(I16)
    places = [lane_iota(16, first) for first in range(start, start + count, LANES)]
    return jnp.concatenate([hot(col == short(place[:1], col.shape[0])) for place in places], axis=1)


def hot_cols(rows, count):
    return hot_codes(lax.broadcasted_iota(I32, (count, LANES), 0), rows)


def hot_codes(col, rows):
    col = col.astype(I16)
    return jnp.concatenate([hot(col == short(rows[i : i + 1], col.shape[0])) for i in range(rows.shape[0])], axis=1)


def gather(row, block, blocks, all_there=False):
    return pick(hot_rows(row, blocks[0].shape[0]), block, blocks, all_there)


def pick(hots, block, blocks, all_there=False):
    wide = dot(hots, jnp.concatenate(blocks, axis=1))
    if block is None:
        return wide
    out = wide[:, :LANES] if all_there else jnp.zeros((hots.shape[0], LANES), F32)
    for i in range(1 if all_there else 0, len(blocks)):
        out = jnp.where(block == i, wide[:, i * LANES : (i + 1) * LANES], out)
    return out


def cut(table):
    short = -table.shape[0] % CUT
    if short:
        table = jnp.concatenate([table, jnp.zeros((short, LANES), BF16)], axis=0)
    return [table[i : i + CUT] for i in range(0, table.shape[0], CUT)]


def segment_sum(rows, block, values):
    chosen = hot_cols(jnp.bitwise_and(rows, CUT - 1), CUT)
    if block is None:
        return jnp.concatenate([dot(chosen[: CUT // 2], values), dot(chosen[CUT // 2 :], values)], axis=0)
    upper = values * block
    wide = jnp.concatenate([values - upper, upper], axis=1)
    out = jnp.concatenate([dot(chosen[: CUT // 2], wide), dot(chosen[CUT // 2 :], wide)], axis=0)
    return jnp.concatenate([out[:, :LANES], out[:, LANES:]], axis=0)


def centre(second):
    exact = second.astype(F32)
    return (exact - jnp.mean(exact, axis=1, keepdims=True)).astype(BF16)


def perceptron(before, centred_second):
    out = dot(jnp.maximum(before.astype(BF16), 0.0), centred_second)
    return out * lax.rsqrt(jnp.mean(out * out, axis=-1, keepdims=True) + EPSILON)


def node_update(nodes, summed, first, second):
    before = dot(nodes, first[:LANES]) + dot(summed.astype(BF16), first[LANES:])
    return (nodes.astype(F32) + perceptron(before, centre(second))).astype(BF16)


def project(blocks, matrix):
    return [dot(block, matrix).astype(BF16) for block in blocks]


def edge_columns(own, count):
    shape = (count, LANES)
    if own == 2 * CUT:
        return [(shape, I32), (shape, I32), (shape, I32), (shape, I32), (shape, I32), (shape, BF16)]
    return [(shape, I32), (shape, I32), (shape, I32)]


def fill_columns(own, senders, receivers, outs):
    send, recv = columns(senders), columns(receivers)
    low, high = jnp.bitwise_and(send, CUT - 1), jnp.right_shift(send, CUT_BITS)
    if own == 2 * CUT:
        low = jnp.where(send < own, low, -1)
        recv_high = jnp.right_shift(recv, CUT_BITS)
        values = [send, low, high, jnp.bitwise_and(recv, CUT - 1), recv_high, recv_high.astype(F32)]
    else:
        values = [low, high, recv]
    for value, out in zip(values, outs):
        out[...] = value.astype(out.dtype)


def from_own(cols, nodes, first):
    _, low, high, recv_low, recv_high, _ = cols
    blocks = cut(nodes)
    sent, received = project(blocks, first[:LANES]), project(blocks, first[LANES : 2 * LANES])
    return lambda rows: (
        gather(low[rows, :], high[rows, :], sent, True) + gather(recv_low[rows, :], recv_high[rows, :], received, True)
    )


def from_halo(cols, halo, own, first):
    sent = dot(halo, first[:LANES]).astype(BF16)
    return lambda rows: dot(hot_rows(cols[0][rows, :], LANES, own), sent)


def from_table(cols, table, first):
    low, high, recv = cols
    sent = project(cut(table), first[:LANES])
    received = project([table[:CUT]], first[LANES : 2 * LANES])
    return lambda rows: gather(low[rows, :], high[rows, :], sent, True) + gather(recv[rows, :], None, received)


def finish(before_at, nodes, receivers, block, edges, weights, new_edges=None, step=STEP):
    second = centre(weights[1].get()[...])
    receivers = receivers.get()
    summed = 0.0
    for at in range(0, edges.shape[0], step):
        rows = slice(at, min(at + step, edges.shape[0]))
        edge = edges[rows, :]
        new = (edge.astype(F32) + perceptron(before_at(rows), second)).astype(BF16)
        if new_edges is not None:
            new_edges[rows, :] = new
        recv = receivers[rows.start // LANES : rows.stop // LANES, :]
        summed = summed + segment_sum(recv, None if block is None else block[rows, :], new)
    return node_update(nodes, summed, weights[2].get()[...], weights[3].get()[...])


def tail_of(block, count):
    return block[count : count + TAIL, :].astype(F32).astype(I32)


def row_layout(fine, coarse):
    f, c = fine // LANES, coarse // LANES
    return {"dest": 0, "target": f, "high": 2 * f, "low": 2 * f + c, "coarse": 2 * f + 2 * c, "fine_high": 2 * f + 2 * c + 1, "fine_low": 2 * f + 2 * c + 2}


def near_tails(tails, me, count):
    out = []
    for other in (me - 1, me + 1):
        there = jnp.logical_and(other >= 0, other < count)
        near = jnp.where(there, jnp.bitwise_xor(me, other), 0)
        picked = sum(jnp.where(near == j, tail, 0) for j, tail in enumerate(tails))
        out.append((other, there, picked))
    return out


def pick_kernel(halo, coarse_halo, fine, coarse, nodes, rows, coarse_rows, dest, target, parent, paired, crossed, own_tail, lists):
    at = row_layout(fine, coarse)
    lists[...] = jnp.zeros_like(lists)
    listed, coarse_listed = rows.get()[...], coarse_rows.get()[...]
    for side in (0, 1):
        lists[at["coarse"] : at["coarse"] + 1, side * coarse_halo : (side + 1) * coarse_halo] = coarse_listed[side : side + 1]
        lanes = slice(side * halo, (side + 1) * halo)
        lists[at["fine_high"] : at["fine_high"] + 1, lanes] = jnp.right_shift(listed[side : side + 1], 7)
        lists[at["fine_low"] : at["fine_low"] + 1, lanes] = jnp.bitwise_and(listed[side : side + 1], LANES - 1)
    lists[at["dest"] : at["target"], :] = dest.get()[...]
    lists[at["target"] : at["high"], :] = target.get()[...]
    parents = parent.get()[...]
    lists[at["high"] : at["low"], :] = jnp.right_shift(parents, 7)
    lists[at["low"] : at["coarse"], :] = jnp.bitwise_and(parents, LANES - 1)
    tail = lists[...].astype(F32).astype(BF16)
    nodes = nodes.get()
    odd = jnp.bitwise_and(lax.axis_index("region"), 1)
    for out, up in ((paired, 1 - odd), (crossed, odd)):
        col = column(jnp.where(up == 1, listed[1:2], listed[0:1]))
        out[:halo, :] = dot(hot_rows(col, fine), nodes[...]).astype(BF16)
        out[halo:, :] = tail
    own_tail[...] = tail


def lower_higher(paired, crossed):
    odd = jnp.bitwise_and(lax.axis_index("region"), 1) == 1
    paired, crossed = paired.astype(F32), crossed.astype(F32)
    return jnp.where(odd, paired, crossed).astype(BF16), jnp.where(odd, crossed, paired).astype(BF16)


def ready_kernel(nodes, senders, receivers, edges, first, _1, _2, _3, *outs):
    *cols, before = outs
    nodes, first = nodes.get()[...], first.get()[...]
    fill_columns(nodes.shape[0], senders.get()[...], receivers.get()[...], cols)
    edges, inner = edges.get(), from_own(cols, nodes, first)
    for at in range(0, edges.shape[0], STEP):
        rows = slice(at, min(at + STEP, edges.shape[0]))
        before[rows, :] = dot(edges[rows, :], first[2 * LANES :]) + inner(rows)


def fine_kernel(halo, paired, crossed, tail, before, *refs):
    cols, (nodes, receivers, edges, *weights), (payload, new_edges) = refs[:6], refs[6:13], refs[13:]
    nodes = nodes.get()[...]
    fine = nodes.shape[0]
    outer = jnp.concatenate(lower_higher(paired[:halo, :], crossed[:halo, :]), axis=0)
    outside = from_halo(cols, outer, fine, weights[0].get()[...])
    payload[:fine, :] = finish(lambda rows: before[rows, :] + outside(rows), nodes, receivers, cols[-1], edges.get(), weights, new_edges)
    payload[fine:, :] = tail[...]


def columns_kernel(own, senders, receivers, edges, first, *outs):
    *cols, before = outs
    fill_columns(own, senders.get()[...], receivers.get()[...], cols)
    before[...] = dot(edges.get()[...], first.get()[2 * LANES :, :])


def edge_kernel(edges, first, before):
    before[...] = dot(edges[...], first.get()[2 * LANES :, :])


def coarse_kernel(regions, halo, coarse, *refs):
    blocks, (before, *rest) = refs[:regions], refs[regions:]
    cols, (receivers, edges, *weights), (payload, new_edges) = rest[:3], rest[3:9], rest[9:]
    me = lax.axis_index("region")
    fine = blocks[0].shape[0] - TAIL
    at = row_layout(fine, coarse)
    tails = [tail_of(block, fine) for block in blocks]
    near = near_tails(tails, me, regions)
    codes = [me * coarse + lax.broadcasted_iota(I32, (coarse, LANES), 0)]
    for side, (other, there, tail) in enumerate(near):
        listed = tail[at["coarse"] : at["coarse"] + 1, :]
        first = halo * (1 - side)
        col = columns(listed)[first : first + halo]
        codes.append(jnp.where(there, other * coarse + col, -1))
    codes = jnp.concatenate(codes, axis=0)
    half = codes.shape[0] // 2
    parts = []
    for part in (codes[:half], codes[half:]):
        total, members = 0.0, 0.0
        for block, tail in zip(blocks, tails):
            f = fine // LANES
            parent = tail[at["dest"] : at["dest"] + f] * coarse + tail[at["target"] : at["target"] + f]
            more, counted = sums_and_counts(hot_codes(part, parent), block[:fine, :])
            total, members = total + more, members + counted
        parts.append((total / jnp.maximum(members, 1.0)).astype(BF16))
    table = jnp.concatenate(parts, axis=0)
    inner = from_table(cols, table, weights[0].get()[...])
    payload[:coarse, :] = finish(lambda rows: before[rows, :] + inner(rows), table[:coarse], receivers, None, edges.get(), weights, new_edges)
    own_tail = tails[0]
    c = coarse // LANES
    payload[coarse:, :] = jnp.concatenate(
        [own_tail[at["high"] : at["high"] + 2 * c], jnp.zeros((TAIL - 2 * c, LANES), I32)], axis=0
    ).astype(F32).astype(BF16)


def compact(first, ranks, codes, edges, size, at_once=8):
    place = lax.broadcasted_iota(I32, (size, LANES), 0) + first

    def body(g, carry):
        latents, found = carry
        rank = ranks[pl.ds(pl.multiple_of(g * at_once, at_once), at_once), :]
        code = codes[pl.ds(pl.multiple_of(g * at_once, at_once), at_once), :]
        for i in range(at_once):
            found = found + jnp.where(place == rank[i : i + 1], code[i : i + 1], 0)
        wide = at_once * LANES
        rows = edges[pl.ds(pl.multiple_of(g * wide, wide), wide), :]
        return latents + dot(hot_codes(place, rank), rows), found

    zero = jnp.zeros((size, LANES), F32), jnp.zeros((size, LANES), I32)
    latents, found = lax.fori_loop(0, ranks.shape[0] // at_once, body, zero)
    found = jnp.sum(found.astype(F32), axis=1, keepdims=True).astype(I32)
    return latents.astype(BF16), jnp.broadcast_to(found, (size, LANES))


def below(rows, same):
    square = (rows, rows)
    mask = same(lax.broadcasted_iota(I32, square, 0), lax.broadcasted_iota(I32, square, 1))
    return jnp.where(mask, 1.0, 0.0).astype(BF16)


def running(flags):
    upto = jnp.where(lax.broadcasted_iota(I32, (LANES, LANES), 0) <= lane_iota(LANES), 1.0, 0.0).astype(BF16)
    inside = dot(flags.astype(BF16), upto)
    return inside, jnp.broadcast_to(inside[:, LANES - 1 :], flags.shape)


def listed_kernel(regions, halo, fine, coarse, *refs):
    own, paired, crossed, senders, receivers, edges, parents, firsts, halo_rows, halo_blocks, ranks, codes = refs[:12]
    latents, send, recv, recv_rows = refs[12:]
    me = lax.axis_index("region")
    at = row_layout(fine, coarse)
    start = paired.shape[0] - TAIL
    lower, higher = lower_higher(paired[start:, :], crossed[start:, :])
    own_tail, lower_tail, higher_tail = (tail.astype(F32).astype(I32) for tail in (own[...], lower, higher))
    near = ((me - 1, me > 0, lower_tail), (me + 1, me < regions - 1, higher_tail))
    c = coarse // LANES
    wide, size = parents.shape[0], latents.shape[0]

    def own_parents(tail):
        return tail[at["high"] : at["high"] + c] * LANES + tail[at["low"] : at["low"] + c]

    cols = [columns(own_parents(own_tail))]
    for side, (other, there, tail) in enumerate(near):
        first = halo * (1 - side)
        col = columns(tail[at["coarse"] : at["coarse"] + 1])[first : first + halo]
        halo_rows[side * halo : (side + 1) * halo, :] = col
        halo_blocks[side * halo : (side + 1) * halo, :] = jnp.full(col.shape, jnp.where(there, jnp.bitwise_xor(me, other), -1))
        theirs = own_parents(tail).astype(F32)
        value = jnp.zeros((halo, LANES), F32)
        for i in range(c):
            value = value + jnp.where(col == lane_iota(halo, i * LANES), theirs[i : i + 1], 0.0)
        value = jnp.broadcast_to(jnp.sum(value, axis=1, keepdims=True), (halo, LANES)).astype(I32)
        cols.append(jnp.where(there, value, -1))
    cols.append(jnp.full((wide - coarse - 2 * halo, LANES), -1, I32))
    cols = jnp.concatenate(cols, axis=0)
    parents[...] = cols

    high_count = TOP // LANES
    rows = as_rows(cols)
    row_at = lax.broadcasted_iota(I32, (wide, LANES), 0)
    for i in range(wide // LANES):
        earlier = jnp.logical_and(cols == rows[i : i + 1], row_at < lane_iota(wide, i * LANES))
        seen = jnp.max(jnp.where(earlier, 1.0, 0.0), axis=0, keepdims=True)
        firsts[i : i + 1, :] = jnp.where(seen > 0.0, -2, rows[i : i + 1])
    tops = dot(
        hot_cols(jnp.right_shift(rows, 7), high_count), hot_rows(jnp.bitwise_and(cols, LANES - 1), LANES)
    )
    tops = jnp.minimum(tops, 1.0).astype(BF16)
    receivers = receivers.get()
    count = receivers.shape[0]
    high = lax.broadcasted_iota(I32, (high_count, LANES), 0)
    needed = []
    for i in range(0, count, 8):
        some = receivers[i : i + 8, :]
        match = dot(tops, hot_cols(jnp.bitwise_and(some, LANES - 1), LANES))
        for k in range(8):
            mine = jnp.where(high == jnp.right_shift(some[k : k + 1], 7), match[:, k * LANES : (k + 1) * LANES], 0.0)
            needed.append(jnp.sum(mine, axis=0, keepdims=True))
    needed = jnp.concatenate(needed, axis=0)

    group_of = lambda i: jnp.right_shift(i, GROUP.bit_length() - 1)
    inside, sums = running(needed)
    sums = sums.astype(BF16)
    local = dot(below(count, lambda i, j: jnp.logical_and(j < i, group_of(i) == group_of(j))), sums) + inside - 1.0
    in_group = dot(below(count, lambda i, j: group_of(i) == group_of(j)), sums)
    used = jnp.minimum(in_group, float(SLOTS))
    before = dot(below(count, lambda i, j: group_of(j) < group_of(i)), (used / GROUP).astype(BF16))
    placed = jnp.logical_and(local < SLOTS, local + before < size)
    others = jnp.where(placed, 0.0, needed)
    inside, sums = running(others)
    rank = dot(below(count, lambda i, j: j < i), sums.astype(BF16)) + inside - 1.0
    ranks[...] = jnp.where(others > 0.0, rank, -1.0).astype(I32)
    total = jnp.sum(jnp.sum(needed - others, axis=0, keepdims=True), axis=1, keepdims=True).astype(I32)
    codes[...] = senders.get()[...] * TOP + receivers[...]

    slot = jnp.where(needed > 0.0, local, -1.0).astype(I32)
    place = lax.broadcasted_iota(I32, (SLOTS, LANES), 0)
    edges = edges.get()
    lane = lane_iota(SLOTS)
    slots, targets = [], []
    for first in range(0, count, GROUP):
        code = jnp.zeros((SLOTS, LANES), F32)
        for i in range(first, first + GROUP):
            code = code + jnp.where(place == slot[i : i + 1], codes[i : i + 1, :].astype(F32), 0.0)
        code = jnp.broadcast_to(jnp.sum(code, axis=1, keepdims=True), (SLOTS, LANES)).astype(I32)
        parts = jnp.where(
            lane == 0,
            jnp.right_shift(code, 16),
            jnp.where(lane == 1, jnp.bitwise_and(jnp.right_shift(code, 8), 255), jnp.bitwise_and(code, 255)),
        )
        parts = jnp.where(lane < 3, parts, 0).astype(F32).astype(BF16)
        chosen = hot_cols(slot[first : first + GROUP], SLOTS)
        packed = dot(chosen, edges[first * LANES : (first + GROUP) * LANES, :]).astype(BF16)
        slots.append(jnp.concatenate([packed, parts], axis=1))
        target = before[first : first + 1] + lane_iota(1).astype(F32)
        targets.append(jnp.where(lane_iota(1).astype(F32) < used[first : first + 1], target, -1.0).astype(I32)[:, :SLOTS])
    per = LANES // SLOTS
    targets = [jnp.concatenate(targets[i : i + per], axis=1) for i in range(0, len(targets), per)]
    packed = dot(hot_cols(jnp.concatenate(targets, axis=0), size), jnp.concatenate(slots, axis=0))
    latents[...] = packed[:, :LANES].astype(BF16)
    parts = packed[:, LANES:]
    lane = lane_iota(size)
    code = jnp.where(lane == 0, parts * 65536.0, jnp.where(lane == 1, parts * 256.0, parts))
    code = jnp.broadcast_to(jnp.sum(code, axis=1, keepdims=True), (size, LANES)).astype(I32)
    send[...], recv[...] = ends(code, 0, total)
    recv_rows[...] = as_rows(recv[...])


def ends(code, first_place, total):
    place = lax.broadcasted_iota(I32, code.shape, 0) + first_place
    recv = jnp.where(place < total, jnp.bitwise_and(code, TOP - 1), -3)
    return jnp.right_shift(code, TOP.bit_length() - 1), recv


def parent_kernel(regions, halo, coarse, *refs):
    blocks, (table, parent_hots, parent_blocks) = refs[:regions], refs[regions:]
    me = lax.axis_index("region")
    fine = blocks[0].shape[0] - TAIL
    at = row_layout(fine, coarse)
    tails = [tail_of(block, fine) for block in blocks]
    f = fine // LANES

    def own_parents(tail):
        return tail[at["dest"] : at["dest"] + f] * coarse + tail[at["target"] : at["target"] + f]

    table[:fine, :] = blocks[0][:fine, :]
    owner = lambda tail: tail[at["dest"] : at["dest"] + f]
    parent_hots[:fine, :] = hot_rows(columns(tails[0][at["target"] : at["target"] + f]), coarse)
    parent_blocks[:fine, :] = jnp.bitwise_xor(columns(owner(tails[0])), me)
    for side, (other, there, tail) in enumerate(near_tails(tails, me, regions)):
        rows = slice(fine + side * halo, fine + (side + 1) * halo)
        first = halo * (1 - side)
        listed = tail[at["fine_high"] : at["fine_high"] + 1] * LANES + tail[at["fine_low"] : at["fine_low"] + 1]
        col = columns(listed)[first : first + halo]
        theirs = own_parents(tail).astype(F32)
        value = jnp.zeros((halo, LANES), F32)
        for i in range(f):
            value = value + jnp.where(col == lane_iota(halo, i * LANES), theirs[i : i + 1], 0.0)
        value = jnp.broadcast_to(jnp.sum(value, axis=1, keepdims=True), (halo, LANES)).astype(I32)
        parent_hots[rows, :] = hot_rows(jnp.bitwise_and(value, coarse - 1), coarse)
        block = jnp.bitwise_xor(jnp.right_shift(value, coarse.bit_length() - 1), me)
        parent_blocks[rows, :] = jnp.where(there, block, -1)
        total = jnp.zeros((halo, LANES), F32)
        for j, block in enumerate(blocks):
            here = jnp.logical_and(there, jnp.bitwise_xor(me, j) == other)
            total = total + dot(hot_rows(jnp.where(here, col, -1), fine), block[:fine, :])
        table[rows, :] = total.astype(BF16)


def sums_and_counts(chosen, rows):
    both = dot(chosen, jnp.concatenate([rows, jnp.ones(rows.shape, BF16)], axis=1))
    return both[:, :LANES], both[:, LANES:]


def add_blocks(cols, blocks, coarse, sums):
    c = coarse // LANES

    def add(block, sums):
        tail = tail_of(block, coarse)
        parent = tail[:c] * LANES + tail[c : 2 * c]
        more = [sums_and_counts(hot_codes(col, parent), block[:coarse, :]) for col in cols]
        return tuple((total + a, members + b) for (total, members), (a, b) in zip(sums, more))

    if isinstance(blocks, tuple):
        for block in blocks:
            sums = add(block, sums)
        return sums
    return lax.fori_loop(0, blocks.shape[0], lambda n, sums: add(blocks.at[n], sums), sums)


def nothing(cols):
    return tuple((jnp.zeros(col.shape, F32),) * 2 for col in cols)


def means(sums):
    return [(total / jnp.maximum(members, 1.0)).astype(BF16) for total, members in sums]


def half_kernel(coarse, *refs):
    blocks, (parents, send, *outs) = refs[:-6], refs[-6:]
    cols = [parents[...], send[...]]
    for i, value in enumerate(sum(add_blocks(cols, blocks, coarse, nothing(cols)), ())):
        outs[i][...] = value


def as_rows(col):
    return jnp.concatenate(
        [jnp.transpose(col[i : i + LANES])[:1] for i in range(0, col.shape[0], LANES)], axis=0
    )


def top_kernel(regions, halo, coarse, size, count, *refs):
    subs = lax.axis_size("sub")
    if count > 1:
        rows = coarse + TAIL
        stacks = refs[count - regions // 2 : count]
        there = tuple(stack.at[i * rows : (i + 1) * rows] for stack in stacks for i in range(subs))
        blocks = tuple((there if j % 2 else refs)[j // 2 * subs + k] for j in range(regions) for k in range(subs))
        begun = [ref[...] for ref in refs[count : count + 4]]
        begun, refs = ((begun[0], begun[1]), (begun[2], begun[3])), refs[count + 4 :]
    else:
        there = blocks = refs[0]
        begun, refs = None, refs[count:]
    parents, firsts, halo_rows, halo_blocks, ranks, codes, latents, send, recv, recv_rows, all_edges = refs[:11]
    edges, before3, *cols = refs[11:16]
    receivers, top_weights, weights = refs[16], refs[17:21], refs[21:25]
    out, agg, fallback, semaphore = refs[25:]
    me = lax.axis_index("region")
    own_sub = lambda j: blocks[j * subs] if count > 1 else blocks.at[j * subs]
    mine, firsts = parents[...], firsts[...]
    cols_here = [mine, send[...]]
    top_own, from_send = means(add_blocks(cols_here, there, coarse, nothing(cols_here) if begun is None else begun))
    near = gather(halo_rows[...], halo_blocks[...], [own_sub(j)[:coarse, :] for j in range(regions)])
    down = jnp.concatenate([own_sub(0)[:coarse, :].astype(F32), near], axis=0)
    first, second = top_weights[0].get()[...], centre(top_weights[1].get()[...])
    received = dot(top_own, first[LANES : 2 * LANES]).astype(BF16)
    others = jnp.concatenate([first[:LANES], first[2 * LANES :]], axis=0)

    def one(edge, from_send, recv, recv_rows):
        before = dot(jnp.concatenate([from_send, edge], axis=1), others) + dot(hot_codes(recv, firsts), received)
        new = (edge.astype(F32) + perceptron(before, second)).astype(BF16)
        return dot(hot_codes(mine, recv_rows), new)

    agg[...] = one(latents[...], from_send, recv[...], recv_rows[...])

    def more(b, carry):
        copy = pltpu.make_async_copy(all_edges, fallback, semaphore.at[0])
        copy.start()
        copy.wait()
        edge, code = compact(b * LANES, ranks, codes, fallback, LANES)
        send, recv = ends(code, b * LANES, left)
        (from_send,) = means(add_blocks([send], blocks, coarse, nothing([send])))
        agg[...] += one(edge, from_send, recv, as_rows(recv))
        return carry

    left = jnp.max(ranks[...]) + 1
    lax.fori_loop(0, (left + LANES - 1) // LANES, more, 0)
    top_final = node_update(top_own, agg[...], top_weights[2].get()[...], top_weights[3].get()[...])
    table = (down + top_final[: coarse + 2 * halo].astype(F32)).astype(BF16)
    inner = from_table(cols, table, weights[0].get()[...])
    out[...] = finish(lambda rows: before3[rows, :] + inner(rows), table[:coarse], receivers, None, edges, weights)


def last_kernel(regions, *refs):
    blocks, (down, parent_hots, parent_blocks, edges, before, *rest) = refs[:regions], refs[regions:]
    cols, receivers, weights, out = rest[:6], rest[6], rest[7:11], rest[11]
    own = out.shape[0]
    parent = pick(parent_hots[...], parent_blocks[...], [block[...] for block in blocks])
    table = (down[...].astype(F32) + parent).astype(BF16)
    first = weights[0].get()[...]
    inner, outside = from_own(cols, table[:own], first), from_halo(cols, table[own:], own, first)
    out[...] = finish(lambda rows: before[rows, :] + inner(rows) + outside(rows), table[:own], receivers, cols[-1], edges, weights)


class Here:
    def __init__(self, place):
        self.place = place

    def get(self):
        return self.place


class Arriving(Here):
    def __init__(self, source, place, semaphore):
        super().__init__(place)
        self.copy, self.waiting = pltpu.make_async_copy(source, place, semaphore), True
        self.copy.start()

    def get(self):
        if self.waiting:
            self.copy.wait()
            self.waiting = False
        return self.place


def call(kernel, args, outs, more=(), scratch=(), raw=(), cost=1, far=False, limit=LIMIT):
    specs = [pl.BlockSpec(memory_space=pltpu.HBM if i in raw else pltpu.VMEM) for i in range(len(args))]
    specs += [pl.BlockSpec(memory_space=pltpu.HBM if far else pltpu.VMEM)] * len(more)
    out_specs = [pl.BlockSpec(memory_space=pltpu.VMEM)] * len(outs)
    places = []
    if far:
        places = [pltpu.VMEM(array.shape, array.dtype) for array, _ in more]
        places.append(pltpu.SemaphoreType.DMA((len(more),)))
    n, k, o = len(args), len(more), len(outs)

    def body(*refs):
        given, sources, results, rest = refs[:n], refs[n : n + k], refs[n + k : n + k + o], refs[n + k + o :]
        if far:
            near, semaphores, rest = rest[:k], rest[k], rest[k + 1 :]
            operands = [Arriving(source, near[i], semaphores.at[i]) for i, source in enumerate(sources)]
        else:
            operands = [Here(ref if at is None else ref.at[at]) for ref, (_, at) in zip(sources, more)]
        kernel(*given, *operands, *results, *rest)

    return pl.pallas_call(
        body,
        out_shape=[jax.ShapeDtypeStruct(shape, dtype) for shape, dtype in outs],
        in_specs=specs,
        out_specs=out_specs,
        scratch_shapes=places + list(scratch),
        compiler_params=pltpu.CompilerParams(vmem_limit_bytes=limit),
        cost_estimate=pl.CostEstimate(flops=cost * 10**9, bytes_accessed=cost * 10**5, transcendentals=0),
    )(*args, *[array for array, _ in more])


def over_region(rows, beside=None):
    count = lax.axis_size("region")
    blocks = {0: rows}
    bit = count // 2
    while bit:
        going = dict(blocks)
        if beside is not None and len(going) > 1:
            for j in (0, max(going)):
                going[j], beside = lax.optimization_barrier((going[j], beside))
        for j in blocks:
            going[j + bit] = lax.ppermute(going[j], "region", [(i, i ^ bit) for i in range(count)])
        blocks = going
        bit //= 2
    blocks = [blocks[j] for j in range(count)]
    return blocks if beside is None else (blocks, beside)


def over_both(rows, beside):
    regions, subs = lax.axis_size("region"), lax.axis_size("sub")
    swap = lambda array, axis, bits: lax.ppermute(array, axis, [(i, i ^ bits) for i in range(lax.axis_size(axis))])
    turns = [rows] + [swap(rows, "sub", k) for k in range(1, subs)]
    if regions * subs <= 16:
        turns[1], beside = lax.optimization_barrier((turns[1], beside))
        blocks = {0: turns}
        bit = regions // 2
        while bit > 1:
            for j in list(blocks):
                blocks[j + bit] = [swap(block, "region", bit) for block in blocks[j]]
            bit //= 2
        here = [block for j in range(0, regions, 2) for block in blocks[j]]
        return here + [swap(jnp.concatenate(blocks[j]), "region", 1) for j in range(0, regions, 2)], beside
    blocks, bit = jnp.stack(turns), 1
    while bit < regions:
        blocks, bit = jnp.concatenate([blocks, swap(blocks, "region", bit)]), 2 * bit
    return [blocks], beside


def on_device(
    node_feats,
    fine_senders,
    fine_receivers,
    fine_edges,
    halo_rows,
    coarse_senders,
    coarse_receivers,
    coarse_edges,
    coarse_halo_rows,
    pool_dest,
    pool_target,
    pool3_target,
    top_senders,
    top_receivers,
    top_edges,
    edge_in,
    edge_out,
    node_in,
    node_out,
):
    weights = (edge_in, edge_out, node_in, node_out)
    regions = lax.axis_size("region")
    fine, coarse = node_feats.shape[0], pool3_target.shape[0]
    halo, halo2 = halo_rows.shape[1], coarse_halo_rows.shape[1]
    rows = lambda a: a.reshape(-1, LANES)
    fine_send, fine_recv = rows(fine_senders), rows(fine_receivers)
    coarse_send, coarse_recv = rows(coarse_senders), rows(coarse_receivers)
    top_send, top_recv = rows(top_senders), rows(top_receivers)

    level = lambda index: [(matrix, index) for matrix in weights]
    plain = lambda *arrays: [(array, None) for array in arrays]

    to_pair, to_other, tail = call(
        functools.partial(pick_kernel, halo, halo2, fine, coarse),
        [],
        [((halo + TAIL, LANES), BF16)] * 2 + [((TAIL, LANES), BF16)],
        plain(node_feats, halo_rows, coarse_halo_rows, rows(pool_dest), rows(pool_target), rows(pool3_target)),
        scratch=[pltpu.VMEM((TAIL, LANES), I32)],
        far=True,
        limit=60 * 1024 * 1024,
    )
    pairs = lambda first: [(i, j) for low in range(first, regions - 1, 2) for i, j in ((low, low + 1), (low + 1, low))]
    paired = lax.ppermute(to_pair, "region", pairs(0))
    crossed = lax.ppermute(to_other, "region", pairs(1))
    one = lambda index: [(edge_in, index)]
    fine_cols, coarse_cols = edge_columns(fine, fine_edges.shape[0]), edge_columns(coarse, coarse_edges.shape[0])
    late_send, tail = lax.optimization_barrier((fine_send, tail))
    *fine_cols, before = call(
        ready_kernel,
        [],
        fine_cols + [(fine_edges.shape, F32)],
        plain(node_feats, late_send, fine_recv, fine_edges) + level(0),
        cost=2,
    )
    payload, fine_edges2 = call(
        functools.partial(fine_kernel, halo),
        [paired, crossed, tail, before, *fine_cols],
        [((fine + TAIL, LANES), BF16), (fine_edges.shape, BF16)],
        plain(node_feats, fine_recv, fine_edges) + level(0),
        cost=3,
    )
    wide = -(-(coarse + 2 * halo2) // LANES) * LANES
    size = min(384, top_edges.shape[0])
    listed_shapes = [
        ((wide, LANES), I32),
        ((wide // LANES, LANES), I32),
        ((2 * halo2, LANES), I32),
        ((2 * halo2, LANES), I32),
        (top_send.shape, I32),
        (top_send.shape, I32),
        ((size, LANES), BF16),
        ((size, LANES), I32),
        ((size, LANES), I32),
        ((size // LANES, LANES), I32),
    ]
    selected = call(
        functools.partial(listed_kernel, regions, halo2, fine, coarse),
        [tail, paired, crossed],
        listed_shapes,
        plain(top_send, top_recv, top_edges),
        cost=3,
    )
    payload, late_edges = lax.optimization_barrier((payload, coarse_edges))
    *coarse_cols, before = call(
        functools.partial(columns_kernel, coarse),
        [],
        coarse_cols + [(coarse_edges.shape, F32)],
        plain(coarse_send, coarse_recv, late_edges) + one(1),
    )
    blocks, selected = over_region(payload, selected)
    payload2, coarse_edges2 = call(
        functools.partial(coarse_kernel, regions, halo2, coarse),
        blocks + [before, *coarse_cols],
        [((coarse + TAIL, LANES), BF16), (coarse_edges.shape, BF16)],
        plain(coarse_recv, coarse_edges) + level(1),
        cost=3,
    )
    table_shape = (fine + 2 * halo, LANES)
    table = call(
        functools.partial(parent_kernel, regions, halo, coarse),
        blocks,
        [(table_shape, BF16), ((table_shape[0], coarse), BF16), (table_shape, I32)],
    )
    before = call(edge_kernel, [coarse_edges2], [(coarse_edges.shape, F32)], one(3))
    blocks2, (table, before) = over_both(payload2, (table, before))
    many = len(blocks2)
    begun = []
    if many > 1:
        begun = call(
            functools.partial(half_kernel, coarse),
            blocks2[: -(regions // 2)] + [selected[0], selected[7]],
            [((wide, LANES), F32)] * 2 + [((size, LANES), F32)] * 2,
        )
    (coarse_final,) = call(
        functools.partial(top_kernel, regions, halo2, coarse, size, many),
        blocks2 + [*begun, *selected, top_edges, coarse_edges2, *before, *coarse_cols],
        [((coarse, LANES), BF16)],
        plain(coarse_recv) + level(2) + level(3),
        scratch=[
            pltpu.VMEM((wide, LANES), F32),
            pltpu.VMEM(top_edges.shape, BF16),
            pltpu.SemaphoreType.DMA((1,)),
        ],
        raw=(many + len(begun) + len(selected),),
        cost=6,
    )
    before = call(edge_kernel, [fine_edges2], [(fine_edges.shape, F32)], one(4))
    blocks3, before = over_region(coarse_final, before)
    (fine_final,) = call(
        functools.partial(last_kernel, regions),
        blocks3 + [*table, fine_edges2, *before, *fine_cols],
        [((fine, LANES), BF16)],
        plain(fine_recv) + level(4),
        cost=3,
    )
    return fine_final


def solution(mesh):
    spread = ("parts", "region", "sub")
    rows, flat = P(spread, None), P(spread)
    in_specs = (
        (rows, flat, flat, rows, rows, flat, flat, rows, rows, rows, flat, flat)
        + (P("parts"), P("parts"), P("parts", None))
        + (P(),) * 4
    )
    return jax.shard_map(on_device, mesh=mesh, in_specs=in_specs, out_specs=rows, check_vma=False)
```

```python
import functools

import jax
import jax.numpy as jnp
from jax import lax
from jax.experimental import pallas as pl
from jax.experimental.pallas import tpu as pltpu
from jax.sharding import PartitionSpec as P

EPSILON = 1e-05
TOP = 2048
LANES = 128
F32, BF16, I32, I16 = jnp.float32, jnp.bfloat16, jnp.int32, jnp.int16
GROUP, SLOTS = 8, 64
STEP = 3072
CUT_BITS = 8
CUT = 1 << CUT_BITS
TAIL = 16
LIMIT = 32 * 1024 * 1024


def dot(a, b):
    return jnp.dot(a, b, preferred_element_type=F32)


def lane_iota(rows, first=0):
    return lax.broadcasted_iota(I32, (rows, LANES), 1) + first


def column(row):
    return jnp.transpose(jnp.broadcast_to(row, (LANES, row.shape[1])))


def columns(rows):
    return jnp.concatenate([column(rows[i : i + 1]) for i in range(rows.shape[0])], axis=0)


def hot(mask):
    return jnp.where(mask, jnp.ones(mask.shape, BF16), jnp.zeros(mask.shape, BF16))


def short(row, count):
    return jnp.concatenate([jnp.broadcast_to(row, (16, LANES)).astype(I16)] * (count // 16), axis=0)


def hot_rows(col, count, start=0):
    col = col.astype(I16)
    places = [lane_iota(16, first) for first in range(start, start + count, LANES)]
    return jnp.concatenate([hot(col == short(place[:1], col.shape[0])) for place in places], axis=1)


def hot_cols(rows, count):
    return hot_codes(lax.broadcasted_iota(I32, (count, LANES), 0), rows)


def hot_codes(col, rows):
    col = col.astype(I16)
    return jnp.concatenate([hot(col == short(rows[i : i + 1], col.shape[0])) for i in range(rows.shape[0])], axis=1)


def gather(row, block, blocks, all_there=False):
    return pick(hot_rows(row, blocks[0].shape[0]), block, blocks, all_there)


def pick(hots, block, blocks, all_there=False):
    wide = dot(hots, jnp.concatenate(blocks, axis=1))
    if block is None:
        return wide
    out = wide[:, :LANES] if all_there else jnp.zeros((hots.shape[0], LANES), F32)
    for i in range(1 if all_there else 0, len(blocks)):
        out = jnp.where(block == i, wide[:, i * LANES : (i + 1) * LANES], out)
    return out


def cut(table):
    short = -table.shape[0] % CUT
    if short:
        table = jnp.concatenate([table, jnp.zeros((short, LANES), BF16)], axis=0)
    return [table[i : i + CUT] for i in range(0, table.shape[0], CUT)]


def segment_sum(rows, block, values):
    chosen = hot_cols(jnp.bitwise_and(rows, CUT - 1), CUT)
    if block is None:
        return jnp.concatenate([dot(chosen[: CUT // 2], values), dot(chosen[CUT // 2 :], values)], axis=0)
    upper = values * block
    wide = jnp.concatenate([values - upper, upper], axis=1)
    out = jnp.concatenate([dot(chosen[: CUT // 2], wide), dot(chosen[CUT // 2 :], wide)], axis=0)
    return jnp.concatenate([out[:, :LANES], out[:, LANES:]], axis=0)


def centre(second):
    exact = second.astype(F32)
    return (exact - jnp.mean(exact, axis=1, keepdims=True)).astype(BF16)


def perceptron(before, centred_second):
    out = dot(jnp.maximum(before.astype(BF16), 0.0), centred_second)
    return out * lax.rsqrt(jnp.mean(out * out, axis=-1, keepdims=True) + EPSILON)


def node_update(nodes, summed, first, second):
    before = dot(nodes, first[:LANES]) + dot(summed.astype(BF16), first[LANES:])
    return (nodes.astype(F32) + perceptron(before, centre(second))).astype(BF16)


def project(blocks, matrix):
    return [dot(block, matrix).astype(BF16) for block in blocks]


def edge_columns(own, count):
    shape = (count, LANES)
    if own == 2 * CUT:
        return [(shape, I32), (shape, I32), (shape, I32), (shape, I32), (shape, I32), (shape, BF16)]
    return [(shape, I32), (shape, I32), (shape, I32)]


def fill_columns(own, senders, receivers, outs):
    send, recv = columns(senders), columns(receivers)
    low, high = jnp.bitwise_and(send, CUT - 1), jnp.right_shift(send, CUT_BITS)
    if own == 2 * CUT:
        low = jnp.where(send < own, low, -1)
        recv_high = jnp.right_shift(recv, CUT_BITS)
        values = [send, low, high, jnp.bitwise_and(recv, CUT - 1), recv_high, recv_high.astype(F32)]
    else:
        values = [low, high, recv]
    for value, out in zip(values, outs):
        out[...] = value.astype(out.dtype)


def from_own(cols, nodes, first):
    _, low, high, recv_low, recv_high, _ = cols
    blocks = cut(nodes)
    sent, received = project(blocks, first[:LANES]), project(blocks, first[LANES : 2 * LANES])
    return lambda rows: (
        gather(low[rows, :], high[rows, :], sent, True) + gather(recv_low[rows, :], recv_high[rows, :], received, True)
    )


def from_halo(cols, halo, own, first):
    sent = dot(halo, first[:LANES]).astype(BF16)
    return lambda rows: dot(hot_rows(cols[0][rows, :], LANES, own), sent)


def from_table(cols, table, first):
    low, high, recv = cols
    sent = project(cut(table), first[:LANES])
    received = project([table[:CUT]], first[LANES : 2 * LANES])
    return lambda rows: gather(low[rows, :], high[rows, :], sent, True) + gather(recv[rows, :], None, received)


def finish(before_at, nodes, receivers, block, edges, weights, new_edges=None, step=STEP):
    second = centre(weights[1].get()[...])
    receivers = receivers.get()
    summed = 0.0
    for at in range(0, edges.shape[0], step):
        rows = slice(at, min(at + step, edges.shape[0]))
        edge = edges[rows, :]
        new = (edge.astype(F32) + perceptron(before_at(rows), second)).astype(BF16)
        if new_edges is not None:
            new_edges[rows, :] = new
        recv = receivers[rows.start // LANES : rows.stop // LANES, :]
        summed = summed + segment_sum(recv, None if block is None else block[rows, :], new)
    return node_update(nodes, summed, weights[2].get()[...], weights[3].get()[...])


def tail_of(block, count):
    return block[count : count + TAIL, :].astype(F32).astype(I32)


def row_layout(fine, coarse):
    f, c = fine // LANES, coarse // LANES
    return {"dest": 0, "target": f, "high": 2 * f, "low": 2 * f + c, "coarse": 2 * f + 2 * c, "fine_high": 2 * f + 2 * c + 1, "fine_low": 2 * f + 2 * c + 2}


def near_tails(tails, me, count):
    out = []
    for other in (me - 1, me + 1):
        there = jnp.logical_and(other >= 0, other < count)
        near = jnp.where(there, jnp.bitwise_xor(me, other), 0)
        picked = sum(jnp.where(near == j, tail, 0) for j, tail in enumerate(tails))
        out.append((other, there, picked))
    return out


def pick_kernel(halo, coarse_halo, fine, coarse, nodes, rows, coarse_rows, dest, target, parent, paired, crossed, own_tail, lists):
    at = row_layout(fine, coarse)
    lists[...] = jnp.zeros_like(lists)
    listed, coarse_listed = rows.get()[...], coarse_rows.get()[...]
    for side in (0, 1):
        lists[at["coarse"] : at["coarse"] + 1, side * coarse_halo : (side + 1) * coarse_halo] = coarse_listed[side : side + 1]
        lanes = slice(side * halo, (side + 1) * halo)
        lists[at["fine_high"] : at["fine_high"] + 1, lanes] = jnp.right_shift(listed[side : side + 1], 7)
        lists[at["fine_low"] : at["fine_low"] + 1, lanes] = jnp.bitwise_and(listed[side : side + 1], LANES - 1)
    lists[at["dest"] : at["target"], :] = dest.get()[...]
    lists[at["target"] : at["high"], :] = target.get()[...]
    parents = parent.get()[...]
    lists[at["high"] : at["low"], :] = jnp.right_shift(parents, 7)
    lists[at["low"] : at["coarse"], :] = jnp.bitwise_and(parents, LANES - 1)
    tail = lists[...].astype(F32).astype(BF16)
    nodes = nodes.get()
    odd = jnp.bitwise_and(lax.axis_index("region"), 1)
    for out, up in ((paired, 1 - odd), (crossed, odd)):
        col = column(jnp.where(up == 1, listed[1:2], listed[0:1]))
        out[:halo, :] = dot(hot_rows(col, fine), nodes[...]).astype(BF16)
        out[halo:, :] = tail
    own_tail[...] = tail


def lower_higher(paired, crossed):
    odd = jnp.bitwise_and(lax.axis_index("region"), 1) == 1
    paired, crossed = paired.astype(F32), crossed.astype(F32)
    return jnp.where(odd, paired, crossed).astype(BF16), jnp.where(odd, crossed, paired).astype(BF16)


def ready_kernel(nodes, senders, receivers, edges, first, _1, _2, _3, *outs):
    *cols, before = outs
    nodes, first = nodes.get()[...], first.get()[...]
    fill_columns(nodes.shape[0], senders.get()[...], receivers.get()[...], cols)
    edges, inner = edges.get(), from_own(cols, nodes, first)
    for at in range(0, edges.shape[0], STEP):
        rows = slice(at, min(at + STEP, edges.shape[0]))
        before[rows, :] = dot(edges[rows, :], first[2 * LANES :]) + inner(rows)


def fine_kernel(halo, paired, crossed, tail, before, *refs):
    cols, (nodes, receivers, edges, *weights), (payload, new_edges) = refs[:6], refs[6:13], refs[13:]
    nodes = nodes.get()[...]
    fine = nodes.shape[0]
    outer = jnp.concatenate(lower_higher(paired[:halo, :], crossed[:halo, :]), axis=0)
    outside = from_halo(cols, outer, fine, weights[0].get()[...])
    payload[:fine, :] = finish(lambda rows: before[rows, :] + outside(rows), nodes, receivers, cols[-1], edges.get(), weights, new_edges)
    payload[fine:, :] = tail[...]


def columns_kernel(own, senders, receivers, edges, first, *outs):
    *cols, before = outs
    fill_columns(own, senders.get()[...], receivers.get()[...], cols)
    before[...] = dot(edges.get()[...], first.get()[2 * LANES :, :])


def edge_kernel(edges, first, before):
    before[...] = dot(edges[...], first.get()[2 * LANES :, :])


def add_fine(codes, blocks, coarse, sums):
    half = codes.shape[0] // 2
    for block in blocks:
        fine = block.shape[0] - TAIL
        at, tail, f = row_layout(fine, coarse), tail_of(block, fine), fine // LANES
        parent = tail[at["dest"] : at["dest"] + f] * coarse + tail[at["target"] : at["target"] + f]
        more = [sums_and_counts(hot_codes(part, parent), block[:fine, :]) for part in (codes[:half], codes[half:])]
        sums = [(total + a, members + b) for (total, members), (a, b) in zip(sums, more)]
    return sums


def begin_kernel(coarse, *refs):
    *blocks, codes, totals, members = refs
    half = codes.shape[0] // 2
    zero = jnp.zeros((half, LANES), F32)
    for i, (total, count) in enumerate(add_fine(codes[...], blocks, coarse, [(zero, zero)] * 2)):
        totals[i * half : (i + 1) * half, :] = total
        members[i * half : (i + 1) * half, :] = count


def coarse_kernel(coarse, own, last, codes, totals, members, before, *rest):
    cols, (receivers, edges, *weights), (payload, new_edges) = rest[:3], rest[3:9], rest[9:]
    half = codes.shape[0] // 2
    halves = (slice(0, half), slice(half, 2 * half))
    sums = [(totals[rows, :], members[rows, :]) for rows in halves]
    table = jnp.concatenate(means(add_fine(codes[...], [last], coarse, sums)), axis=0)
    inner = from_table(cols, table, weights[0].get()[...])
    payload[:coarse, :] = finish(lambda rows: before[rows, :] + inner(rows), table[:coarse], receivers, None, edges.get(), weights, new_edges)
    fine, c = own.shape[0] - TAIL, coarse // LANES
    high = row_layout(fine, coarse)["high"]
    payload[coarse:, :] = jnp.concatenate(
        [tail_of(own, fine)[high : high + 2 * c], jnp.zeros((TAIL - 2 * c, LANES), I32)], axis=0
    ).astype(F32).astype(BF16)


def compact(first, ranks, codes, edges, size, at_once=8):
    place = lax.broadcasted_iota(I32, (size, LANES), 0) + first

    def body(g, carry):
        latents, found = carry
        rank = ranks[pl.ds(pl.multiple_of(g * at_once, at_once), at_once), :]
        code = codes[pl.ds(pl.multiple_of(g * at_once, at_once), at_once), :]
        for i in range(at_once):
            found = found + jnp.where(place == rank[i : i + 1], code[i : i + 1], 0)
        wide = at_once * LANES
        rows = edges[pl.ds(pl.multiple_of(g * wide, wide), wide), :]
        return latents + dot(hot_codes(place, rank), rows), found

    zero = jnp.zeros((size, LANES), F32), jnp.zeros((size, LANES), I32)
    latents, found = lax.fori_loop(0, ranks.shape[0] // at_once, body, zero)
    found = jnp.sum(found.astype(F32), axis=1, keepdims=True).astype(I32)
    return latents.astype(BF16), jnp.broadcast_to(found, (size, LANES))


def below(rows, same):
    square = (rows, rows)
    mask = same(lax.broadcasted_iota(I32, square, 0), lax.broadcasted_iota(I32, square, 1))
    return jnp.where(mask, 1.0, 0.0).astype(BF16)


def running(flags):
    upto = jnp.where(lax.broadcasted_iota(I32, (LANES, LANES), 0) <= lane_iota(LANES), 1.0, 0.0).astype(BF16)
    inside = dot(flags.astype(BF16), upto)
    return inside, jnp.broadcast_to(inside[:, LANES - 1 :], flags.shape)


def listed_kernel(regions, halo, fine, coarse, *refs):
    own, paired, crossed, senders, receivers, edges, parents, firsts, halo_rows, halo_blocks, ranks, codes = refs[:12]
    latents, send, recv, recv_rows, pool_codes = refs[12:]
    me = lax.axis_index("region")
    at = row_layout(fine, coarse)
    start = paired.shape[0] - TAIL
    lower, higher = lower_higher(paired[start:, :], crossed[start:, :])
    own_tail, lower_tail, higher_tail = (tail.astype(F32).astype(I32) for tail in (own[...], lower, higher))
    near = ((me - 1, me > 0, lower_tail), (me + 1, me < regions - 1, higher_tail))
    c = coarse // LANES
    wide, size = parents.shape[0], latents.shape[0]

    def own_parents(tail):
        return tail[at["high"] : at["high"] + c] * LANES + tail[at["low"] : at["low"] + c]

    cols = [columns(own_parents(own_tail))]
    pool_codes[:coarse, :] = me * coarse + lax.broadcasted_iota(I32, (coarse, LANES), 0)
    for side, (other, there, tail) in enumerate(near):
        first = halo * (1 - side)
        col = columns(tail[at["coarse"] : at["coarse"] + 1])[first : first + halo]
        halo_rows[side * halo : (side + 1) * halo, :] = col
        pool_codes[coarse + side * halo : coarse + (side + 1) * halo, :] = jnp.where(there, other * coarse + col, -1)
        halo_blocks[side * halo : (side + 1) * halo, :] = jnp.full(col.shape, jnp.where(there, jnp.bitwise_xor(me, other), -1))
        theirs = own_parents(tail).astype(F32)
        value = jnp.zeros((halo, LANES), F32)
        for i in range(c):
            value = value + jnp.where(col == lane_iota(halo, i * LANES), theirs[i : i + 1], 0.0)
        value = jnp.broadcast_to(jnp.sum(value, axis=1, keepdims=True), (halo, LANES)).astype(I32)
        cols.append(jnp.where(there, value, -1))
    cols.append(jnp.full((wide - coarse - 2 * halo, LANES), -1, I32))
    cols = jnp.concatenate(cols, axis=0)
    parents[...] = cols

    high_count = TOP // LANES
    rows = as_rows(cols)
    row_at = lax.broadcasted_iota(I32, (wide, LANES), 0)
    for i in range(wide // LANES):
        earlier = jnp.logical_and(cols == rows[i : i + 1], row_at < lane_iota(wide, i * LANES))
        seen = jnp.max(jnp.where(earlier, 1.0, 0.0), axis=0, keepdims=True)
        firsts[i : i + 1, :] = jnp.where(seen > 0.0, -2, rows[i : i + 1])
    tops = dot(
        hot_cols(jnp.right_shift(rows, 7), high_count), hot_rows(jnp.bitwise_and(cols, LANES - 1), LANES)
    )
    tops = jnp.minimum(tops, 1.0).astype(BF16)
    receivers = receivers.get()
    count = receivers.shape[0]
    high = lax.broadcasted_iota(I32, (high_count, LANES), 0)
    needed = []
    for i in range(0, count, 8):
        some = receivers[i : i + 8, :]
        match = dot(tops, hot_cols(jnp.bitwise_and(some, LANES - 1), LANES))
        for k in range(8):
            mine = jnp.where(high == jnp.right_shift(some[k : k + 1], 7), match[:, k * LANES : (k + 1) * LANES], 0.0)
            needed.append(jnp.sum(mine, axis=0, keepdims=True))
    needed = jnp.concatenate(needed, axis=0)

    group_of = lambda i: jnp.right_shift(i, GROUP.bit_length() - 1)
    inside, sums = running(needed)
    sums = sums.astype(BF16)
    local = dot(below(count, lambda i, j: jnp.logical_and(j < i, group_of(i) == group_of(j))), sums) + inside - 1.0
    in_group = dot(below(count, lambda i, j: group_of(i) == group_of(j)), sums)
    used = jnp.minimum(in_group, float(SLOTS))
    before = dot(below(count, lambda i, j: group_of(j) < group_of(i)), (used / GROUP).astype(BF16))
    placed = jnp.logical_and(local < SLOTS, local + before < size)
    others = jnp.where(placed, 0.0, needed)
    inside, sums = running(others)
    rank = dot(below(count, lambda i, j: j < i), sums.astype(BF16)) + inside - 1.0
    ranks[...] = jnp.where(others > 0.0, rank, -1.0).astype(I32)
    total = jnp.sum(jnp.sum(needed - others, axis=0, keepdims=True), axis=1, keepdims=True).astype(I32)
    codes[...] = senders.get()[...] * TOP + receivers[...]

    slot = jnp.where(needed > 0.0, local, -1.0).astype(I32)
    place = lax.broadcasted_iota(I32, (SLOTS, LANES), 0)
    edges = edges.get()
    lane = lane_iota(SLOTS)
    slots, targets = [], []
    for first in range(0, count, GROUP):
        code = jnp.zeros((SLOTS, LANES), F32)
        for i in range(first, first + GROUP):
            code = code + jnp.where(place == slot[i : i + 1], codes[i : i + 1, :].astype(F32), 0.0)
        code = jnp.broadcast_to(jnp.sum(code, axis=1, keepdims=True), (SLOTS, LANES)).astype(I32)
        parts = jnp.where(
            lane == 0,
            jnp.right_shift(code, 16),
            jnp.where(lane == 1, jnp.bitwise_and(jnp.right_shift(code, 8), 255), jnp.bitwise_and(code, 255)),
        )
        parts = jnp.where(lane < 3, parts, 0).astype(F32).astype(BF16)
        chosen = hot_cols(slot[first : first + GROUP], SLOTS)
        packed = dot(chosen, edges[first * LANES : (first + GROUP) * LANES, :]).astype(BF16)
        slots.append(jnp.concatenate([packed, parts], axis=1))
        target = before[first : first + 1] + lane_iota(1).astype(F32)
        targets.append(jnp.where(lane_iota(1).astype(F32) < used[first : first + 1], target, -1.0).astype(I32)[:, :SLOTS])
    per = LANES // SLOTS
    targets = [jnp.concatenate(targets[i : i + per], axis=1) for i in range(0, len(targets), per)]
    packed = dot(hot_cols(jnp.concatenate(targets, axis=0), size), jnp.concatenate(slots, axis=0))
    latents[...] = packed[:, :LANES].astype(BF16)
    parts = packed[:, LANES:]
    lane = lane_iota(size)
    code = jnp.where(lane == 0, parts * 65536.0, jnp.where(lane == 1, parts * 256.0, parts))
    code = jnp.broadcast_to(jnp.sum(code, axis=1, keepdims=True), (size, LANES)).astype(I32)
    send[...], recv[...] = ends(code, 0, total)
    recv_rows[...] = as_rows(recv[...])


def ends(code, first_place, total):
    place = lax.broadcasted_iota(I32, code.shape, 0) + first_place
    recv = jnp.where(place < total, jnp.bitwise_and(code, TOP - 1), -3)
    return jnp.right_shift(code, TOP.bit_length() - 1), recv


def parent_kernel(regions, halo, coarse, *refs):
    blocks, (table, parent_hots, parent_blocks) = refs[:regions], refs[regions:]
    me = lax.axis_index("region")
    fine = blocks[0].shape[0] - TAIL
    at = row_layout(fine, coarse)
    tails = [tail_of(block, fine) for block in blocks]
    f = fine // LANES

    def own_parents(tail):
        return tail[at["dest"] : at["dest"] + f] * coarse + tail[at["target"] : at["target"] + f]

    table[:fine, :] = blocks[0][:fine, :]
    owner = lambda tail: tail[at["dest"] : at["dest"] + f]
    parent_hots[:fine, :] = hot_rows(columns(tails[0][at["target"] : at["target"] + f]), coarse)
    parent_blocks[:fine, :] = jnp.bitwise_xor(columns(owner(tails[0])), me)
    for side, (other, there, tail) in enumerate(near_tails(tails, me, regions)):
        rows = slice(fine + side * halo, fine + (side + 1) * halo)
        first = halo * (1 - side)
        listed = tail[at["fine_high"] : at["fine_high"] + 1] * LANES + tail[at["fine_low"] : at["fine_low"] + 1]
        col = columns(listed)[first : first + halo]
        theirs = own_parents(tail).astype(F32)
        value = jnp.zeros((halo, LANES), F32)
        for i in range(f):
            value = value + jnp.where(col == lane_iota(halo, i * LANES), theirs[i : i + 1], 0.0)
        value = jnp.broadcast_to(jnp.sum(value, axis=1, keepdims=True), (halo, LANES)).astype(I32)
        parent_hots[rows, :] = hot_rows(jnp.bitwise_and(value, coarse - 1), coarse)
        block = jnp.bitwise_xor(jnp.right_shift(value, coarse.bit_length() - 1), me)
        parent_blocks[rows, :] = jnp.where(there, block, -1)
        total = jnp.zeros((halo, LANES), F32)
        for j, block in enumerate(blocks):
            here = jnp.logical_and(there, jnp.bitwise_xor(me, j) == other)
            total = total + dot(hot_rows(jnp.where(here, col, -1), fine), block[:fine, :])
        table[rows, :] = total.astype(BF16)


def sums_and_counts(chosen, rows):
    both = dot(chosen, jnp.concatenate([rows, jnp.ones(rows.shape, BF16)], axis=1))
    return both[:, :LANES], both[:, LANES:]


def add_blocks(cols, blocks, coarse, sums):
    c = coarse // LANES

    def add(block, sums):
        tail = tail_of(block, coarse)
        parent = tail[:c] * LANES + tail[c : 2 * c]
        more = [sums_and_counts(hot_codes(col, parent), block[:coarse, :]) for col in cols]
        return tuple((total + a, members + b) for (total, members), (a, b) in zip(sums, more))

    if isinstance(blocks, tuple):
        for block in blocks:
            sums = add(block, sums)
        return sums
    return lax.fori_loop(0, blocks.shape[0], lambda n, sums: add(blocks.at[n], sums), sums)


def nothing(cols):
    return tuple((jnp.zeros(col.shape, F32),) * 2 for col in cols)


def means(sums):
    return [(total / jnp.maximum(members, 1.0)).astype(BF16) for total, members in sums]


def half_kernel(coarse, *refs):
    *blocks, stack = refs[:-6]
    rows = coarse + TAIL
    blocks = tuple(blocks) + tuple(stack.at[i : i + rows] for i in range(0, stack.shape[0], rows))
    parents, send, *outs = refs[-6:]
    cols = [parents[...], send[...]]
    for i, value in enumerate(sum(add_blocks(cols, blocks, coarse, nothing(cols)), ())):
        outs[i][...] = value


def as_rows(col):
    return jnp.concatenate(
        [jnp.transpose(col[i : i + LANES])[:1] for i in range(0, col.shape[0], LANES)], axis=0
    )


def top_kernel(regions, halo, coarse, size, count, *refs):
    subs = lax.axis_size("sub")
    if count > 1:
        rows = coarse + TAIL
        stacks = refs[count - regions // 2 : count]
        there = tuple(stack.at[i * rows : (i + 1) * rows] for stack in stacks for i in range(subs))
        blocks = tuple((there if j % 2 else refs)[j // 2 * subs + k] for j in range(regions) for k in range(subs))
        begun = [ref[...] for ref in refs[count : count + 4]]
        begun, refs = ((begun[0], begun[1]), (begun[2], begun[3])), refs[count + 4 :]
    else:
        there = blocks = refs[0]
        begun, refs = None, refs[count:]
    parents, firsts, halo_rows, halo_blocks, ranks, codes, latents, send, recv, recv_rows, all_edges = refs[:11]
    edges, before3, *cols = refs[11:16]
    receivers, top_weights, weights = refs[16], refs[17:21], refs[21:25]
    out, agg, fallback, semaphore = refs[25:]
    me = lax.axis_index("region")
    own_sub = lambda j: blocks[j * subs] if count > 1 else blocks.at[j * subs]
    mine, firsts = parents[...], firsts[...]
    cols_here = [mine, send[...]]
    top_own, from_send = means(add_blocks(cols_here, there[subs:] if count > 1 else there, coarse, nothing(cols_here) if begun is None else begun))
    near = gather(halo_rows[...], halo_blocks[...], [own_sub(j)[:coarse, :] for j in range(regions)])
    down = jnp.concatenate([own_sub(0)[:coarse, :].astype(F32), near], axis=0)
    first, second = top_weights[0].get()[...], centre(top_weights[1].get()[...])
    received = dot(top_own, first[LANES : 2 * LANES]).astype(BF16)
    others = jnp.concatenate([first[:LANES], first[2 * LANES :]], axis=0)

    def one(edge, from_send, recv, recv_rows):
        before = dot(jnp.concatenate([from_send, edge], axis=1), others) + dot(hot_codes(recv, firsts), received)
        new = (edge.astype(F32) + perceptron(before, second)).astype(BF16)
        return dot(hot_codes(mine, recv_rows), new)

    agg[...] = one(latents[...], from_send, recv[...], recv_rows[...])

    def more(b, carry):
        copy = pltpu.make_async_copy(all_edges, fallback, semaphore.at[0])
        copy.start()
        copy.wait()
        edge, code = compact(b * LANES, ranks, codes, fallback, LANES)
        send, recv = ends(code, b * LANES, left)
        (from_send,) = means(add_blocks([send], blocks, coarse, nothing([send])))
        agg[...] += one(edge, from_send, recv, as_rows(recv))
        return carry

    left = jnp.max(ranks[...]) + 1
    lax.fori_loop(0, (left + LANES - 1) // LANES, more, 0)
    top_final = node_update(top_own, agg[...], top_weights[2].get()[...], top_weights[3].get()[...])
    table = (down + top_final[: coarse + 2 * halo].astype(F32)).astype(BF16)
    inner = from_table(cols, table, weights[0].get()[...])
    out[...] = finish(lambda rows: before3[rows, :] + inner(rows), table[:coarse], receivers, None, edges, weights)


def last_kernel(regions, *refs):
    blocks, (down, parent_hots, parent_blocks, edges, before, *rest) = refs[:regions], refs[regions:]
    cols, receivers, weights, out = rest[:6], rest[6], rest[7:11], rest[11]
    own = out.shape[0]
    parent = pick(parent_hots[...], parent_blocks[...], [block[...] for block in blocks])
    table = (down[...].astype(F32) + parent).astype(BF16)
    first = weights[0].get()[...]
    inner, outside = from_own(cols, table[:own], first), from_halo(cols, table[own:], own, first)
    out[...] = finish(lambda rows: before[rows, :] + inner(rows) + outside(rows), table[:own], receivers, cols[-1], edges, weights)


class Here:
    def __init__(self, place):
        self.place = place

    def get(self):
        return self.place


class Arriving(Here):
    def __init__(self, source, place, semaphore):
        super().__init__(place)
        self.copy, self.waiting = pltpu.make_async_copy(source, place, semaphore), True
        self.copy.start()

    def get(self):
        if self.waiting:
            self.copy.wait()
            self.waiting = False
        return self.place


def call(kernel, args, outs, more=(), scratch=(), raw=(), cost=1, far=False, limit=LIMIT):
    specs = [pl.BlockSpec(memory_space=pltpu.HBM if i in raw else pltpu.VMEM) for i in range(len(args))]
    specs += [pl.BlockSpec(memory_space=pltpu.HBM if far else pltpu.VMEM)] * len(more)
    out_specs = [pl.BlockSpec(memory_space=pltpu.VMEM)] * len(outs)
    places = []
    if far:
        places = [pltpu.VMEM(array.shape, array.dtype) for array, _ in more]
        places.append(pltpu.SemaphoreType.DMA((len(more),)))
    n, k, o = len(args), len(more), len(outs)

    def body(*refs):
        given, sources, results, rest = refs[:n], refs[n : n + k], refs[n + k : n + k + o], refs[n + k + o :]
        if far:
            near, semaphores, rest = rest[:k], rest[k], rest[k + 1 :]
            operands = [Arriving(source, near[i], semaphores.at[i]) for i, source in enumerate(sources)]
        else:
            operands = [Here(ref if at is None else ref.at[at]) for ref, (_, at) in zip(sources, more)]
        kernel(*given, *operands, *results, *rest)

    return pl.pallas_call(
        body,
        out_shape=[jax.ShapeDtypeStruct(shape, dtype) for shape, dtype in outs],
        in_specs=specs,
        out_specs=out_specs,
        scratch_shapes=places + list(scratch),
        compiler_params=pltpu.CompilerParams(vmem_limit_bytes=limit),
        cost_estimate=pl.CostEstimate(flops=cost * 10**9, bytes_accessed=cost * 10**5, transcendentals=0),
    )(*args, *[array for array, _ in more])


def over_region(rows, beside=None):
    count = lax.axis_size("region")
    blocks = {0: rows}
    bit = count // 2
    while bit:
        going = dict(blocks)
        if beside is not None and len(going) > 1:
            for j in (0, max(going)):
                going[j], beside = lax.optimization_barrier((going[j], beside))
        for j in blocks:
            going[j + bit] = lax.ppermute(going[j], "region", [(i, i ^ bit) for i in range(count)])
        blocks = going
        bit //= 2
    blocks = [blocks[j] for j in range(count)]
    return blocks if beside is None else (blocks, beside)


def over_both(rows, beside):
    regions, subs = lax.axis_size("region"), lax.axis_size("sub")
    swap = lambda array, axis, bits: lax.ppermute(array, axis, [(i, i ^ bits) for i in range(lax.axis_size(axis))])
    turns = [rows] + [swap(rows, "sub", k) for k in range(1, subs)]
    if regions * subs <= 16:
        turns[1], beside = lax.optimization_barrier((turns[1], beside))
        blocks = {0: turns}
        bit = regions // 2
        while bit > 1:
            for j in list(blocks):
                blocks[j + bit] = [swap(block, "region", bit) for block in blocks[j]]
            bit //= 2
        here = [block for j in range(0, regions, 2) for block in blocks[j]]
        return here + [swap(jnp.concatenate(blocks[j]), "region", 1) for j in range(0, regions, 2)], beside
    blocks, bit = jnp.stack(turns), 1
    while bit < regions:
        blocks, bit = jnp.concatenate([blocks, swap(blocks, "region", bit)]), 2 * bit
    return [blocks], beside


def on_device(
    node_feats,
    fine_senders,
    fine_receivers,
    fine_edges,
    halo_rows,
    coarse_senders,
    coarse_receivers,
    coarse_edges,
    coarse_halo_rows,
    pool_dest,
    pool_target,
    pool3_target,
    top_senders,
    top_receivers,
    top_edges,
    edge_in,
    edge_out,
    node_in,
    node_out,
):
    weights = (edge_in, edge_out, node_in, node_out)
    regions = lax.axis_size("region")
    fine, coarse = node_feats.shape[0], pool3_target.shape[0]
    halo, halo2 = halo_rows.shape[1], coarse_halo_rows.shape[1]
    rows = lambda a: a.reshape(-1, LANES)
    fine_send, fine_recv = rows(fine_senders), rows(fine_receivers)
    coarse_send, coarse_recv = rows(coarse_senders), rows(coarse_receivers)
    top_send, top_recv = rows(top_senders), rows(top_receivers)

    level = lambda index: [(matrix, index) for matrix in weights]
    plain = lambda *arrays: [(array, None) for array in arrays]

    to_pair, to_other, tail = call(
        functools.partial(pick_kernel, halo, halo2, fine, coarse),
        [],
        [((halo + TAIL, LANES), BF16)] * 2 + [((TAIL, LANES), BF16)],
        plain(node_feats, halo_rows, coarse_halo_rows, rows(pool_dest), rows(pool_target), rows(pool3_target)),
        scratch=[pltpu.VMEM((TAIL, LANES), I32)],
        far=True,
        limit=60 * 1024 * 1024,
    )
    pairs = lambda first: [(i, j) for low in range(first, regions - 1, 2) for i, j in ((low, low + 1), (low + 1, low))]
    paired = lax.ppermute(to_pair, "region", pairs(0))
    crossed = lax.ppermute(to_other, "region", pairs(1))
    one = lambda index: [(edge_in, index)]
    fine_cols, coarse_cols = edge_columns(fine, fine_edges.shape[0]), edge_columns(coarse, coarse_edges.shape[0])
    late_send, tail = lax.optimization_barrier((fine_send, tail))
    *fine_cols, before = call(
        ready_kernel,
        [],
        fine_cols + [(fine_edges.shape, F32)],
        plain(node_feats, late_send, fine_recv, fine_edges) + level(0),
        cost=2,
    )
    payload, fine_edges2 = call(
        functools.partial(fine_kernel, halo),
        [paired, crossed, tail, before, *fine_cols],
        [((fine + TAIL, LANES), BF16), (fine_edges.shape, BF16)],
        plain(node_feats, fine_recv, fine_edges) + level(0),
        cost=3,
    )
    wide = -(-(coarse + 2 * halo2) // LANES) * LANES
    size = min(384, top_edges.shape[0])
    listed_shapes = [
        ((wide, LANES), I32),
        ((wide // LANES, LANES), I32),
        ((2 * halo2, LANES), I32),
        ((2 * halo2, LANES), I32),
        (top_send.shape, I32),
        (top_send.shape, I32),
        ((size, LANES), BF16),
        ((size, LANES), I32),
        ((size, LANES), I32),
        ((size // LANES, LANES), I32),
        ((coarse + 2 * halo2, LANES), I32),
    ]
    selected = call(
        functools.partial(listed_kernel, regions, halo2, fine, coarse),
        [tail, paired, crossed],
        listed_shapes,
        plain(top_send, top_recv, top_edges),
        cost=3,
    )
    payload, late_edges = lax.optimization_barrier((payload, coarse_edges))
    *coarse_cols, before = call(
        functools.partial(columns_kernel, coarse),
        [],
        coarse_cols + [(coarse_edges.shape, F32)],
        plain(coarse_send, coarse_recv, late_edges) + one(1),
    )
    blocks, selected = over_region(payload, selected)
    *selected, pool_codes = selected
    totals, members = call(
        functools.partial(begin_kernel, coarse),
        blocks[:-1] + [pool_codes],
        [(pool_codes.shape, F32)] * 2,
    )
    payload2, coarse_edges2 = call(
        functools.partial(coarse_kernel, coarse),
        [blocks[0], blocks[-1], pool_codes, totals, members, before, *coarse_cols],
        [((coarse + TAIL, LANES), BF16), (coarse_edges.shape, BF16)],
        plain(coarse_recv, coarse_edges) + level(1),
        cost=3,
    )
    table_shape = (fine + 2 * halo, LANES)
    table = call(
        functools.partial(parent_kernel, regions, halo, coarse),
        blocks,
        [(table_shape, BF16), ((table_shape[0], coarse), BF16), (table_shape, I32)],
    )
    before = call(edge_kernel, [coarse_edges2], [(coarse_edges.shape, F32)], one(3))
    blocks2, (table, before) = over_both(payload2, (table, before))
    many = len(blocks2)
    begun = []
    if many > 1:
        begun = call(
            functools.partial(half_kernel, coarse),
            blocks2[: 1 - regions // 2] + [selected[0], selected[7]],
            [((wide, LANES), F32)] * 2 + [((size, LANES), F32)] * 2,
        )
    (coarse_final,) = call(
        functools.partial(top_kernel, regions, halo2, coarse, size, many),
        blocks2 + [*begun, *selected, top_edges, coarse_edges2, *before, *coarse_cols],
        [((coarse, LANES), BF16)],
        plain(coarse_recv) + level(2) + level(3),
        scratch=[
            pltpu.VMEM((wide, LANES), F32),
            pltpu.VMEM(top_edges.shape, BF16),
            pltpu.SemaphoreType.DMA((1,)),
        ],
        raw=(many + len(begun) + len(selected),),
        cost=6,
    )
    before = call(edge_kernel, [fine_edges2], [(fine_edges.shape, F32)], one(4))
    blocks3, before = over_region(coarse_final, before)
    (fine_final,) = call(
        functools.partial(last_kernel, regions),
        blocks3 + [*table, fine_edges2, *before, *fine_cols],
        [((fine, LANES), BF16)],
        plain(fine_recv) + level(4),
        cost=3,
    )
    return fine_final


def solution(mesh):
    spread = ("parts", "region", "sub")
    rows, flat = P(spread, None), P(spread)
    in_specs = (
        (rows, flat, flat, rows, rows, flat, flat, rows, rows, rows, flat, flat)
        + (P("parts"), P("parts"), P("parts", None))
        + (P(),) * 4
    )
    return jax.shard_map(on_device, mesh=mesh, in_specs=in_specs, out_specs=rows, check_vma=False)
```

```python
import functools

import jax
import jax.numpy as jnp
from jax import lax
from jax.experimental import pallas as pl
from jax.experimental.pallas import tpu as pltpu
from jax.sharding import PartitionSpec as P

EPSILON = 1e-05
TOP = 2048
LANES = 128
F32, BF16, I32, I16 = jnp.float32, jnp.bfloat16, jnp.int32, jnp.int16
GROUP, SLOTS = 8, 64
STEP = 3072
CUT_BITS = 8
CUT = 1 << CUT_BITS
TAIL = 16
LIMIT = 32 * 1024 * 1024


def dot(a, b):
    return jnp.dot(a, b, preferred_element_type=F32)


def lane_iota(rows, first=0):
    return lax.broadcasted_iota(I32, (rows, LANES), 1) + first


def column(row):
    return jnp.transpose(jnp.broadcast_to(row, (LANES, row.shape[1])))


def columns(rows):
    return jnp.concatenate([column(rows[i : i + 1]) for i in range(rows.shape[0])], axis=0)


def hot(mask):
    return jnp.where(mask, jnp.ones(mask.shape, BF16), jnp.zeros(mask.shape, BF16))


def short(row, count):
    return jnp.concatenate([jnp.broadcast_to(row, (16, LANES)).astype(I16)] * (count // 16), axis=0)


def hot_rows(col, count, start=0):
    col = col.astype(I16)
    places = [lane_iota(16, first) for first in range(start, start + count, LANES)]
    return jnp.concatenate([hot(col == short(place[:1], col.shape[0])) for place in places], axis=1)


def hot_cols(rows, count):
    return hot_codes(lax.broadcasted_iota(I32, (count, LANES), 0), rows)


def hot_codes(col, rows):
    col = col.astype(I16)
    return jnp.concatenate([hot(col == short(rows[i : i + 1], col.shape[0])) for i in range(rows.shape[0])], axis=1)


def gather(row, block, blocks, all_there=False):
    return pick(hot_rows(row, blocks[0].shape[0]), block, blocks, all_there)


def pick(hots, block, blocks, all_there=False):
    wide = dot(hots, jnp.concatenate(blocks, axis=1))
    if block is None:
        return wide
    out = wide[:, :LANES] if all_there else jnp.zeros((hots.shape[0], LANES), F32)
    for i in range(1 if all_there else 0, len(blocks)):
        out = jnp.where(block == i, wide[:, i * LANES : (i + 1) * LANES], out)
    return out


def cut(table):
    short = -table.shape[0] % CUT
    if short:
        table = jnp.concatenate([table, jnp.zeros((short, LANES), BF16)], axis=0)
    return [table[i : i + CUT] for i in range(0, table.shape[0], CUT)]


def segment_sum(rows, block, values):
    chosen = hot_cols(jnp.bitwise_and(rows, CUT - 1), CUT)
    if block is None:
        return jnp.concatenate([dot(chosen[: CUT // 2], values), dot(chosen[CUT // 2 :], values)], axis=0)
    upper = values * block
    wide = jnp.concatenate([values - upper, upper], axis=1)
    out = jnp.concatenate([dot(chosen[: CUT // 2], wide), dot(chosen[CUT // 2 :], wide)], axis=0)
    return jnp.concatenate([out[:, :LANES], out[:, LANES:]], axis=0)


def centre(second):
    exact = second.astype(F32)
    return (exact - jnp.mean(exact, axis=1, keepdims=True)).astype(BF16)


def perceptron(before, centred_second):
    out = dot(jnp.maximum(before.astype(BF16), 0.0), centred_second)
    return out * lax.rsqrt(jnp.mean(out * out, axis=-1, keepdims=True) + EPSILON)


def node_update(nodes, summed, first, second):
    before = dot(nodes, first[:LANES]) + dot(summed.astype(BF16), first[LANES:])
    return (nodes.astype(F32) + perceptron(before, centre(second))).astype(BF16)


def project(blocks, matrix):
    return [dot(block, matrix).astype(BF16) for block in blocks]


def edge_columns(own, count):
    shape = (count, LANES)
    if own == 2 * CUT:
        return [(shape, I32), (shape, I32), (shape, I32), (shape, I32), (shape, I32), (shape, BF16)]
    return [(shape, I32), (shape, I32), (shape, I32)]


def fill_columns(own, senders, receivers, outs):
    send, recv = columns(senders), columns(receivers)
    low, high = jnp.bitwise_and(send, CUT - 1), jnp.right_shift(send, CUT_BITS)
    if own == 2 * CUT:
        low = jnp.where(send < own, low, -1)
        recv_high = jnp.right_shift(recv, CUT_BITS)
        values = [send, low, high, jnp.bitwise_and(recv, CUT - 1), recv_high, recv_high.astype(F32)]
    else:
        values = [low, high, recv]
    for value, out in zip(values, outs):
        out[...] = value.astype(out.dtype)


def from_own(cols, nodes, first):
    _, low, high, recv_low, recv_high, _ = cols
    blocks = cut(nodes)
    sent, received = project(blocks, first[:LANES]), project(blocks, first[LANES : 2 * LANES])
    return lambda rows: (
        gather(low[rows, :], high[rows, :], sent, True) + gather(recv_low[rows, :], recv_high[rows, :], received, True)
    )


def from_halo(cols, halo, own, first):
    sent = dot(halo, first[:LANES]).astype(BF16)
    return lambda rows: dot(hot_rows(cols[0][rows, :], LANES, own), sent)


def from_table(cols, table, first):
    low, high, recv = cols
    sent = project(cut(table), first[:LANES])
    received = project([table[:CUT]], first[LANES : 2 * LANES])
    return lambda rows: gather(low[rows, :], high[rows, :], sent, True) + gather(recv[rows, :], None, received)


def finish(before_at, nodes, receivers, block, edges, weights, new_edges=None, step=STEP):
    second = centre(weights[1].get()[...])
    receivers = receivers.get()
    summed = 0.0
    for at in range(0, edges.shape[0], step):
        rows = slice(at, min(at + step, edges.shape[0]))
        edge = edges[rows, :]
        new = (edge.astype(F32) + perceptron(before_at(rows), second)).astype(BF16)
        if new_edges is not None:
            new_edges[rows, :] = new
        recv = receivers[rows.start // LANES : rows.stop // LANES, :]
        summed = summed + segment_sum(recv, None if block is None else block[rows, :], new)
    return node_update(nodes, summed, weights[2].get()[...], weights[3].get()[...])


def tail_of(block, count):
    return block[count : count + TAIL, :].astype(F32).astype(I32)


def row_layout(fine, coarse):
    f, c = fine // LANES, coarse // LANES
    return {"dest": 0, "target": f, "high": 2 * f, "low": 2 * f + c, "coarse": 2 * f + 2 * c, "fine_high": 2 * f + 2 * c + 1, "fine_low": 2 * f + 2 * c + 2}


def near_tails(tails, me, count):
    out = []
    for other in (me - 1, me + 1):
        there = jnp.logical_and(other >= 0, other < count)
        near = jnp.where(there, jnp.bitwise_xor(me, other), 0)
        picked = sum(jnp.where(near == j, tail, 0) for j, tail in enumerate(tails))
        out.append((other, there, picked))
    return out


def pick_kernel(halo, coarse_halo, fine, coarse, nodes, rows, coarse_rows, dest, target, parent, paired, crossed, own_tail, lists):
    at = row_layout(fine, coarse)
    lists[...] = jnp.zeros_like(lists)
    listed, coarse_listed = rows.get()[...], coarse_rows.get()[...]
    for side in (0, 1):
        lists[at["coarse"] : at["coarse"] + 1, side * coarse_halo : (side + 1) * coarse_halo] = coarse_listed[side : side + 1]
        lanes = slice(side * halo, (side + 1) * halo)
        lists[at["fine_high"] : at["fine_high"] + 1, lanes] = jnp.right_shift(listed[side : side + 1], 7)
        lists[at["fine_low"] : at["fine_low"] + 1, lanes] = jnp.bitwise_and(listed[side : side + 1], LANES - 1)
    lists[at["dest"] : at["target"], :] = dest.get()[...]
    lists[at["target"] : at["high"], :] = target.get()[...]
    parents = parent.get()[...]
    lists[at["high"] : at["low"], :] = jnp.right_shift(parents, 7)
    lists[at["low"] : at["coarse"], :] = jnp.bitwise_and(parents, LANES - 1)
    tail = lists[...].astype(F32).astype(BF16)
    nodes = nodes.get()
    odd = jnp.bitwise_and(lax.axis_index("region"), 1)
    for out, up in ((paired, 1 - odd), (crossed, odd)):
        col = column(jnp.where(up == 1, listed[1:2], listed[0:1]))
        out[:halo, :] = dot(hot_rows(col, fine), nodes[...]).astype(BF16)
        out[halo:, :] = tail
    own_tail[...] = tail


def lower_higher(paired, crossed):
    odd = jnp.bitwise_and(lax.axis_index("region"), 1) == 1
    paired, crossed = paired.astype(F32), crossed.astype(F32)
    return jnp.where(odd, paired, crossed).astype(BF16), jnp.where(odd, crossed, paired).astype(BF16)


def ready_kernel(nodes, senders, receivers, edges, first, _1, _2, _3, *outs):
    *cols, before = outs
    nodes, first = nodes.get()[...], first.get()[...]
    fill_columns(nodes.shape[0], senders.get()[...], receivers.get()[...], cols)
    edges, inner = edges.get(), from_own(cols, nodes, first)
    for at in range(0, edges.shape[0], STEP):
        rows = slice(at, min(at + STEP, edges.shape[0]))
        before[rows, :] = dot(edges[rows, :], first[2 * LANES :]) + inner(rows)


def fine_kernel(halo, paired, crossed, tail, before, *refs):
    cols, (nodes, receivers, edges, *weights), (payload, new_edges) = refs[:6], refs[6:13], refs[13:]
    nodes = nodes.get()[...]
    fine = nodes.shape[0]
    outer = jnp.concatenate(lower_higher(paired[:halo, :], crossed[:halo, :]), axis=0)
    outside = from_halo(cols, outer, fine, weights[0].get()[...])
    payload[:fine, :] = finish(lambda rows: before[rows, :] + outside(rows), nodes, receivers, cols[-1], edges.get(), weights, new_edges)
    payload[fine:, :] = tail[...]


def columns_kernel(own, senders, receivers, edges, first, *outs):
    *cols, before = outs
    fill_columns(own, senders.get()[...], receivers.get()[...], cols)
    before[...] = dot(edges.get()[...], first.get()[2 * LANES :, :])


def edge_kernel(edges, first, before):
    before[...] = dot(edges[...], first.get()[2 * LANES :, :])


def add_fine(codes, blocks, coarse, sums):
    half = codes.shape[0] // 2
    for block in blocks:
        fine = block.shape[0] - TAIL
        at, tail, f = row_layout(fine, coarse), tail_of(block, fine), fine // LANES
        parent = tail[at["dest"] : at["dest"] + f] * coarse + tail[at["target"] : at["target"] + f]
        more = [sums_and_counts(hot_codes(part, parent), block[:fine, :]) for part in (codes[:half], codes[half:])]
        sums = [(total + a, members + b) for (total, members), (a, b) in zip(sums, more)]
    return sums


def begin_kernel(coarse, *refs):
    *blocks, codes, totals, members = refs
    half = codes.shape[0] // 2
    zero = jnp.zeros((half, LANES), F32)
    for i, (total, count) in enumerate(add_fine(codes[...], blocks, coarse, [(zero, zero)] * 2)):
        totals[i * half : (i + 1) * half, :] = total
        members[i * half : (i + 1) * half, :] = count


def coarse_kernel(coarse, own, last, codes, totals, members, before, *rest):
    cols, (receivers, edges, *weights), (payload, new_edges) = rest[:3], rest[3:9], rest[9:]
    half = codes.shape[0] // 2
    halves = (slice(0, half), slice(half, 2 * half))
    sums = [(totals[rows, :], members[rows, :]) for rows in halves]
    table = jnp.concatenate(means(add_fine(codes[...], [last], coarse, sums)), axis=0)
    inner = from_table(cols, table, weights[0].get()[...])
    payload[:coarse, :] = finish(lambda rows: before[rows, :] + inner(rows), table[:coarse], receivers, None, edges.get(), weights, new_edges)
    fine, c = own.shape[0] - TAIL, coarse // LANES
    high = row_layout(fine, coarse)["high"]
    payload[coarse:, :] = jnp.concatenate(
        [tail_of(own, fine)[high : high + 2 * c], jnp.zeros((TAIL - 2 * c, LANES), I32)], axis=0
    ).astype(F32).astype(BF16)


def compact(first, ranks, codes, edges, size, at_once=8):
    place = lax.broadcasted_iota(I32, (size, LANES), 0) + first

    def body(g, carry):
        latents, found = carry
        rank = ranks[pl.ds(pl.multiple_of(g * at_once, at_once), at_once), :]
        code = codes[pl.ds(pl.multiple_of(g * at_once, at_once), at_once), :]
        for i in range(at_once):
            found = found + jnp.where(place == rank[i : i + 1], code[i : i + 1], 0)
        wide = at_once * LANES
        rows = edges[pl.ds(pl.multiple_of(g * wide, wide), wide), :]
        return latents + dot(hot_codes(place, rank), rows), found

    zero = jnp.zeros((size, LANES), F32), jnp.zeros((size, LANES), I32)
    latents, found = lax.fori_loop(0, ranks.shape[0] // at_once, body, zero)
    found = jnp.sum(found.astype(F32), axis=1, keepdims=True).astype(I32)
    return latents.astype(BF16), jnp.broadcast_to(found, (size, LANES))


def below(rows, same):
    square = (rows, rows)
    mask = same(lax.broadcasted_iota(I32, square, 0), lax.broadcasted_iota(I32, square, 1))
    return jnp.where(mask, 1.0, 0.0).astype(BF16)


def running(flags):
    upto = jnp.where(lax.broadcasted_iota(I32, (LANES, LANES), 0) <= lane_iota(LANES), 1.0, 0.0).astype(BF16)
    inside = dot(flags.astype(BF16), upto)
    return inside, jnp.broadcast_to(inside[:, LANES - 1 :], flags.shape)


def listed_kernel(regions, halo, fine, coarse, *refs):
    own, paired, crossed, senders, receivers, edges, parents, firsts, halo_rows, halo_blocks, ranks, codes = refs[:12]
    latents, send, recv, recv_rows, pool_codes = refs[12:]
    me = lax.axis_index("region")
    at = row_layout(fine, coarse)
    start = paired.shape[0] - TAIL
    lower, higher = lower_higher(paired[start:, :], crossed[start:, :])
    own_tail, lower_tail, higher_tail = (tail.astype(F32).astype(I32) for tail in (own[...], lower, higher))
    near = ((me - 1, me > 0, lower_tail), (me + 1, me < regions - 1, higher_tail))
    c = coarse // LANES
    wide, size = parents.shape[0], latents.shape[0]

    def own_parents(tail):
        return tail[at["high"] : at["high"] + c] * LANES + tail[at["low"] : at["low"] + c]

    cols = [columns(own_parents(own_tail))]
    pool_codes[:coarse, :] = me * coarse + lax.broadcasted_iota(I32, (coarse, LANES), 0)
    for side, (other, there, tail) in enumerate(near):
        first = halo * (1 - side)
        col = columns(tail[at["coarse"] : at["coarse"] + 1])[first : first + halo]
        halo_rows[side * halo : (side + 1) * halo, :] = col
        pool_codes[coarse + side * halo : coarse + (side + 1) * halo, :] = jnp.where(there, other * coarse + col, -1)
        halo_blocks[side * halo : (side + 1) * halo, :] = jnp.full(col.shape, jnp.where(there, jnp.bitwise_xor(me, other), -1))
        theirs = own_parents(tail).astype(F32)
        value = jnp.zeros((halo, LANES), F32)
        for i in range(c):
            value = value + jnp.where(col == lane_iota(halo, i * LANES), theirs[i : i + 1], 0.0)
        value = jnp.broadcast_to(jnp.sum(value, axis=1, keepdims=True), (halo, LANES)).astype(I32)
        cols.append(jnp.where(there, value, -1))
    cols.append(jnp.full((wide - coarse - 2 * halo, LANES), -1, I32))
    cols = jnp.concatenate(cols, axis=0)
    parents[...] = cols

    high_count = TOP // LANES
    rows = as_rows(cols)
    row_at = lax.broadcasted_iota(I32, (wide, LANES), 0)
    for i in range(wide // LANES):
        earlier = jnp.logical_and(cols == rows[i : i + 1], row_at < lane_iota(wide, i * LANES))
        seen = jnp.max(jnp.where(earlier, 1.0, 0.0), axis=0, keepdims=True)
        firsts[i : i + 1, :] = jnp.where(seen > 0.0, -2, rows[i : i + 1])
    tops = dot(
        hot_cols(jnp.right_shift(rows, 7), high_count), hot_rows(jnp.bitwise_and(cols, LANES - 1), LANES)
    )
    tops = jnp.minimum(tops, 1.0).astype(BF16)
    receivers = receivers.get()
    count = receivers.shape[0]
    high = lax.broadcasted_iota(I32, (high_count, LANES), 0)
    needed = []
    for i in range(0, count, 8):
        some = receivers[i : i + 8, :]
        match = dot(tops, hot_cols(jnp.bitwise_and(some, LANES - 1), LANES))
        for k in range(8):
            mine = jnp.where(high == jnp.right_shift(some[k : k + 1], 7), match[:, k * LANES : (k + 1) * LANES], 0.0)
            needed.append(jnp.sum(mine, axis=0, keepdims=True))
    needed = jnp.concatenate(needed, axis=0)

    group_of = lambda i: jnp.right_shift(i, GROUP.bit_length() - 1)
    inside, sums = running(needed)
    sums = sums.astype(BF16)
    local = dot(below(count, lambda i, j: jnp.logical_and(j < i, group_of(i) == group_of(j))), sums) + inside - 1.0
    in_group = dot(below(count, lambda i, j: group_of(i) == group_of(j)), sums)
    used = jnp.minimum(in_group, float(SLOTS))
    before = dot(below(count, lambda i, j: group_of(j) < group_of(i)), (used / GROUP).astype(BF16))
    placed = jnp.logical_and(local < SLOTS, local + before < size)
    others = jnp.where(placed, 0.0, needed)
    inside, sums = running(others)
    rank = dot(below(count, lambda i, j: j < i), sums.astype(BF16)) + inside - 1.0
    ranks[...] = jnp.where(others > 0.0, rank, -1.0).astype(I32)
    total = jnp.sum(jnp.sum(needed - others, axis=0, keepdims=True), axis=1, keepdims=True).astype(I32)
    codes[...] = senders.get()[...] * TOP + receivers[...]

    slot = jnp.where(needed > 0.0, local, -1.0).astype(I32)
    place = lax.broadcasted_iota(I32, (SLOTS, LANES), 0)
    edges = edges.get()
    lane = lane_iota(SLOTS)
    slots, targets = [], []
    for first in range(0, count, GROUP):
        code = jnp.zeros((SLOTS, LANES), F32)
        for i in range(first, first + GROUP):
            code = code + jnp.where(place == slot[i : i + 1], codes[i : i + 1, :].astype(F32), 0.0)
        code = jnp.broadcast_to(jnp.sum(code, axis=1, keepdims=True), (SLOTS, LANES)).astype(I32)
        parts = jnp.where(
            lane == 0,
            jnp.right_shift(code, 16),
            jnp.where(lane == 1, jnp.bitwise_and(jnp.right_shift(code, 8), 255), jnp.bitwise_and(code, 255)),
        )
        parts = jnp.where(lane < 3, parts, 0).astype(F32).astype(BF16)
        chosen = hot_cols(slot[first : first + GROUP], SLOTS)
        packed = dot(chosen, edges[first * LANES : (first + GROUP) * LANES, :]).astype(BF16)
        slots.append(jnp.concatenate([packed, parts], axis=1))
        target = before[first : first + 1] + lane_iota(1).astype(F32)
        targets.append(jnp.where(lane_iota(1).astype(F32) < used[first : first + 1], target, -1.0).astype(I32)[:, :SLOTS])
    per = LANES // SLOTS
    targets = [jnp.concatenate(targets[i : i + per], axis=1) for i in range(0, len(targets), per)]
    packed = dot(hot_cols(jnp.concatenate(targets, axis=0), size), jnp.concatenate(slots, axis=0))
    latents[...] = packed[:, :LANES].astype(BF16)
    parts = packed[:, LANES:]
    lane = lane_iota(size)
    code = jnp.where(lane == 0, parts * 65536.0, jnp.where(lane == 1, parts * 256.0, parts))
    code = jnp.broadcast_to(jnp.sum(code, axis=1, keepdims=True), (size, LANES)).astype(I32)
    send[...], recv[...] = ends(code, 0, total)
    recv_rows[...] = as_rows(recv[...])


def ends(code, first_place, total):
    place = lax.broadcasted_iota(I32, code.shape, 0) + first_place
    recv = jnp.where(place < total, jnp.bitwise_and(code, TOP - 1), -3)
    return jnp.right_shift(code, TOP.bit_length() - 1), recv


def parent_kernel(regions, halo, coarse, *refs):
    blocks, (table, parent_hots, parent_blocks) = refs[:regions], refs[regions:]
    me = lax.axis_index("region")
    fine = blocks[0].shape[0] - TAIL
    at = row_layout(fine, coarse)
    tails = [tail_of(block, fine) for block in blocks]
    f = fine // LANES

    def own_parents(tail):
        return tail[at["dest"] : at["dest"] + f] * coarse + tail[at["target"] : at["target"] + f]

    table[:fine, :] = blocks[0][:fine, :]
    owner = lambda tail: tail[at["dest"] : at["dest"] + f]
    parent_hots[:fine, :] = hot_rows(columns(tails[0][at["target"] : at["target"] + f]), coarse)
    parent_blocks[:fine, :] = jnp.bitwise_xor(columns(owner(tails[0])), me)
    for side, (other, there, tail) in enumerate(near_tails(tails, me, regions)):
        rows = slice(fine + side * halo, fine + (side + 1) * halo)
        first = halo * (1 - side)
        listed = tail[at["fine_high"] : at["fine_high"] + 1] * LANES + tail[at["fine_low"] : at["fine_low"] + 1]
        col = columns(listed)[first : first + halo]
        theirs = own_parents(tail).astype(F32)
        value = jnp.zeros((halo, LANES), F32)
        for i in range(f):
            value = value + jnp.where(col == lane_iota(halo, i * LANES), theirs[i : i + 1], 0.0)
        value = jnp.broadcast_to(jnp.sum(value, axis=1, keepdims=True), (halo, LANES)).astype(I32)
        parent_hots[rows, :] = hot_rows(jnp.bitwise_and(value, coarse - 1), coarse)
        block = jnp.bitwise_xor(jnp.right_shift(value, coarse.bit_length() - 1), me)
        parent_blocks[rows, :] = jnp.where(there, block, -1)
        total = jnp.zeros((halo, LANES), F32)
        for j, block in enumerate(blocks):
            here = jnp.logical_and(there, jnp.bitwise_xor(me, j) == other)
            total = total + dot(hot_rows(jnp.where(here, col, -1), fine), block[:fine, :])
        table[rows, :] = total.astype(BF16)


def sums_and_counts(chosen, rows):
    both = dot(chosen, jnp.concatenate([rows, jnp.ones(rows.shape, BF16)], axis=1))
    return both[:, :LANES], both[:, LANES:]


def add_blocks(cols, blocks, coarse, sums):
    c = coarse // LANES

    def add(block, sums):
        tail = tail_of(block, coarse)
        parent = tail[:c] * LANES + tail[c : 2 * c]
        more = [sums_and_counts(hot_codes(col, parent), block[:coarse, :]) for col in cols]
        return tuple((total + a, members + b) for (total, members), (a, b) in zip(sums, more))

    if isinstance(blocks, tuple):
        for block in blocks:
            sums = add(block, sums)
        return sums
    return lax.fori_loop(0, blocks.shape[0], lambda n, sums: add(blocks.at[n], sums), sums)


def nothing(cols):
    return tuple((jnp.zeros(col.shape, F32),) * 2 for col in cols)


def means(sums):
    return [(total / jnp.maximum(members, 1.0)).astype(BF16) for total, members in sums]


def half_kernel(coarse, *refs):
    *blocks, stack = refs[:-6]
    rows = coarse + TAIL
    blocks = tuple(blocks) + tuple(stack.at[i : i + rows] for i in range(0, stack.shape[0], rows))
    parents, send, *outs = refs[-6:]
    cols = [parents[...], send[...]]
    for i, value in enumerate(sum(add_blocks(cols, blocks, coarse, nothing(cols)), ())):
        outs[i][...] = value


def as_rows(col):
    return jnp.concatenate(
        [jnp.transpose(col[i : i + LANES])[:1] for i in range(0, col.shape[0], LANES)], axis=0
    )


def top_kernel(regions, halo, coarse, size, count, *refs):
    subs = lax.axis_size("sub")
    if count > 1:
        rows = coarse + TAIL
        stacks = refs[count - regions // 2 : count]
        there = tuple(stack.at[i * rows : (i + 1) * rows] for stack in stacks for i in range(subs))
        blocks = tuple((there if j % 2 else refs)[j // 2 * subs + k] for j in range(regions) for k in range(subs))
        begun = [ref[...] for ref in refs[count : count + 4]]
        begun, refs = ((begun[0], begun[1]), (begun[2], begun[3])), refs[count + 4 :]
    else:
        there = blocks = refs[0]
        begun, refs = None, refs[count:]
    parents, firsts, halo_rows, halo_blocks, ranks, codes, latents, send, recv, recv_rows, all_edges = refs[:11]
    edges, before3, *cols = refs[11:16]
    receivers, top_weights, weights = refs[16], refs[17:21], refs[21:25]
    out, agg, fallback, semaphore = refs[25:]
    me = lax.axis_index("region")
    own_sub = lambda j: blocks[j * subs] if count > 1 else blocks.at[j * subs]
    mine, firsts = parents[...], firsts[...]
    cols_here = [mine, send[...]]
    top_own, from_send = means(add_blocks(cols_here, there[subs:] if count > 1 else there, coarse, nothing(cols_here) if begun is None else begun))
    near = gather(halo_rows[...], halo_blocks[...], [own_sub(j)[:coarse, :] for j in range(regions)])
    down = jnp.concatenate([own_sub(0)[:coarse, :].astype(F32), near], axis=0)
    first, second = top_weights[0].get()[...], centre(top_weights[1].get()[...])
    received = dot(top_own, first[LANES : 2 * LANES]).astype(BF16)
    others = jnp.concatenate([first[:LANES], first[2 * LANES :]], axis=0)

    def one(edge, from_send, recv, recv_rows):
        before = dot(jnp.concatenate([from_send, edge], axis=1), others) + dot(hot_codes(recv, firsts), received)
        new = (edge.astype(F32) + perceptron(before, second)).astype(BF16)
        return dot(hot_codes(mine, recv_rows), new)

    agg[...] = one(latents[...], from_send, recv[...], recv_rows[...])

    def more(b, carry):
        copy = pltpu.make_async_copy(all_edges, fallback, semaphore.at[0])
        copy.start()
        copy.wait()
        edge, code = compact(b * LANES, ranks, codes, fallback, LANES)
        send, recv = ends(code, b * LANES, left)
        (from_send,) = means(add_blocks([send], blocks, coarse, nothing([send])))
        agg[...] += one(edge, from_send, recv, as_rows(recv))
        return carry

    left = jnp.max(ranks[...]) + 1
    lax.fori_loop(0, (left + LANES - 1) // LANES, more, 0)
    top_final = node_update(top_own, agg[...], top_weights[2].get()[...], top_weights[3].get()[...])
    table = (down + top_final[: coarse + 2 * halo].astype(F32)).astype(BF16)
    inner = from_table(cols, table, weights[0].get()[...])
    out[...] = finish(lambda rows: before3[rows, :] + inner(rows), table[:coarse], receivers, None, edges, weights)


def raise_kernel(*refs):
    *blocks, down, hots, which, out = refs
    out[...] = down[...].astype(F32) + pick(hots[...], which[...], [block[...] for block in blocks])


def last_kernel(place, last, raised, hots, which, edges, before, *rest):
    cols, receivers, weights, out = rest[:6], rest[6], rest[7:11], rest[11]
    own = out.shape[0]
    table = (raised[...] + jnp.where(which[...] == place, dot(hots[...], last[...]), 0.0)).astype(BF16)
    first = weights[0].get()[...]
    inner, outside = from_own(cols, table[:own], first), from_halo(cols, table[own:], own, first)
    out[...] = finish(lambda rows: before[rows, :] + inner(rows) + outside(rows), table[:own], receivers, cols[-1], edges, weights)


class Here:
    def __init__(self, place):
        self.place = place

    def get(self):
        return self.place


class Arriving(Here):
    def __init__(self, source, place, semaphore):
        super().__init__(place)
        self.copy, self.waiting = pltpu.make_async_copy(source, place, semaphore), True
        self.copy.start()

    def get(self):
        if self.waiting:
            self.copy.wait()
            self.waiting = False
        return self.place


def call(kernel, args, outs, more=(), scratch=(), raw=(), cost=1, far=False, limit=LIMIT):
    specs = [pl.BlockSpec(memory_space=pltpu.HBM if i in raw else pltpu.VMEM) for i in range(len(args))]
    specs += [pl.BlockSpec(memory_space=pltpu.HBM if far else pltpu.VMEM)] * len(more)
    out_specs = [pl.BlockSpec(memory_space=pltpu.VMEM)] * len(outs)
    places = []
    if far:
        places = [pltpu.VMEM(array.shape, array.dtype) for array, _ in more]
        places.append(pltpu.SemaphoreType.DMA((len(more),)))
    n, k, o = len(args), len(more), len(outs)

    def body(*refs):
        given, sources, results, rest = refs[:n], refs[n : n + k], refs[n + k : n + k + o], refs[n + k + o :]
        if far:
            near, semaphores, rest = rest[:k], rest[k], rest[k + 1 :]
            operands = [Arriving(source, near[i], semaphores.at[i]) for i, source in enumerate(sources)]
        else:
            operands = [Here(ref if at is None else ref.at[at]) for ref, (_, at) in zip(sources, more)]
        kernel(*given, *operands, *results, *rest)

    return pl.pallas_call(
        body,
        out_shape=[jax.ShapeDtypeStruct(shape, dtype) for shape, dtype in outs],
        in_specs=specs,
        out_specs=out_specs,
        scratch_shapes=places + list(scratch),
        compiler_params=pltpu.CompilerParams(vmem_limit_bytes=limit),
        cost_estimate=pl.CostEstimate(flops=cost * 10**9, bytes_accessed=cost * 10**5, transcendentals=0),
    )(*args, *[array for array, _ in more])


def over_region(rows, beside=None):
    count = lax.axis_size("region")
    blocks = {0: rows}
    bit = count // 2
    while bit:
        going = dict(blocks)
        if beside is not None and len(going) > 1:
            for j in (0, max(going)):
                going[j], beside = lax.optimization_barrier((going[j], beside))
        for j in blocks:
            going[j + bit] = lax.ppermute(going[j], "region", [(i, i ^ bit) for i in range(count)])
        blocks = going
        bit //= 2
    blocks = [blocks[j] for j in range(count)]
    return blocks if beside is None else (blocks, beside)


def over_both(rows, beside):
    regions, subs = lax.axis_size("region"), lax.axis_size("sub")
    swap = lambda array, axis, bits: lax.ppermute(array, axis, [(i, i ^ bits) for i in range(lax.axis_size(axis))])
    turns = [rows] + [swap(rows, "sub", k) for k in range(1, subs)]
    if regions * subs <= 16:
        turns[1], beside = lax.optimization_barrier((turns[1], beside))
        blocks = {0: turns}
        bit = regions // 2
        while bit > 1:
            for j in list(blocks):
                blocks[j + bit] = [swap(block, "region", bit) for block in blocks[j]]
            bit //= 2
        here = [block for j in range(0, regions, 2) for block in blocks[j]]
        return here + [swap(jnp.concatenate(blocks[j]), "region", 1) for j in range(0, regions, 2)], beside
    blocks, bit = jnp.stack(turns), 1
    while bit < regions:
        blocks, bit = jnp.concatenate([blocks, swap(blocks, "region", bit)]), 2 * bit
    return [blocks], beside


def on_device(
    node_feats,
    fine_senders,
    fine_receivers,
    fine_edges,
    halo_rows,
    coarse_senders,
    coarse_receivers,
    coarse_edges,
    coarse_halo_rows,
    pool_dest,
    pool_target,
    pool3_target,
    top_senders,
    top_receivers,
    top_edges,
    edge_in,
    edge_out,
    node_in,
    node_out,
):
    weights = (edge_in, edge_out, node_in, node_out)
    regions = lax.axis_size("region")
    fine, coarse = node_feats.shape[0], pool3_target.shape[0]
    halo, halo2 = halo_rows.shape[1], coarse_halo_rows.shape[1]
    rows = lambda a: a.reshape(-1, LANES)
    fine_send, fine_recv = rows(fine_senders), rows(fine_receivers)
    coarse_send, coarse_recv = rows(coarse_senders), rows(coarse_receivers)
    top_send, top_recv = rows(top_senders), rows(top_receivers)

    level = lambda index: [(matrix, index) for matrix in weights]
    plain = lambda *arrays: [(array, None) for array in arrays]

    to_pair, to_other, tail = call(
        functools.partial(pick_kernel, halo, halo2, fine, coarse),
        [],
        [((halo + TAIL, LANES), BF16)] * 2 + [((TAIL, LANES), BF16)],
        plain(node_feats, halo_rows, coarse_halo_rows, rows(pool_dest), rows(pool_target), rows(pool3_target)),
        scratch=[pltpu.VMEM((TAIL, LANES), I32)],
        far=True,
        limit=60 * 1024 * 1024,
    )
    pairs = lambda first: [(i, j) for low in range(first, regions - 1, 2) for i, j in ((low, low + 1), (low + 1, low))]
    paired = lax.ppermute(to_pair, "region", pairs(0))
    crossed = lax.ppermute(to_other, "region", pairs(1))
    one = lambda index: [(edge_in, index)]
    fine_cols, coarse_cols = edge_columns(fine, fine_edges.shape[0]), edge_columns(coarse, coarse_edges.shape[0])
    late_send, tail = lax.optimization_barrier((fine_send, tail))
    *fine_cols, before = call(
        ready_kernel,
        [],
        fine_cols + [(fine_edges.shape, F32)],
        plain(node_feats, late_send, fine_recv, fine_edges) + level(0),
        cost=2,
    )
    payload, fine_edges2 = call(
        functools.partial(fine_kernel, halo),
        [paired, crossed, tail, before, *fine_cols],
        [((fine + TAIL, LANES), BF16), (fine_edges.shape, BF16)],
        plain(node_feats, fine_recv, fine_edges) + level(0),
        cost=3,
    )
    wide = -(-(coarse + 2 * halo2) // LANES) * LANES
    size = min(384, top_edges.shape[0])
    listed_shapes = [
        ((wide, LANES), I32),
        ((wide // LANES, LANES), I32),
        ((2 * halo2, LANES), I32),
        ((2 * halo2, LANES), I32),
        (top_send.shape, I32),
        (top_send.shape, I32),
        ((size, LANES), BF16),
        ((size, LANES), I32),
        ((size, LANES), I32),
        ((size // LANES, LANES), I32),
        ((coarse + 2 * halo2, LANES), I32),
    ]
    selected = call(
        functools.partial(listed_kernel, regions, halo2, fine, coarse),
        [tail, paired, crossed],
        listed_shapes,
        plain(top_send, top_recv, top_edges),
        cost=3,
    )
    payload, late_edges = lax.optimization_barrier((payload, coarse_edges))
    *coarse_cols, before = call(
        functools.partial(columns_kernel, coarse),
        [],
        coarse_cols + [(coarse_edges.shape, F32)],
        plain(coarse_send, coarse_recv, late_edges) + one(1),
    )
    blocks, selected = over_region(payload, selected)
    *selected, pool_codes = selected
    totals, members = call(
        functools.partial(begin_kernel, coarse),
        blocks[:-1] + [pool_codes],
        [(pool_codes.shape, F32)] * 2,
    )
    payload2, coarse_edges2 = call(
        functools.partial(coarse_kernel, coarse),
        [blocks[0], blocks[-1], pool_codes, totals, members, before, *coarse_cols],
        [((coarse + TAIL, LANES), BF16), (coarse_edges.shape, BF16)],
        plain(coarse_recv, coarse_edges) + level(1),
        cost=3,
    )
    table_shape = (fine + 2 * halo, LANES)
    table = call(
        functools.partial(parent_kernel, regions, halo, coarse),
        blocks,
        [(table_shape, BF16), ((table_shape[0], coarse), BF16), (table_shape, I32)],
    )
    before = call(edge_kernel, [coarse_edges2], [(coarse_edges.shape, F32)], one(3))
    blocks2, (table, before) = over_both(payload2, (table, before))
    many = len(blocks2)
    begun = []
    if many > 1:
        begun = call(
            functools.partial(half_kernel, coarse),
            blocks2[: 1 - regions // 2] + [selected[0], selected[7]],
            [((wide, LANES), F32)] * 2 + [((size, LANES), F32)] * 2,
        )
    (coarse_final,) = call(
        functools.partial(top_kernel, regions, halo2, coarse, size, many),
        blocks2 + [*begun, *selected, top_edges, coarse_edges2, *before, *coarse_cols],
        [((coarse, LANES), BF16)],
        plain(coarse_recv) + level(2) + level(3),
        scratch=[
            pltpu.VMEM((wide, LANES), F32),
            pltpu.VMEM(top_edges.shape, BF16),
            pltpu.SemaphoreType.DMA((1,)),
        ],
        raw=(many + len(begun) + len(selected),),
        cost=6,
    )
    before = call(edge_kernel, [fine_edges2], [(fine_edges.shape, F32)], one(4))
    blocks3, before = over_region(coarse_final, before)
    table, hots, which = table
    (raised,) = call(raise_kernel, blocks3[:-1] + [table, hots, which], [(table_shape, F32)])
    (fine_final,) = call(
        functools.partial(last_kernel, regions - 1),
        [blocks3[-1], raised, hots, which, fine_edges2, *before, *fine_cols],
        [((fine, LANES), BF16)],
        plain(fine_recv) + level(4),
        cost=3,
    )
    return fine_final


def solution(mesh):
    spread = ("parts", "region", "sub")
    rows, flat = P(spread, None), P(spread)
    in_specs = (
        (rows, flat, flat, rows, rows, flat, flat, rows, rows, rows, flat, flat)
        + (P("parts"), P("parts"), P("parts", None))
        + (P(),) * 4
    )
    return jax.shard_map(on_device, mesh=mesh, in_specs=in_specs, out_specs=rows, check_vma=False)
```

```python
import functools

import jax
import jax.numpy as jnp
from jax import lax
from jax.experimental import pallas as pl
from jax.experimental.pallas import tpu as pltpu
from jax.sharding import PartitionSpec as P

EPSILON = 1e-05
TOP = 2048
LANES = 128
F32, BF16, I32, I16 = jnp.float32, jnp.bfloat16, jnp.int32, jnp.int16
GROUP, SLOTS = 8, 64
STEP = 3072
CUT_BITS = 8
CUT = 1 << CUT_BITS
TAIL = 16
LIMIT = 32 * 1024 * 1024


def dot(a, b):
    return jnp.dot(a, b, preferred_element_type=F32)


def lane_iota(rows, first=0):
    return lax.broadcasted_iota(I32, (rows, LANES), 1) + first


def column(row):
    return jnp.transpose(jnp.broadcast_to(row, (LANES, row.shape[1])))


def columns(rows):
    return jnp.concatenate([column(rows[i : i + 1]) for i in range(rows.shape[0])], axis=0)


def hot(mask):
    return jnp.where(mask, jnp.ones(mask.shape, BF16), jnp.zeros(mask.shape, BF16))


def short(row, count):
    return jnp.concatenate([jnp.broadcast_to(row, (16, LANES)).astype(I16)] * (count // 16), axis=0)


def hot_rows(col, count, start=0):
    col = col.astype(I16)
    places = [lane_iota(16, first) for first in range(start, start + count, LANES)]
    return jnp.concatenate([hot(col == short(place[:1], col.shape[0])) for place in places], axis=1)


def hot_cols(rows, count):
    return hot_codes(lax.broadcasted_iota(I32, (count, LANES), 0), rows)


def hot_codes(col, rows):
    col = col.astype(I16)
    return jnp.concatenate([hot(col == short(rows[i : i + 1], col.shape[0])) for i in range(rows.shape[0])], axis=1)


def gather(row, block, blocks, all_there=False):
    return pick(hot_rows(row, blocks[0].shape[0]), block, blocks, all_there)


def pick(hots, block, blocks, all_there=False):
    wide = dot(hots, jnp.concatenate(blocks, axis=1))
    if block is None:
        return wide
    out = wide[:, :LANES] if all_there else jnp.zeros((hots.shape[0], LANES), F32)
    for i in range(1 if all_there else 0, len(blocks)):
        out = jnp.where(block == i, wide[:, i * LANES : (i + 1) * LANES], out)
    return out


def cut(table):
    short = -table.shape[0] % CUT
    if short:
        table = jnp.concatenate([table, jnp.zeros((short, LANES), BF16)], axis=0)
    return [table[i : i + CUT] for i in range(0, table.shape[0], CUT)]


def segment_sum(rows, block, values):
    chosen = hot_cols(jnp.bitwise_and(rows, CUT - 1), CUT)
    if block is None:
        return jnp.concatenate([dot(chosen[: CUT // 2], values), dot(chosen[CUT // 2 :], values)], axis=0)
    upper = values * block
    wide = jnp.concatenate([values - upper, upper], axis=1)
    out = jnp.concatenate([dot(chosen[: CUT // 2], wide), dot(chosen[CUT // 2 :], wide)], axis=0)
    return jnp.concatenate([out[:, :LANES], out[:, LANES:]], axis=0)


def centre(second):
    exact = second.astype(F32)
    return (exact - jnp.mean(exact, axis=1, keepdims=True)).astype(BF16)


def perceptron(before, centred_second):
    out = dot(jnp.maximum(before.astype(BF16), 0.0), centred_second)
    return out * lax.rsqrt(jnp.mean(out * out, axis=-1, keepdims=True) + EPSILON)


def node_update(nodes, summed, first, second):
    before = dot(nodes, first[:LANES]) + dot(summed.astype(BF16), first[LANES:])
    return (nodes.astype(F32) + perceptron(before, centre(second))).astype(BF16)


def project(blocks, matrix):
    return [dot(block, matrix).astype(BF16) for block in blocks]


def edge_columns(own, count):
    shape = (count, LANES)
    if own == 2 * CUT:
        return [(shape, I32), (shape, I32), (shape, I32), (shape, I32), (shape, I32), (shape, BF16)]
    return [(shape, I32), (shape, I32), (shape, I32)]


def fill_columns(own, senders, receivers, outs):
    send, recv = columns(senders), columns(receivers)
    low, high = jnp.bitwise_and(send, CUT - 1), jnp.right_shift(send, CUT_BITS)
    if own == 2 * CUT:
        low = jnp.where(send < own, low, -1)
        recv_high = jnp.right_shift(recv, CUT_BITS)
        values = [send, low, high, jnp.bitwise_and(recv, CUT - 1), recv_high, recv_high.astype(F32)]
    else:
        values = [low, high, recv]
    for value, out in zip(values, outs):
        out[...] = value.astype(out.dtype)


def from_own(cols, nodes, first):
    _, low, high, recv_low, recv_high, _ = cols
    blocks = cut(nodes)
    sent, received = project(blocks, first[:LANES]), project(blocks, first[LANES : 2 * LANES])
    return lambda rows: (
        gather(low[rows, :], high[rows, :], sent, True) + gather(recv_low[rows, :], recv_high[rows, :], received, True)
    )


def from_halo(cols, halo, own, first):
    sent = dot(halo, first[:LANES]).astype(BF16)
    return lambda rows: dot(hot_rows(cols[0][rows, :], LANES, own), sent)


def from_table(cols, table, first):
    low, high, recv = cols
    sent = project(cut(table), first[:LANES])
    received = project([table[:CUT]], first[LANES : 2 * LANES])
    return lambda rows: gather(low[rows, :], high[rows, :], sent, True) + gather(recv[rows, :], None, received)


def finish(before_at, nodes, receivers, block, edges, weights, new_edges=None, step=STEP):
    second = centre(weights[1].get()[...])
    receivers = receivers.get()
    summed = 0.0
    for at in range(0, edges.shape[0], step):
        rows = slice(at, min(at + step, edges.shape[0]))
        edge = edges[rows, :]
        new = (edge.astype(F32) + perceptron(before_at(rows), second)).astype(BF16)
        if new_edges is not None:
            new_edges[rows, :] = new
        recv = receivers[rows.start // LANES : rows.stop // LANES, :]
        summed = summed + segment_sum(recv, None if block is None else block[rows, :], new)
    return node_update(nodes, summed, weights[2].get()[...], weights[3].get()[...])


def tail_of(block, count):
    return block[count : count + TAIL, :].astype(F32).astype(I32)


def row_layout(fine, coarse):
    f, c = fine // LANES, coarse // LANES
    return {"dest": 0, "target": f, "high": 2 * f, "low": 2 * f + c, "coarse": 2 * f + 2 * c, "fine_high": 2 * f + 2 * c + 1, "fine_low": 2 * f + 2 * c + 2}


def near_tails(tails, me, count):
    out = []
    for other in (me - 1, me + 1):
        there = jnp.logical_and(other >= 0, other < count)
        near = jnp.where(there, jnp.bitwise_xor(me, other), 0)
        picked = sum(jnp.where(near == j, tail, 0) for j, tail in enumerate(tails))
        out.append((other, there, picked))
    return out


def pick_kernel(halo, coarse_halo, fine, coarse, nodes, rows, coarse_rows, dest, target, parent, paired, crossed, own_tail, lists):
    at = row_layout(fine, coarse)
    lists[...] = jnp.zeros_like(lists)
    listed, coarse_listed = rows.get()[...], coarse_rows.get()[...]
    for side in (0, 1):
        lists[at["coarse"] : at["coarse"] + 1, side * coarse_halo : (side + 1) * coarse_halo] = coarse_listed[side : side + 1]
        lanes = slice(side * halo, (side + 1) * halo)
        lists[at["fine_high"] : at["fine_high"] + 1, lanes] = jnp.right_shift(listed[side : side + 1], 7)
        lists[at["fine_low"] : at["fine_low"] + 1, lanes] = jnp.bitwise_and(listed[side : side + 1], LANES - 1)
    lists[at["dest"] : at["target"], :] = dest.get()[...]
    lists[at["target"] : at["high"], :] = target.get()[...]
    parents = parent.get()[...]
    lists[at["high"] : at["low"], :] = jnp.right_shift(parents, 7)
    lists[at["low"] : at["coarse"], :] = jnp.bitwise_and(parents, LANES - 1)
    tail = lists[...].astype(F32).astype(BF16)
    nodes = nodes.get()
    odd = jnp.bitwise_and(lax.axis_index("region"), 1)
    for out, up in ((paired, 1 - odd), (crossed, odd)):
        col = column(jnp.where(up == 1, listed[1:2], listed[0:1]))
        out[:halo, :] = dot(hot_rows(col, fine), nodes[...]).astype(BF16)
        out[halo:, :] = tail
    own_tail[...] = tail


def lower_higher(paired, crossed):
    odd = jnp.bitwise_and(lax.axis_index("region"), 1) == 1
    paired, crossed = paired.astype(F32), crossed.astype(F32)
    return jnp.where(odd, paired, crossed).astype(BF16), jnp.where(odd, crossed, paired).astype(BF16)


def ready_kernel(nodes, senders, receivers, edges, first, _1, _2, _3, *outs):
    *cols, before = outs
    nodes, first = nodes.get()[...], first.get()[...]
    fill_columns(nodes.shape[0], senders.get()[...], receivers.get()[...], cols)
    edges, inner = edges.get(), from_own(cols, nodes, first)
    for at in range(0, edges.shape[0], STEP):
        rows = slice(at, min(at + STEP, edges.shape[0]))
        before[rows, :] = dot(edges[rows, :], first[2 * LANES :]) + inner(rows)


def fine_kernel(halo, paired, crossed, tail, before, *refs):
    cols, (nodes, receivers, edges, *weights), (payload, new_edges) = refs[:6], refs[6:13], refs[13:]
    nodes = nodes.get()[...]
    fine = nodes.shape[0]
    outer = jnp.concatenate(lower_higher(paired[:halo, :], crossed[:halo, :]), axis=0)
    outside = from_halo(cols, outer, fine, weights[0].get()[...])
    payload[:fine, :] = finish(lambda rows: before[rows, :] + outside(rows), nodes, receivers, cols[-1], edges.get(), weights, new_edges)
    payload[fine:, :] = tail[...]


def columns_kernel(own, senders, receivers, edges, first, *outs):
    *cols, before = outs
    fill_columns(own, senders.get()[...], receivers.get()[...], cols)
    before[...] = dot(edges.get()[...], first.get()[2 * LANES :, :])


def edge_kernel(edges, first, before):
    before[...] = dot(edges[...], first.get()[2 * LANES :, :])


def add_fine(codes, blocks, coarse, sums):
    half = codes.shape[0] // 2
    for block in blocks:
        fine = block.shape[0] - TAIL
        at, tail, f = row_layout(fine, coarse), tail_of(block, fine), fine // LANES
        parent = tail[at["dest"] : at["dest"] + f] * coarse + tail[at["target"] : at["target"] + f]
        more = [sums_and_counts(hot_codes(part, parent), block[:fine, :]) for part in (codes[:half], codes[half:])]
        sums = [(total + a, members + b) for (total, members), (a, b) in zip(sums, more)]
    return sums


def begin_kernel(coarse, *refs):
    *blocks, codes, totals, members = refs
    half = codes.shape[0] // 2
    zero = jnp.zeros((half, LANES), F32)
    for i, (total, count) in enumerate(add_fine(codes[...], blocks, coarse, [(zero, zero)] * 2)):
        totals[i * half : (i + 1) * half, :] = total
        members[i * half : (i + 1) * half, :] = count


def coarse_kernel(coarse, own, last, codes, totals, members, before, *rest):
    cols, (receivers, edges, *weights), (payload, new_edges) = rest[:3], rest[3:9], rest[9:]
    half = codes.shape[0] // 2
    halves = (slice(0, half), slice(half, 2 * half))
    sums = [(totals[rows, :], members[rows, :]) for rows in halves]
    table = jnp.concatenate(means(add_fine(codes[...], [last], coarse, sums)), axis=0)
    inner = from_table(cols, table, weights[0].get()[...])
    payload[:coarse, :] = finish(lambda rows: before[rows, :] + inner(rows), table[:coarse], receivers, None, edges.get(), weights, new_edges)
    fine, c = own.shape[0] - TAIL, coarse // LANES
    high = row_layout(fine, coarse)["high"]
    payload[coarse:, :] = jnp.concatenate(
        [tail_of(own, fine)[high : high + 2 * c], jnp.zeros((TAIL - 2 * c, LANES), I32)], axis=0
    ).astype(F32).astype(BF16)


def compact(first, ranks, codes, edges, size, at_once=8):
    place = lax.broadcasted_iota(I32, (size, LANES), 0) + first

    def body(g, carry):
        latents, found = carry
        rank = ranks[pl.ds(pl.multiple_of(g * at_once, at_once), at_once), :]
        code = codes[pl.ds(pl.multiple_of(g * at_once, at_once), at_once), :]
        for i in range(at_once):
            found = found + jnp.where(place == rank[i : i + 1], code[i : i + 1], 0)
        wide = at_once * LANES
        rows = edges[pl.ds(pl.multiple_of(g * wide, wide), wide), :]
        return latents + dot(hot_codes(place, rank), rows), found

    zero = jnp.zeros((size, LANES), F32), jnp.zeros((size, LANES), I32)
    latents, found = lax.fori_loop(0, ranks.shape[0] // at_once, body, zero)
    found = jnp.sum(found.astype(F32), axis=1, keepdims=True).astype(I32)
    return latents.astype(BF16), jnp.broadcast_to(found, (size, LANES))


def below(rows, same):
    square = (rows, rows)
    mask = same(lax.broadcasted_iota(I32, square, 0), lax.broadcasted_iota(I32, square, 1))
    return jnp.where(mask, 1.0, 0.0).astype(BF16)


def running(flags):
    upto = jnp.where(lax.broadcasted_iota(I32, (LANES, LANES), 0) <= lane_iota(LANES), 1.0, 0.0).astype(BF16)
    inside = dot(flags.astype(BF16), upto)
    return inside, jnp.broadcast_to(inside[:, LANES - 1 :], flags.shape)


def listed_kernel(regions, halo, fine, coarse, *refs):
    own, paired, crossed, senders, receivers, edges, parents, firsts, halo_rows, halo_blocks, ranks, codes = refs[:12]
    latents, send, recv, recv_rows, pool_codes = refs[12:]
    me = lax.axis_index("region")
    at = row_layout(fine, coarse)
    start = paired.shape[0] - TAIL
    lower, higher = lower_higher(paired[start:, :], crossed[start:, :])
    own_tail, lower_tail, higher_tail = (tail.astype(F32).astype(I32) for tail in (own[...], lower, higher))
    near = ((me - 1, me > 0, lower_tail), (me + 1, me < regions - 1, higher_tail))
    c = coarse // LANES
    wide, size = parents.shape[0], latents.shape[0]

    def own_parents(tail):
        return tail[at["high"] : at["high"] + c] * LANES + tail[at["low"] : at["low"] + c]

    cols = [columns(own_parents(own_tail))]
    pool_codes[:coarse, :] = me * coarse + lax.broadcasted_iota(I32, (coarse, LANES), 0)
    for side, (other, there, tail) in enumerate(near):
        first = halo * (1 - side)
        col = columns(tail[at["coarse"] : at["coarse"] + 1])[first : first + halo]
        halo_rows[side * halo : (side + 1) * halo, :] = col
        pool_codes[coarse + side * halo : coarse + (side + 1) * halo, :] = jnp.where(there, other * coarse + col, -1)
        halo_blocks[side * halo : (side + 1) * halo, :] = jnp.full(col.shape, jnp.where(there, jnp.bitwise_xor(me, other), -1))
        theirs = own_parents(tail).astype(F32)
        value = jnp.zeros((halo, LANES), F32)
        for i in range(c):
            value = value + jnp.where(col == lane_iota(halo, i * LANES), theirs[i : i + 1], 0.0)
        value = jnp.broadcast_to(jnp.sum(value, axis=1, keepdims=True), (halo, LANES)).astype(I32)
        cols.append(jnp.where(there, value, -1))
    cols.append(jnp.full((wide - coarse - 2 * halo, LANES), -1, I32))
    cols = jnp.concatenate(cols, axis=0)
    parents[...] = cols

    high_count = TOP // LANES
    rows = as_rows(cols)
    row_at = lax.broadcasted_iota(I32, (wide, LANES), 0)
    for i in range(wide // LANES):
        earlier = jnp.logical_and(cols == rows[i : i + 1], row_at < lane_iota(wide, i * LANES))
        seen = jnp.max(jnp.where(earlier, 1.0, 0.0), axis=0, keepdims=True)
        firsts[i : i + 1, :] = jnp.where(seen > 0.0, -2, rows[i : i + 1])
    tops = dot(
        hot_cols(jnp.right_shift(rows, 7), high_count), hot_rows(jnp.bitwise_and(cols, LANES - 1), LANES)
    )
    tops = jnp.minimum(tops, 1.0).astype(BF16)
    receivers = receivers.get()
    count = receivers.shape[0]
    high = lax.broadcasted_iota(I32, (high_count, LANES), 0)
    needed = []
    for i in range(0, count, 8):
        some = receivers[i : i + 8, :]
        match = dot(tops, hot_cols(jnp.bitwise_and(some, LANES - 1), LANES))
        for k in range(8):
            mine = jnp.where(high == jnp.right_shift(some[k : k + 1], 7), match[:, k * LANES : (k + 1) * LANES], 0.0)
            needed.append(jnp.sum(mine, axis=0, keepdims=True))
    needed = jnp.concatenate(needed, axis=0)

    group_of = lambda i: jnp.right_shift(i, GROUP.bit_length() - 1)
    inside, sums = running(needed)
    sums = sums.astype(BF16)
    local = dot(below(count, lambda i, j: jnp.logical_and(j < i, group_of(i) == group_of(j))), sums) + inside - 1.0
    in_group = dot(below(count, lambda i, j: group_of(i) == group_of(j)), sums)
    used = jnp.minimum(in_group, float(SLOTS))
    before = dot(below(count, lambda i, j: group_of(j) < group_of(i)), (used / GROUP).astype(BF16))
    placed = jnp.logical_and(local < SLOTS, local + before < size)
    others = jnp.where(placed, 0.0, needed)
    inside, sums = running(others)
    rank = dot(below(count, lambda i, j: j < i), sums.astype(BF16)) + inside - 1.0
    ranks[...] = jnp.where(others > 0.0, rank, -1.0).astype(I32)
    total = jnp.sum(jnp.sum(needed - others, axis=0, keepdims=True), axis=1, keepdims=True).astype(I32)
    codes[...] = senders.get()[...] * TOP + receivers[...]

    slot = jnp.where(needed > 0.0, local, -1.0).astype(I32)
    place = lax.broadcasted_iota(I32, (SLOTS, LANES), 0)
    edges = edges.get()
    lane = lane_iota(SLOTS)
    slots, targets = [], []
    for first in range(0, count, GROUP):
        code = jnp.zeros((SLOTS, LANES), F32)
        for i in range(first, first + GROUP):
            code = code + jnp.where(place == slot[i : i + 1], codes[i : i + 1, :].astype(F32), 0.0)
        code = jnp.broadcast_to(jnp.sum(code, axis=1, keepdims=True), (SLOTS, LANES)).astype(I32)
        parts = jnp.where(
            lane == 0,
            jnp.right_shift(code, 16),
            jnp.where(lane == 1, jnp.bitwise_and(jnp.right_shift(code, 8), 255), jnp.bitwise_and(code, 255)),
        )
        parts = jnp.where(lane < 3, parts, 0).astype(F32).astype(BF16)
        chosen = hot_cols(slot[first : first + GROUP], SLOTS)
        packed = dot(chosen, edges[first * LANES : (first + GROUP) * LANES, :]).astype(BF16)
        slots.append(jnp.concatenate([packed, parts], axis=1))
        target = before[first : first + 1] + lane_iota(1).astype(F32)
        targets.append(jnp.where(lane_iota(1).astype(F32) < used[first : first + 1], target, -1.0).astype(I32)[:, :SLOTS])
    per = LANES // SLOTS
    targets = [jnp.concatenate(targets[i : i + per], axis=1) for i in range(0, len(targets), per)]
    packed = dot(hot_cols(jnp.concatenate(targets, axis=0), size), jnp.concatenate(slots, axis=0))
    latents[...] = packed[:, :LANES].astype(BF16)
    parts = packed[:, LANES:]
    lane = lane_iota(size)
    code = jnp.where(lane == 0, parts * 65536.0, jnp.where(lane == 1, parts * 256.0, parts))
    code = jnp.broadcast_to(jnp.sum(code, axis=1, keepdims=True), (size, LANES)).astype(I32)
    send[...], recv[...] = ends(code, 0, total)
    recv_rows[...] = as_rows(recv[...])


def ends(code, first_place, total):
    place = lax.broadcasted_iota(I32, code.shape, 0) + first_place
    recv = jnp.where(place < total, jnp.bitwise_and(code, TOP - 1), -3)
    return jnp.right_shift(code, TOP.bit_length() - 1), recv


def parent_kernel(regions, halo, coarse, *refs):
    blocks, (table, parent_hots, parent_blocks) = refs[:regions], refs[regions:]
    me = lax.axis_index("region")
    fine = blocks[0].shape[0] - TAIL
    at = row_layout(fine, coarse)
    tails = [tail_of(block, fine) for block in blocks]
    f = fine // LANES

    def own_parents(tail):
        return tail[at["dest"] : at["dest"] + f] * coarse + tail[at["target"] : at["target"] + f]

    table[:fine, :] = blocks[0][:fine, :]
    owner = lambda tail: tail[at["dest"] : at["dest"] + f]
    parent_hots[:fine, :] = hot_rows(columns(tails[0][at["target"] : at["target"] + f]), coarse)
    parent_blocks[:fine, :] = jnp.bitwise_xor(columns(owner(tails[0])), me)
    for side, (other, there, tail) in enumerate(near_tails(tails, me, regions)):
        rows = slice(fine + side * halo, fine + (side + 1) * halo)
        first = halo * (1 - side)
        listed = tail[at["fine_high"] : at["fine_high"] + 1] * LANES + tail[at["fine_low"] : at["fine_low"] + 1]
        col = columns(listed)[first : first + halo]
        theirs = own_parents(tail).astype(F32)
        value = jnp.zeros((halo, LANES), F32)
        for i in range(f):
            value = value + jnp.where(col == lane_iota(halo, i * LANES), theirs[i : i + 1], 0.0)
        value = jnp.broadcast_to(jnp.sum(value, axis=1, keepdims=True), (halo, LANES)).astype(I32)
        parent_hots[rows, :] = hot_rows(jnp.bitwise_and(value, coarse - 1), coarse)
        block = jnp.bitwise_xor(jnp.right_shift(value, coarse.bit_length() - 1), me)
        parent_blocks[rows, :] = jnp.where(there, block, -1)
        total = jnp.zeros((halo, LANES), F32)
        for j, block in enumerate(blocks):
            here = jnp.logical_and(there, jnp.bitwise_xor(me, j) == other)
            total = total + dot(hot_rows(jnp.where(here, col, -1), fine), block[:fine, :])
        table[rows, :] = total.astype(BF16)


def sums_and_counts(chosen, rows):
    both = dot(chosen, jnp.concatenate([rows, jnp.ones(rows.shape, BF16)], axis=1))
    return both[:, :LANES], both[:, LANES:]


def add_blocks(cols, blocks, coarse, sums):
    c = coarse // LANES

    def add(block, sums):
        tail = tail_of(block, coarse)
        parent = tail[:c] * LANES + tail[c : 2 * c]
        more = [sums_and_counts(hot_codes(col, parent), block[:coarse, :]) for col in cols]
        return tuple((total + a, members + b) for (total, members), (a, b) in zip(sums, more))

    if isinstance(blocks, tuple):
        for block in blocks:
            sums = add(block, sums)
        return sums
    return lax.fori_loop(0, blocks.shape[0], lambda n, sums: add(blocks.at[n], sums), sums)


def nothing(cols):
    return tuple((jnp.zeros(col.shape, F32),) * 2 for col in cols)


def means(sums):
    return [(total / jnp.maximum(members, 1.0)).astype(BF16) for total, members in sums]


def half_kernel(coarse, *refs):
    *blocks, stack = refs[:-6]
    rows = coarse + TAIL
    blocks = tuple(blocks) + tuple(stack.at[i : i + rows] for i in range(0, stack.shape[0], rows))
    parents, send, *outs = refs[-6:]
    cols = [parents[...], send[...]]
    for i, value in enumerate(sum(add_blocks(cols, blocks, coarse, nothing(cols)), ())):
        outs[i][...] = value


def as_rows(col):
    return jnp.concatenate(
        [jnp.transpose(col[i : i + LANES])[:1] for i in range(0, col.shape[0], LANES)], axis=0
    )


def top_kernel(regions, halo, coarse, size, count, *refs):
    subs = lax.axis_size("sub")
    if count > 1:
        rows = coarse + TAIL
        stacks = refs[count - regions // 2 : count]
        there = tuple(stack.at[i * rows : (i + 1) * rows] for stack in stacks for i in range(subs))
        blocks = tuple((there if j % 2 else refs)[j // 2 * subs + k] for j in range(regions) for k in range(subs))
        begun = [ref[...] for ref in refs[count : count + 4]]
        begun, refs = ((begun[0], begun[1]), (begun[2], begun[3])), refs[count + 4 :]
    else:
        there = blocks = refs[0]
        begun, refs = None, refs[count:]
    parents, firsts, halo_rows, halo_blocks, ranks, codes, latents, send, recv, recv_rows, all_edges = refs[:11]
    edges, before3, *cols = refs[11:16]
    receivers, top_weights, weights = refs[16], refs[17:21], refs[21:25]
    out, agg, fallback, semaphore = refs[25:]
    me = lax.axis_index("region")
    own_sub = lambda j: blocks[j * subs] if count > 1 else blocks.at[j * subs]
    mine, firsts = parents[...], firsts[...]
    cols_here = [mine, send[...]]
    top_own, from_send = means(add_blocks(cols_here, there[subs:] if count > 1 else there, coarse, nothing(cols_here) if begun is None else begun))
    near = gather(halo_rows[...], halo_blocks[...], [own_sub(j)[:coarse, :] for j in range(regions)])
    down = jnp.concatenate([own_sub(0)[:coarse, :].astype(F32), near], axis=0)
    first, second = top_weights[0].get()[...], centre(top_weights[1].get()[...])
    received = dot(top_own, first[LANES : 2 * LANES]).astype(BF16)
    others = jnp.concatenate([first[:LANES], first[2 * LANES :]], axis=0)

    def one(edge, from_send, recv, recv_rows):
        before = dot(jnp.concatenate([from_send, edge], axis=1), others) + dot(hot_codes(recv, firsts), received)
        new = (edge.astype(F32) + perceptron(before, second)).astype(BF16)
        return dot(hot_codes(mine, recv_rows), new)

    agg[...] = one(latents[...], from_send, recv[...], recv_rows[...])

    def more(b, carry):
        copy = pltpu.make_async_copy(all_edges, fallback, semaphore.at[0])
        copy.start()
        copy.wait()
        edge, code = compact(b * LANES, ranks, codes, fallback, LANES)
        send, recv = ends(code, b * LANES, left)
        (from_send,) = means(add_blocks([send], blocks, coarse, nothing([send])))
        agg[...] += one(edge, from_send, recv, as_rows(recv))
        return carry

    left = jnp.max(ranks[...]) + 1
    lax.fori_loop(0, (left + LANES - 1) // LANES, more, 0)
    top_final = node_update(top_own, agg[...], top_weights[2].get()[...], top_weights[3].get()[...])
    table = (down + top_final[: coarse + 2 * halo].astype(F32)).astype(BF16)
    inner = from_table(cols, table, weights[0].get()[...])
    out[...] = finish(lambda rows: before3[rows, :] + inner(rows), table[:coarse], receivers, None, edges, weights)


def last_kernel(regions, *refs):
    blocks, (down, parent_hots, parent_blocks, edges, before, *rest) = refs[:regions], refs[regions:]
    cols, receivers, weights, out = rest[:6], rest[6], rest[7:11], rest[11]
    own = out.shape[0]
    parent = pick(parent_hots[...], parent_blocks[...], [block[...] for block in blocks])
    table = (down[...].astype(F32) + parent).astype(BF16)
    first = weights[0].get()[...]
    inner, outside = from_own(cols, table[:own], first), from_halo(cols, table[own:], own, first)
    out[...] = finish(lambda rows: before[rows, :] + inner(rows) + outside(rows), table[:own], receivers, cols[-1], edges, weights)


class Here:
    def __init__(self, place):
        self.place = place

    def get(self):
        return self.place


class Arriving(Here):
    def __init__(self, source, place, semaphore):
        super().__init__(place)
        self.copy, self.waiting = pltpu.make_async_copy(source, place, semaphore), True
        self.copy.start()

    def get(self):
        if self.waiting:
            self.copy.wait()
            self.waiting = False
        return self.place


def call(kernel, args, outs, more=(), scratch=(), raw=(), cost=1, far=False, limit=LIMIT):
    specs = [pl.BlockSpec(memory_space=pltpu.HBM if i in raw else pltpu.VMEM) for i in range(len(args))]
    specs += [pl.BlockSpec(memory_space=pltpu.HBM if far else pltpu.VMEM)] * len(more)
    out_specs = [pl.BlockSpec(memory_space=pltpu.VMEM)] * len(outs)
    places = []
    if far:
        places = [pltpu.VMEM(array.shape, array.dtype) for array, _ in more]
        places.append(pltpu.SemaphoreType.DMA((len(more),)))
    n, k, o = len(args), len(more), len(outs)

    def body(*refs):
        given, sources, results, rest = refs[:n], refs[n : n + k], refs[n + k : n + k + o], refs[n + k + o :]
        if far:
            near, semaphores, rest = rest[:k], rest[k], rest[k + 1 :]
            operands = [Arriving(source, near[i], semaphores.at[i]) for i, source in enumerate(sources)]
        else:
            operands = [Here(ref if at is None else ref.at[at]) for ref, (_, at) in zip(sources, more)]
        kernel(*given, *operands, *results, *rest)

    return pl.pallas_call(
        body,
        out_shape=[jax.ShapeDtypeStruct(shape, dtype) for shape, dtype in outs],
        in_specs=specs,
        out_specs=out_specs,
        scratch_shapes=places + list(scratch),
        compiler_params=pltpu.CompilerParams(vmem_limit_bytes=limit),
        cost_estimate=pl.CostEstimate(flops=cost * 10**9, bytes_accessed=cost * 10**5, transcendentals=0),
    )(*args, *[array for array, _ in more])


def over_region(rows, beside=None):
    count = lax.axis_size("region")
    blocks = {0: rows}
    bit = count // 2
    while bit:
        going = dict(blocks)
        if beside is not None and len(going) > 1:
            for j in (0, max(going)):
                going[j], beside = lax.optimization_barrier((going[j], beside))
        for j in blocks:
            going[j + bit] = lax.ppermute(going[j], "region", [(i, i ^ bit) for i in range(count)])
        blocks = going
        bit //= 2
    blocks = [blocks[j] for j in range(count)]
    return blocks if beside is None else (blocks, beside)


def over_both(rows, beside):
    regions, subs = lax.axis_size("region"), lax.axis_size("sub")
    swap = lambda array, axis, bits: lax.ppermute(array, axis, [(i, i ^ bits) for i in range(lax.axis_size(axis))])
    turns = [rows] + [swap(rows, "sub", k) for k in range(1, subs)]
    if regions * subs <= 16:
        turns[1], beside = lax.optimization_barrier((turns[1], beside))
        blocks = {0: turns}
        bit = regions // 2
        while bit > 1:
            for j in list(blocks):
                blocks[j + bit] = [swap(block, "region", bit) for block in blocks[j]]
            bit //= 2
        here = [block for j in range(0, regions, 2) for block in blocks[j]]
        return here + [swap(jnp.concatenate(blocks[j]), "region", 1) for j in range(0, regions, 2)], beside
    blocks, bit = jnp.stack(turns), 1
    while bit < regions:
        blocks, bit = jnp.concatenate([blocks, swap(blocks, "region", bit)]), 2 * bit
    return [blocks], beside


def on_device(
    node_feats,
    fine_senders,
    fine_receivers,
    fine_edges,
    halo_rows,
    coarse_senders,
    coarse_receivers,
    coarse_edges,
    coarse_halo_rows,
    pool_dest,
    pool_target,
    pool3_target,
    top_senders,
    top_receivers,
    top_edges,
    edge_in,
    edge_out,
    node_in,
    node_out,
):
    weights = (edge_in, edge_out, node_in, node_out)
    regions = lax.axis_size("region")
    fine, coarse = node_feats.shape[0], pool3_target.shape[0]
    halo, halo2 = halo_rows.shape[1], coarse_halo_rows.shape[1]
    rows = lambda a: a.reshape(-1, LANES)
    fine_send, fine_recv = rows(fine_senders), rows(fine_receivers)
    coarse_send, coarse_recv = rows(coarse_senders), rows(coarse_receivers)
    top_send, top_recv = rows(top_senders), rows(top_receivers)

    level = lambda index: [(matrix, index) for matrix in weights]
    plain = lambda *arrays: [(array, None) for array in arrays]

    to_pair, to_other, tail = call(
        functools.partial(pick_kernel, halo, halo2, fine, coarse),
        [],
        [((halo + TAIL, LANES), BF16)] * 2 + [((TAIL, LANES), BF16)],
        plain(node_feats, halo_rows, coarse_halo_rows, rows(pool_dest), rows(pool_target), rows(pool3_target)),
        scratch=[pltpu.VMEM((TAIL, LANES), I32)],
        far=True,
        limit=60 * 1024 * 1024,
    )
    pairs = lambda first: [(i, j) for low in range(first, regions - 1, 2) for i, j in ((low, low + 1), (low + 1, low))]
    paired = lax.ppermute(to_pair, "region", pairs(0))
    crossed = lax.ppermute(to_other, "region", pairs(1))
    one = lambda index: [(edge_in, index)]
    fine_cols, coarse_cols = edge_columns(fine, fine_edges.shape[0]), edge_columns(coarse, coarse_edges.shape[0])
    late_send, tail = lax.optimization_barrier((fine_send, tail))
    *fine_cols, before = call(
        ready_kernel,
        [],
        fine_cols + [(fine_edges.shape, F32)],
        plain(node_feats, late_send, fine_recv, fine_edges) + level(0),
        cost=2,
    )
    payload, fine_edges2 = call(
        functools.partial(fine_kernel, halo),
        [paired, crossed, tail, before, *fine_cols],
        [((fine + TAIL, LANES), BF16), (fine_edges.shape, BF16)],
        plain(node_feats, fine_recv, fine_edges) + level(0),
        cost=3,
    )
    wide = -(-(coarse + 2 * halo2) // LANES) * LANES
    size = min(384, top_edges.shape[0])
    listed_shapes = [
        ((wide, LANES), I32),
        ((wide // LANES, LANES), I32),
        ((2 * halo2, LANES), I32),
        ((2 * halo2, LANES), I32),
        (top_send.shape, I32),
        (top_send.shape, I32),
        ((size, LANES), BF16),
        ((size, LANES), I32),
        ((size, LANES), I32),
        ((size // LANES, LANES), I32),
        ((coarse + 2 * halo2, LANES), I32),
    ]
    selected = call(
        functools.partial(listed_kernel, regions, halo2, fine, coarse),
        [tail, paired, crossed],
        listed_shapes,
        plain(top_send, top_recv, top_edges),
        cost=3,
    )
    payload, late_edges = lax.optimization_barrier((payload, coarse_edges))
    *coarse_cols, before = call(
        functools.partial(columns_kernel, coarse),
        [],
        coarse_cols + [(coarse_edges.shape, F32)],
        plain(coarse_send, coarse_recv, late_edges) + one(1),
    )
    blocks, selected = over_region(payload, selected)
    *selected, pool_codes = selected
    totals, members = call(
        functools.partial(begin_kernel, coarse),
        blocks[:-1] + [pool_codes],
        [(pool_codes.shape, F32)] * 2,
    )
    payload2, coarse_edges2 = call(
        functools.partial(coarse_kernel, coarse),
        [blocks[0], blocks[-1], pool_codes, totals, members, before, *coarse_cols],
        [((coarse + TAIL, LANES), BF16), (coarse_edges.shape, BF16)],
        plain(coarse_recv, coarse_edges) + level(1),
        cost=3,
    )
    table_shape = (fine + 2 * halo, LANES)
    table = call(
        functools.partial(parent_kernel, regions, halo, coarse),
        blocks,
        [(table_shape, BF16), ((table_shape[0], coarse), BF16), (table_shape, I32)],
    )
    before = call(edge_kernel, [coarse_edges2], [(coarse_edges.shape, F32)], one(3))
    blocks2, before = over_both(payload2, before)
    many = len(blocks2)
    begun = []
    if many > 1:
        begun = call(
            functools.partial(half_kernel, coarse),
            blocks2[: 1 - regions // 2] + [selected[0], selected[7]],
            [((wide, LANES), F32)] * 2 + [((size, LANES), F32)] * 2,
        )
    (coarse_final,) = call(
        functools.partial(top_kernel, regions, halo2, coarse, size, many),
        blocks2 + [*begun, *selected, top_edges, coarse_edges2, *before, *coarse_cols],
        [((coarse, LANES), BF16)],
        plain(coarse_recv) + level(2) + level(3),
        scratch=[
            pltpu.VMEM((wide, LANES), F32),
            pltpu.VMEM(top_edges.shape, BF16),
            pltpu.SemaphoreType.DMA((1,)),
        ],
        raw=(many + len(begun) + len(selected),),
        cost=6,
    )
    before = call(edge_kernel, [fine_edges2], [(fine_edges.shape, F32)], one(4))
    blocks3, (before, table) = over_region(coarse_final, (before, table))
    (fine_final,) = call(
        functools.partial(last_kernel, regions),
        blocks3 + [*table, fine_edges2, *before, *fine_cols],
        [((fine, LANES), BF16)],
        plain(fine_recv) + level(4),
        cost=3,
    )
    return fine_final


def solution(mesh):
    spread = ("parts", "region", "sub")
    rows, flat = P(spread, None), P(spread)
    in_specs = (
        (rows, flat, flat, rows, rows, flat, flat, rows, rows, rows, flat, flat)
        + (P("parts"), P("parts"), P("parts", None))
        + (P(),) * 4
    )
    return jax.shard_map(on_device, mesh=mesh, in_specs=in_specs, out_specs=rows, check_vma=False)
```
